32 devices in a mesh: src: 16 (over z, y, x), tgt: 2 (over core).
Axes of the slice: x: 2, y: 2, z: 4, core: 2. Of those that a mesh axis runs over, the one named last changes fastest.
Arguments:
- sources: bfloat16 [6144, 1024], P('src'), may hold values from -72 to 72
- targets: bfloat16 [64, 1024, 1024], P(('src', 'tgt')), may hold values from -72 to 72
- picks: int32 [6144, 4], P('src'), may hold values from 0 to 63, all different within a row; in each aligned block of 384 rows (0 to 383, 384 to 767, ...) at most 48 rows name the same one
- cluster_home: int32 [64], replicated, may hold values from 0 to 63, each once
- row_count: int32 [64], replicated, may hold values from 512 to 1024, as said below
Outputs:
- pooled: bfloat16 [6144, 1024], P('src')
- confidence: bfloat16 [6144], P('src')
The draws below stay inside these ranges and needn't reach their ends.
Inputs may be any that keep to these rules, and one draw needn't show every extreme that they name: `picks`: the 4 clusters of a source are different; among the 384 sources of one index of src no cluster is picked by more than 48 sources; every cluster is picked by some source. Cluster c's block is targets[cluster_home[c]]; each position is used once. Rows of a block at or past row_count of its cluster are not part of it; some cluster uses all 1024 rows.
All inputs are finite; a program needn't handle non-finite values.
Results may differ from the reference program's by a relative error of at most 0.0046.
Values may be sent and summed in bfloat16 or wider, within the bound.
No kernel may reach another device: no remote copies, remote signals or barrier semaphores. Data moves between devices by JAX's collectives and lax.ppermute only.
A program may use at most 64 MiB of HBM per device.

```python
import math
import jax
import jax.numpy as jnp
import numpy as np
from jax import lax

D = 1024
ROWS = 1024
PICKS = 4
SRC_DEV = 384
SOURCES = 6144
CLUSTERS = 64
CAP = 48
N_SRC = 16


def draw_sources(key, part):
    first = jax.random.fold_in(key, 0)
    values = jnp.clip(jax.random.normal(first, (SOURCES, D), jnp.float32), -6.0, 6.0)
    return values.astype(jnp.bfloat16)


def draw_targets(key, part):
    first = jax.random.fold_in(jax.random.fold_in(key, 7), 0)
    values = jnp.clip(jax.random.normal(first, (CLUSTERS, ROWS, D), jnp.float32), -6.0, 6.0)
    return values.astype(jnp.bfloat16)


def draw_row_count(key, part):
    first, second = jax.random.split(jax.random.fold_in(key, 11))
    counts = jax.random.randint(first, (CLUSTERS,), ROWS // 2, ROWS + 1, jnp.int32)
    fullest = jax.random.randint(second, (), 0, CLUSTERS, jnp.int32)
    return jnp.where(jnp.arange(CLUSTERS, dtype=jnp.int32) == fullest, ROWS, counts).astype(jnp.int32)


def shared_out(rng, own, number, rows, amount, top, most, slope):
    order = jax.random.permutation(rng, amount)
    crowded, usual = portions_of(amount, rows * top, most, slope, True), portions_of(amount, rows * top, most, slope, False)
    places = jnp.arange(amount)

    def named(sizes, turn):
        used = int((sizes > 0).sum())
        fixed = max(1, used // 4)
        moved = fixed + (places - fixed + turn * (used - fixed)) % max(1, amount - fixed)
        return jnp.zeros((amount,), jnp.int32).at[order[jnp.where(places < fixed, places, moved)]].set(jnp.asarray(sizes, jnp.int32))

    sizes = jnp.where(number % 4 == 0, named(crowded, number // 4), named(usual, number - number // 4 - 1))
    mixed = jax.random.permutation(jax.random.fold_in(own, 3), amount)
    donor, sink = mixed[0:amount // 2 * 2:2], mixed[1:amount // 2 * 2:2]
    margin = jnp.minimum(sizes[donor] - 1, most - sizes[sink]) // 2
    margin = jnp.where((donor == order[0]) | (sink == order[0]) | (sizes[sink] == 0), 0, jnp.maximum(margin, 0))
    moved = jax.random.randint(jax.random.fold_in(own, 4), (amount // 2,), 0, 1 << 20) % (margin + 1)
    sizes = sizes.at[donor].add(-moved).at[sink].add(moved)
    items = jnp.searchsorted(jnp.cumsum(sizes), jnp.arange(rows * top), side="right").astype(jnp.int32)
    listing = items.reshape(top, rows).T
    listing = listing[jax.random.permutation(jax.random.fold_in(own, 1), rows)]
    turn = jax.random.randint(jax.random.fold_in(own, 2), (rows, 1), 0, top)
    return jnp.take_along_axis(listing, (jnp.arange(top)[None, :] + turn) % top, axis=1)


def portions_of(number_of, total, reach, lean, full):
    portions = [(1 << 20) // math.isqrt(grade ** lean) + 1 for grade in range(1, number_of + 1)]
    largest = reach if full else min(reach, max(-(-total // number_of), total * portions[0] // sum(portions)))
    least = 1 if total - largest >= number_of - 1 else 0
    holding, spare = [largest] + [least] * (number_of - 1), total - largest - least * (number_of - 1)
    while spare > 0:
        candidates = [i for i in range(1, number_of) if holding[i] < largest] or [i for i in range(1, number_of) if holding[i] < reach]
        pool, left = sum([portions[i] for i in candidates]), spare
        for i in candidates:
            more = min(reach - holding[i], max(1, left * portions[i] // pool), spare)
            holding[i] = holding[i] + more
            spare = spare - more
    return np.array(holding)


def setup_inputs(seed: int = 0) -> dict:
    seeds = jax.random.split(jax.random.key(seed), 6)
    sources = draw_sources(jax.random.fold_in(seeds[5], 71), 0)
    targets = draw_targets(jax.random.fold_in(seeds[5], 71), 0)
    picks_keys = jax.random.split(jax.random.fold_in(seeds[2], 1), SOURCES // SRC_DEV)
    picks_turns = jax.random.permutation(jax.random.fold_in(seeds[2], 3), SOURCES // SRC_DEV)
    picks = jax.vmap(lambda own, number: shared_out(jax.random.fold_in(seeds[2], 2), own, number, SRC_DEV, CLUSTERS, PICKS, CAP, 2))(picks_keys, picks_turns).reshape((SOURCES, PICKS))
    cluster_home = jax.random.permutation(seeds[3], CLUSTERS).astype(jnp.int32)
    row_count = draw_row_count(jax.random.fold_in(seeds[5], 71), 0)
    return dict(sources=sources, targets=targets, picks=picks, cluster_home=cluster_home, row_count=row_count)


NEGATIVE = -1e+30
SHARPNESS = 2.5

def masked_lse(values, allowed, along):
    highest = lax.optimization_barrier(jnp.max(jnp.where(allowed, values, NEGATIVE), axis=along, keepdims=True))
    summed = lax.optimization_barrier(jnp.sum(jnp.where(allowed, jnp.exp(values - highest), 0.0), axis=along, keepdims=True))
    return jnp.squeeze(highest + jnp.log(jnp.where(summed > 0.0, summed, 1.0)), axis=along)

def reference(sources, targets, picks, cluster_home, row_count):
    n_sources = sources.shape[0]
    slots_per = N_SRC * CAP
    cluster_ids = jnp.arange(CLUSTERS, dtype=jnp.int32)
    blocks = picks.reshape(N_SRC, SRC_DEV * PICKS)

    def block_ordinal(block):
        one_hot = (block[:, None] == cluster_ids[None, :]).astype(jnp.int32)
        before = jnp.cumsum(one_hot, axis=0) - one_hot
        return lax.optimization_barrier(jnp.sum(before * one_hot, axis=1))
    ordinal = lax.map(block_ordinal, blocks).reshape(n_sources, PICKS)
    block_no = (jnp.arange(n_sources, dtype=jnp.int32) // SRC_DEV)[:, None]
    flat_index = (picks * slots_per + block_no * CAP + ordinal).astype(jnp.int32)
    row_ids = jnp.broadcast_to(jnp.arange(n_sources, dtype=jnp.int32)[:, None], (n_sources, PICKS))
    source_of = jnp.full((CLUSTERS * slots_per,), n_sources, jnp.int32)
    source_of = source_of.at[flat_index.reshape(-1)].set(row_ids.reshape(-1)).reshape(CLUSTERS, slots_per)
    sharp = SHARPNESS / math.sqrt(D)
    row_ids_block = jnp.arange(ROWS, dtype=jnp.int32)

    def per_cluster(cluster):
        members = source_of[cluster]
        live = members < n_sources
        gathered = jnp.take(sources, jnp.minimum(members, n_sources - 1), axis=0)
        queries = jnp.where(live[:, None], gathered, jnp.zeros((), jnp.bfloat16))
        block = lax.dynamic_index_in_dim(targets, cluster_home[cluster].astype(jnp.int32), 0, keepdims=False)
        scores = jnp.dot(queries, block.T, preferred_element_type=jnp.float32) * sharp
        row_valid = row_ids_block < row_count[cluster]
        reverse = masked_lse(scores, live[:, None], 0)
        forward_part = masked_lse(scores, row_valid[None, :], 1)
        shifted = scores - 0.5 * reverse[None, :]
        margin_part = masked_lse(shifted, row_valid[None, :], 1)
        weights = jnp.where(row_valid[None, :], jnp.exp(shifted - margin_part[:, None]), 0.0).astype(jnp.bfloat16)
        pool_part = jnp.dot(weights, block, preferred_element_type=jnp.float32)
        return (forward_part, margin_part, pool_part)
    forward_all, margin_all, pool_all = lax.map(per_cluster, cluster_ids)
    forward_picks = jnp.take(forward_all.reshape(-1), flat_index)
    margin_picks = jnp.take(margin_all.reshape(-1), flat_index)
    every = jnp.ones(forward_picks.shape, dtype=bool)
    forward = masked_lse(forward_picks, every, 1)
    margin_total = masked_lse(margin_picks, every, 1)
    flat_pool = pool_all.reshape(-1, D)
    pooled = jnp.zeros((n_sources, D), jnp.float32)
    for pick_no in range(PICKS):
        factor = jnp.exp(margin_picks[:, pick_no] - margin_total)
        pooled = pooled + factor[:, None] * jnp.take(flat_pool, flat_index[:, pick_no], axis=0)
    return (pooled.astype(jnp.bfloat16), (margin_total - 0.5 * forward).astype(jnp.bfloat16))
```

```python
import functools
import math

import jax
import jax.numpy as jnp
from jax import lax
from jax.experimental import pallas as pl
from jax.experimental.pallas import tpu as pltpu
from jax.sharding import PartitionSpec as P

NEGATIVE = -1e30
SHARPNESS = 2.5
EXTRA = 16
F32, BF16 = jnp.float32, jnp.bfloat16
MIB = 1 << 20


def iota(shape, axis):
    return lax.broadcasted_iota(jnp.int32, shape, axis)


def call(kernel, out_shape, scratch=(), smem=0, n_in=0, limit=32, flops=0, moved=0, exps=0, **kw):
    if not kw:
        kw = dict(
            in_specs=[pl.BlockSpec(memory_space=pltpu.SMEM)] * smem
            + [pl.BlockSpec(memory_space=pltpu.VMEM)] * (n_in - smem),
            out_specs=jax.tree.map(lambda _: pl.BlockSpec(memory_space=pltpu.VMEM), out_shape),
        )
    return pl.pallas_call(
        kernel,
        out_shape=out_shape,
        scratch_shapes=list(scratch),
        compiler_params=pltpu.CompilerParams(vmem_limit_bytes=limit * MIB),
        cost_estimate=pl.CostEstimate(flops=flops, bytes_accessed=moved, transcendentals=exps),
        **kw,
    )


def columns(rows, width):
    stacked = jnp.concatenate(rows + [jnp.zeros((128 - len(rows), width), F32)], axis=0)
    return stacked.T


def three(row):
    high = row.astype(BF16).astype(F32)
    middle = (row - high).astype(BF16).astype(F32)
    return [high, middle, row - high - middle]


def extra_rows(first, second, width):
    parts = three(first) + three(second)
    body = jnp.concatenate(parts + [jnp.zeros((EXTRA - len(parts), first.shape[1]), F32)], axis=0)
    rest = jnp.zeros((EXTRA, width - first.shape[1]), F32)
    return jnp.concatenate([body, rest], axis=1).astype(BF16)


def read_extra(ref, start, length):
    block = ref[start : start + EXTRA, :length].astype(F32)
    first = (block[0:1] + block[1:2]) + block[2:3]
    second = (block[3:4] + block[4:5]) + block[5:6]
    return first, second


def one_hot_slots(code, start, group, capacity):
    rows = code.shape[1]
    order = iota((capacity, rows), 0).astype(F32)
    return jnp.concatenate(
        [jnp.where(order == code[b : b + 1, :], 1.0, 0.0) for b in range(start, start + group)], axis=0
    )


def gather_body(info, picks_ref, home_ref, source, q_ref, code_ref, *, n_tgt, per_device, capacity, group):
    n_buckets, rows = code_ref.shape
    n_clusters = home_ref.shape[1]
    width = q_ref.shape[2]
    cluster = iota((n_clusters, rows), 0)
    member = jnp.zeros((n_clusters, rows), F32)
    for k in range(picks_ref.shape[0]):
        member = jnp.where(cluster == picks_ref[k : k + 1, :], 1.0, member)
    bucket = iota((n_buckets, n_clusters), 0)
    holder = (info[0] + lax.div(bucket, per_device)) * n_tgt + info[1]
    place = holder * per_device + lax.rem(bucket, per_device)
    chosen = jnp.where(home_ref[...] == place, 1.0, 0.0).astype(BF16)
    inside = jnp.dot(chosen, member.astype(BF16), preferred_element_type=F32)
    earlier = jnp.where(iota((rows, rows), 0) < iota((rows, rows), 1), 1.0, 0.0).astype(BF16)
    rank = jnp.dot(inside.astype(BF16), earlier, preferred_element_type=F32)
    code = jnp.where(inside > 0.5, rank, -1.0)
    code_ref[...] = code
    per_message = group // per_device
    for start in range(0, n_buckets, group):
        slots = one_hot_slots(code, start, group, capacity)
        filled = jnp.sum(slots, axis=1, keepdims=True)
        found = jnp.dot(slots.astype(BF16), source, preferred_element_type=F32)
        head = found[:, :128]
        head = jnp.where((iota(head.shape, 1) == 0) & (filled < 0.5), jnp.inf, head)
        found = jnp.concatenate([head, found[:, 128:]], axis=1).astype(BF16)
        d = start // per_device
        q_ref[d : d + per_message] = found.reshape(per_message, per_device * capacity, width)


def gather_own(info, picks_ref, home_ref, src_ref, q_ref, code_ref, **sizes):
    gather_body(info, picks_ref, home_ref, src_ref[...], q_ref, code_ref, **sizes)


def gather_partner(info, picks_ref, home_ref, mine_ref, other_ref, q_ref, code_ref, src_ref, **sizes):
    half = mine_ref.shape[0]
    src_ref[pl.ds(pl.multiple_of(info[1] * half, 16), half), :] = mine_ref[...]
    src_ref[pl.ds(pl.multiple_of((1 - info[1]) * half, 16), half), :] = other_ref[...]
    gather_body(info, picks_ref, home_ref, src_ref[...], q_ref, code_ref, **sizes)


def owner_kernel(count_ref, q1_ref, q2_ref, t_ref, p1_ref, p2_ref, mf_ref, s_ref, w_ref, bias_ref, mf_scr, *, block):
    n_msg, capacity, width = q1_ref.shape
    n_half = n_msg * capacity
    n_rows, n_cols = s_ref.shape
    count = count_ref[pl.program_id(0)]
    column_bias = jnp.where(iota((1, n_cols), 1) < count, 0.0, NEGATIVE).astype(F32)
    sharp = SHARPNESS / math.sqrt(width)
    highest = jnp.full((1, n_cols), NEGATIVE * 4, F32)
    for h, q_ref in enumerate((q1_ref, q2_ref)):
        q = q_ref[...].reshape(n_half, width)
        head = q[:, :128].astype(F32)
        empty = head > 1e38
        slot_bias = jnp.where(empty[:, 0:1], NEGATIVE, 0.0).astype(F32)
        bias_ref[h * n_half : (h + 1) * n_half, :] = jnp.broadcast_to(slot_bias, (n_half, 128))
        q = jnp.concatenate([jnp.where(empty, 0.0, head).astype(BF16), q[:, 128:]], axis=1)
        s = lax.dot_general(q, t_ref[0], (((1,), (1,)), ((), ())), preferred_element_type=F32)
        s = s * sharp + column_bias
        s_ref[h * n_half : (h + 1) * n_half, :] = s
        highest = jnp.maximum(highest, jnp.max(s + slot_bias, axis=0, keepdims=True))

    def column_sums(i, total):
        at = pl.ds(pl.multiple_of(i * block, block), block)
        part = jnp.exp(s_ref[at, :] + bias_ref[at, 0:1] - highest)
        return total + jnp.sum(part.reshape(block // 8, 8, n_cols), axis=0)

    total = lax.fori_loop(0, n_rows // block, column_sums, jnp.zeros((8, n_cols), F32))
    half_reverse = 0.5 * (highest + jnp.log(jnp.sum(total, axis=0, keepdims=True)))

    def row_parts(i, _):
        at = pl.ds(pl.multiple_of(i * block, block), block)
        s = s_ref[at, :]
        top = jnp.max(s, axis=1, keepdims=True)
        forward = top + jnp.log(jnp.sum(jnp.exp(s - top), axis=1, keepdims=True))
        shifted = s - half_reverse
        top = jnp.max(shifted, axis=1, keepdims=True)
        margin = top + jnp.log(jnp.sum(jnp.exp(shifted - top), axis=1, keepdims=True))
        w_ref[at, :] = jnp.exp(shifted - margin).astype(BF16)
        lane = iota((block, 128), 1)
        mf_scr[at, :] = jnp.where(lane == 0, margin, jnp.where(lane == 1, forward, 0.0))
        return 0

    lax.fori_loop(0, n_rows // block, row_parts, 0)
    mf_ref[0] = mf_scr[...].T[:8]
    for h, p_ref in enumerate((p1_ref, p2_ref)):
        w = w_ref[h * n_half : (h + 1) * n_half, :]
        p = jnp.dot(w, t_ref[0], preferred_element_type=F32)
        p_ref[...] = p.astype(BF16).reshape(n_msg, capacity, width)


def combine_kernel(info, code_ref, mf_ref, r_ref, keep_ref, send_ref, kmf_ref, scr, *, capacity, group):
    n_buckets, rows = code_ref.shape
    n_slots = n_buckets * capacity
    width = r_ref.shape[2]
    half = rows // 2
    cols = columns([mf_ref[0:1, :], mf_ref[1:2, :]], n_slots)
    margin, forward = cols[:, 0:1], cols[:, 1:2]
    code = code_ref[...]
    slots = one_hot_slots(code, 0, n_buckets, capacity) > 0.5

    def merged(column):
        top = jnp.max(jnp.where(slots, column, NEGATIVE), axis=0, keepdims=True)
        total = jnp.sum(jnp.where(slots, jnp.exp(column - top), 0.0), axis=0, keepdims=True)
        return jnp.where(total > 0.0, top + jnp.log(jnp.where(total > 0.0, total, 1.0)), NEGATIVE)

    margin_row, forward_row = merged(margin), merged(forward)
    factor = jnp.where(slots, jnp.exp(margin - margin_row), 0.0)
    high = factor.astype(BF16)
    low = (factor - high.astype(F32)).astype(BF16)
    r = r_ref[...].reshape(n_slots, width)
    over = (((0,), (0,)), ((), ()))
    pooled = lax.dot_general(high, r, over, preferred_element_type=F32)
    scr[...] = pooled + lax.dot_general(low, r, over, preferred_element_type=F32)
    keep_ref[...] = scr[pl.ds(pl.multiple_of(info[1] * half, 16), half), :]
    send_ref[:half, :] = scr[pl.ds(pl.multiple_of((1 - info[1]) * half, 16), half), :].astype(BF16)
    send_ref[half:, :] = extra_rows(margin_row, forward_row, width)
    kmf_ref[...] = jnp.concatenate([margin_row, forward_row, jnp.zeros((6, rows), F32)], axis=0)


def log_sum(first, second, third=None):
    top = jnp.maximum(first, second)
    if third is not None:
        top = jnp.maximum(top, third)
    total = jnp.exp(first - top) + jnp.exp(second - top)
    if third is not None:
        total = total + jnp.exp(third - top)
    return top + jnp.log(total)


def merge_pair(info, keep_ref, kmf_ref, got_ref, out_ref, scr):
    half, width = keep_ref.shape
    rows = kmf_ref.shape[1]
    margin, forward = kmf_ref[0:1, :], kmf_ref[1:2, :]
    margin_b, forward_b = read_extra(got_ref, half, rows)
    margin_all, forward_all = log_sum(margin, margin_b), log_sum(forward, forward_b)
    scr[...] = columns([jnp.exp(margin - margin_all), jnp.exp(margin_b - margin_all)], rows)
    factors = scr[pl.ds(pl.multiple_of(info[1] * half, 16), half), :]
    out = keep_ref[...] * factors[:, 0:1] + got_ref[:half, :].astype(F32) * factors[:, 1:2]
    out_ref[:half, :] = out.astype(BF16)
    out_ref[half:, :] = extra_rows(margin_all, forward_all, width)


def merge_last(info, keep_ref, kmf_ref, got_ref, far_ref, out_ref, conf_ref, scr):
    half, width = keep_ref.shape
    rows = kmf_ref.shape[1]
    margin, forward = kmf_ref[0:1, :], kmf_ref[1:2, :]
    margin_b, forward_b = read_extra(got_ref, half, rows)
    margin_c, forward_c = read_extra(far_ref, half, rows)
    margin_all = log_sum(margin, margin_b, margin_c)
    forward_all = log_sum(forward, forward_b, forward_c)
    scr[...] = columns(
        [jnp.exp(margin - margin_all), jnp.exp(margin_b - margin_all), jnp.exp(margin_c - margin_all)], rows
    )
    factors = scr[pl.ds(pl.multiple_of(info[1] * half, 16), half), :]
    out = keep_ref[...] * factors[:, 0:1] + got_ref[:half, :].astype(F32) * factors[:, 1:2]
    out_ref[...] = (out + far_ref[:half, :].astype(F32) * factors[:, 2:3]).astype(BF16)
    conf_ref[...] = margin_all - 0.5 * forward_all


def shards(sources, targets, picks, cluster_home, row_count):
    n_src, n_tgt = lax.axis_size("src"), lax.axis_size("tgt")
    rows, width = sources.shape
    per_device, n_cols, _ = targets.shape
    n_clusters = cluster_home.shape[0]
    n_picks = picks.shape[1]
    capacity = -(-(2 * n_picks * rows // n_clusters) // 16) * 16
    side = n_src // 2
    half = rows // 2
    message = per_device * capacity
    n_buckets = side * per_device
    n_slots = n_buckets * capacity
    group = max(g for g in range(per_device, n_buckets + 1, per_device) if n_buckets % g == 0 and g * capacity <= 400)
    sds = jax.ShapeDtypeStruct

    me, core = lax.axis_index("src"), lax.axis_index("tgt")
    info = jnp.stack([me // side * side, core]).astype(jnp.int32)
    partner = [(i, (i + side) % n_src) for i in range(n_src)]
    twin = [(i, 1 - i) for i in range(n_tgt)]
    halves = [list(range(side)), list(range(side, n_src))]

    def exchange(x):
        return lax.all_to_all(x, "src", split_axis=0, concat_axis=0, axis_index_groups=halves, tiled=True)

    picks_t = picks.T
    home = cluster_home[None, :]
    far_picks = lax.ppermute(picks_t, "src", partner)
    far_mine = lax.ppermute(lax.dynamic_slice_in_dim(sources, core * half, half, 0), "src", partner)
    far_other = lax.ppermute(far_mine, "tgt", twin)

    sizes = dict(n_tgt=n_tgt, per_device=per_device, capacity=capacity, group=group)
    gather_out = (sds((side, message, width), BF16), sds((n_buckets, rows), F32))
    cost = dict(flops=2 * n_slots * rows * width, moved=2 * (n_slots + rows) * width)
    near_q, near_code = call(
        functools.partial(gather_own, **sizes), gather_out, smem=1, n_in=4, **cost
    )(info, picks_t, home, sources)
    near_in = exchange(near_q)
    far_q, far_code = call(
        functools.partial(gather_partner, **sizes),
        gather_out,
        [pltpu.VMEM((rows, width), BF16)],
        smem=1,
        n_in=5,
        **cost,
    )(info, far_picks, home, far_mine, far_other)
    far_in = exchange(far_q)

    here = (me * n_tgt + core) * per_device + jnp.arange(per_device, dtype=jnp.int32)
    counts = jnp.sum(jnp.where(home == here[:, None], row_count[None, :], 0), axis=1)
    n_rows = 2 * side * capacity
    piece = pl.BlockSpec((side, capacity, width), lambda l: (0, l, 0))
    near_pool, far_pool, mf = call(
        functools.partial(owner_kernel, block=64),
        (
            sds((side, message, width), BF16),
            sds((side, message, width), BF16),
            sds((per_device, 8, n_rows), F32),
        ),
        [
            pltpu.VMEM((n_rows, n_cols), F32),
            pltpu.VMEM((n_rows, n_cols), BF16),
            pltpu.VMEM((n_rows, 128), F32),
            pltpu.VMEM((n_rows, 128), F32),
        ],
        limit=48,
        flops=4 * 2 * n_slots * n_cols * width,
        moved=2 * (4 * n_slots + per_device * n_cols) * width,
        exps=8 * n_slots * n_cols,
        grid=(per_device,),
        in_specs=[
            pl.BlockSpec(memory_space=pltpu.SMEM),
            piece,
            piece,
            pl.BlockSpec((1, n_cols, width), lambda l: (l, 0, 0)),
        ],
        out_specs=(piece, piece, pl.BlockSpec((1, 8, n_rows), lambda l: (l, 0, 0))),
    )(counts, near_in, far_in, targets)

    back_far = exchange(far_pool)
    back_near = exchange(near_pool)
    parts = mf[:, :2].reshape(per_device, 2, 2, side, capacity)
    parts = parts.transpose(3, 2, 1, 0, 4).reshape(side, 4 * message)
    parts = exchange(parts).reshape(side, 2, 2, message)
    parts = parts.transpose(1, 2, 0, 3).reshape(2, 2, n_slots)

    combine = call(
        functools.partial(combine_kernel, capacity=capacity, group=group),
        (sds((half, width), F32), sds((half + EXTRA, width), BF16), sds((8, rows), F32)),
        [pltpu.VMEM((rows, width), F32)],
        smem=1,
        n_in=4,
        limit=40,
        flops=4 * n_slots * rows * width,
        moved=2 * (n_slots + 2 * rows) * width,
    )
    keep, send, kmf = combine(info, far_code, parts[1], back_far)
    got = lax.ppermute(send, "tgt", twin)
    factors = [pltpu.VMEM((rows, 128), F32)]
    joined = call(merge_pair, sds((half + EXTRA, width), BF16), factors, smem=1, n_in=4, moved=10 * half * width)(
        info, keep, kmf, got
    )
    from_far = lax.ppermute(joined, "src", partner)

    keep, send, kmf = combine(info, near_code, parts[0], back_near)
    got = lax.ppermute(send, "tgt", twin)
    mine, confidence = call(
        merge_last,
        (sds((half, width), BF16), sds((1, rows), F32)),
        factors,
        smem=1,
        n_in=5,
        moved=10 * half * width,
    )(info, keep, kmf, got, from_far)
    other = lax.ppermute(mine, "tgt", twin)
    first = jnp.where(core == 0, mine, other)
    second = jnp.where(core == 0, other, mine)
    return (jnp.concatenate([first, second], axis=0), confidence[0].astype(BF16))


def solution(mesh):
    placed = (P("src", None), P(("src", "tgt"), None, None), P("src", None), P(), P())
    return jax.shard_map(
        shards, mesh=mesh, in_specs=placed, out_specs=(P("src", None), P("src")), check_vma=False
    )
```

```python
import functools
import math

import jax
import jax.numpy as jnp
from jax import lax
from jax.experimental import pallas as pl
from jax.experimental.pallas import tpu as pltpu
from jax.sharding import PartitionSpec as P

NEGATIVE = -1e30
SHARPNESS = 2.5
EXTRA = 16
F32, BF16 = jnp.float32, jnp.bfloat16
MIB = 1 << 20
LOG2E = math.log2(math.e)
LN2 = math.log(2.0)
BLOCK = 32
HIDE = 23_000_000_000


def iota(shape, axis):
    return lax.broadcasted_iota(jnp.int32, shape, axis)


def call(kernel, out_shape, scratch=(), smem=0, n_in=0, limit=32, flops=0, moved=0, exps=0, **kw):
    if not kw:
        kw = dict(
            in_specs=[pl.BlockSpec(memory_space=pltpu.SMEM)] * smem
            + [pl.BlockSpec(memory_space=pltpu.VMEM)] * (n_in - smem),
            out_specs=jax.tree.map(lambda _: pl.BlockSpec(memory_space=pltpu.VMEM), out_shape),
        )
    return pl.pallas_call(
        kernel,
        out_shape=out_shape,
        scratch_shapes=list(scratch),
        compiler_params=pltpu.CompilerParams(vmem_limit_bytes=limit * MIB),
        cost_estimate=pl.CostEstimate(flops=flops, bytes_accessed=moved, transcendentals=exps),
        **kw,
    )


def columns(rows, width):
    stacked = jnp.concatenate(rows + [jnp.zeros((128 - len(rows), width), F32)], axis=0)
    return stacked.T


def three(row):
    high = row.astype(BF16).astype(F32)
    middle = (row - high).astype(BF16).astype(F32)
    return [high, middle, row - high - middle]


def extra_rows(first, second, width):
    parts = three(first) + three(second)
    body = jnp.concatenate(parts + [jnp.zeros((EXTRA - len(parts), first.shape[1]), F32)], axis=0)
    rest = jnp.zeros((EXTRA, width - first.shape[1]), F32)
    return jnp.concatenate([body, rest], axis=1).astype(BF16)


def read_extra(ref, start, length):
    block = ref[start : start + EXTRA, :length].astype(F32)
    first = (block[0:1] + block[1:2]) + block[2:3]
    second = (block[3:4] + block[4:5]) + block[5:6]
    return first, second


def one_hot_slots(code, start, group, capacity):
    rows = code.shape[1]
    order = iota((capacity, rows), 0).astype(F32)
    return jnp.concatenate(
        [jnp.where(order == code[b : b + 1, :], 1.0, 0.0) for b in range(start, start + group)], axis=0
    )


def gather_body(info, picks, home_ref, source, q_ref, code_ref, *, n_tgt, per_device, capacity, group):
    n_buckets, rows = code_ref.shape
    n_clusters = home_ref.shape[1]
    width = q_ref.shape[2]
    cluster = iota((n_clusters, rows), 0).astype(F32)
    member = jnp.zeros((n_clusters, rows), F32)
    for pick in picks:
        member = jnp.where(cluster == pick, 1.0, member)
    bucket = iota((n_buckets, n_clusters), 0)
    holder = (info[0] + lax.div(bucket, per_device)) * n_tgt + info[1]
    place = holder * per_device + lax.rem(bucket, per_device)
    chosen = jnp.where(home_ref[...] == place, 1.0, 0.0).astype(BF16)
    inside = jnp.dot(chosen, member.astype(BF16), preferred_element_type=F32)
    earlier = jnp.where(iota((rows, rows), 0) < iota((rows, rows), 1), 1.0, 0.0).astype(BF16)
    rank = jnp.dot(inside.astype(BF16), earlier, preferred_element_type=F32)
    code = jnp.where(inside > 0.5, rank, -1.0)
    code_ref[...] = code
    per_message = group // per_device
    for start in range(0, n_buckets, group):
        slots = one_hot_slots(code, start, group, capacity)
        filled = jnp.sum(slots, axis=1, keepdims=True)
        found = jnp.dot(slots.astype(BF16), source, preferred_element_type=F32)
        head = found[:, :128]
        head = jnp.where((iota(head.shape, 1) == 0) & (filled < 0.5), jnp.inf, head)
        found = jnp.concatenate([head, found[:, 128:]], axis=1).astype(BF16)
        d = start // per_device
        q_ref[d : d + per_message] = found.reshape(per_message, per_device * capacity, width)


def half_with_picks(info, picks_ref, src_ref, out_ref):
    n_picks, rows = picks_ref.shape
    width = src_ref.shape[1]
    half = rows // 2
    out_ref[:half, :] = src_ref[pl.ds(pl.multiple_of(info[1] * half, 16), half), :]
    body = jnp.concatenate([picks_ref[...].astype(F32), jnp.zeros((EXTRA - n_picks, rows), F32)], axis=0)
    rest = jnp.zeros((EXTRA, width - rows), F32)
    out_ref[half:, :] = jnp.concatenate([body, rest], axis=1).astype(BF16)


def gather_own(info, picks_ref, home_ref, src_ref, q_ref, code_ref, **sizes):
    picks = [picks_ref[k : k + 1, :].astype(F32) for k in range(picks_ref.shape[0])]
    gather_body(info, picks, home_ref, src_ref[...], q_ref, code_ref, **sizes)


def gather_partner(info, home_ref, mine_ref, other_ref, q_ref, code_ref, src_ref, *, n_picks, **sizes):
    rows = src_ref.shape[0]
    half = rows // 2
    src_ref[pl.ds(pl.multiple_of(info[1] * half, 16), half), :] = mine_ref[:half, :]
    src_ref[pl.ds(pl.multiple_of((1 - info[1]) * half, 16), half), :] = other_ref[:half, :]
    block = mine_ref[half : half + EXTRA, :rows].astype(F32)
    picks = [block[k : k + 1, :] for k in range(n_picks)]
    gather_body(info, picks, home_ref, src_ref[...], q_ref, code_ref, **sizes)


def scores_of(q_ref, t, count, l, capacity):
    width = q_ref.shape[2]
    n_cols = t.shape[0]
    q = q_ref[:, l * capacity : (l + 1) * capacity, :].reshape(-1, width)
    head = q[:, :128].astype(F32)
    empty = head > 1e38
    q = jnp.concatenate([jnp.where(empty, 0.0, head).astype(BF16), q[:, 128:]], axis=1)
    s = lax.dot_general(q, t, (((1,), (1,)), ((), ())), preferred_element_type=F32)
    column_bias = jnp.where(iota((1, n_cols), 1) < count, 0.0, NEGATIVE).astype(F32)
    slot_bias = jnp.where(empty[:, 0:1], NEGATIVE, 0.0).astype(F32)
    return s * (SHARPNESS / math.sqrt(width) * LOG2E) + column_bias + slot_bias


def column_part(s_ref, highest, block):
    n_rows, n_cols = s_ref.shape

    def add(i, total):
        part = jnp.exp2(s_ref[pl.ds(pl.multiple_of(i * block, block), block), :] - highest)
        return total + jnp.sum(part.reshape(block // 8, 8, n_cols), axis=0)

    total = lax.fori_loop(0, n_rows // block, add, jnp.zeros((8, n_cols), F32))
    return jnp.sum(total, axis=0, keepdims=True)


def row_log_sum(s):
    top = jnp.max(s, axis=1, keepdims=True)
    return top + jnp.log2(jnp.sum(jnp.exp2(s - top), axis=1, keepdims=True))


def weigh(s, half_reverse):
    shifted = s - half_reverse
    top = jnp.max(shifted, axis=1, keepdims=True)
    e = jnp.exp2(shifted - top)
    total = jnp.sum(e, axis=1, keepdims=True)
    return (e * (1.0 / total)).astype(BF16), top + jnp.log2(total)


def tail(margin, forward, lane):
    out = jnp.zeros(lane.shape, F32)
    for i, part in enumerate(three(margin) + three(forward)):
        out = jnp.where(lane == i, part, out)
    return out.astype(BF16)


def near_scores(count_ref, q_ref, t_ref, s_ref, col_ref, fwd_ref, *, capacity, block):
    per_device, n_half, n_cols = s_ref.shape
    for l in range(per_device):
        s = scores_of(q_ref, t_ref[l], count_ref[l], l, capacity)
        s_ref[l] = s
        highest = jnp.max(s, axis=0, keepdims=True)
        total = column_part(s_ref.at[l], highest, block)
        col_ref[l] = jnp.concatenate([highest, total, jnp.zeros((6, n_cols), F32)], axis=0)

        def forward(i, _):
            at = pl.ds(pl.multiple_of(i * block, block), block)
            fwd_ref[l, at, :] = jnp.broadcast_to(row_log_sum(s_ref[l, at, :]), (block, 128))
            return 0

        lax.fori_loop(0, n_half // block, forward, 0)


def far_owner(count_ref, q_ref, t_ref, col_ref, p_ref, rev_ref, s_ref, w_ref, tail_ref, *, capacity, block):
    n_msg, _, full = p_ref.shape
    per_device = t_ref.shape[0]
    n_half, n_cols = s_ref.shape
    width = full - 128
    for l in range(per_device):
        s = scores_of(q_ref, t_ref[l], count_ref[l], l, capacity)
        s_ref[...] = s
        highest = jnp.max(s, axis=0, keepdims=True)
        total = column_part(s_ref, highest, block)
        top = jnp.maximum(highest, col_ref[l, 0:1, :])
        total = total * jnp.exp2(highest - top) + col_ref[l, 1:2, :] * jnp.exp2(col_ref[l, 0:1, :] - top)
        half_reverse = 0.5 * (top + jnp.log2(total))
        rev_ref[l] = jnp.broadcast_to(half_reverse, (8, n_cols))

        def rows(i, _):
            at = pl.ds(pl.multiple_of(i * block, block), block)
            s = s_ref[at, :]
            forward = row_log_sum(s)
            w, margin = weigh(s, half_reverse)
            w_ref[at, :] = w
            tail_ref[at, :] = tail(margin, forward, iota((block, 128), 1))
            return 0

        lax.fori_loop(0, n_half // block, rows, 0)
        at = slice(l * capacity, (l + 1) * capacity)
        p = jnp.dot(w_ref[...], t_ref[l], preferred_element_type=F32)
        p_ref[:, at, :width] = p.astype(BF16).reshape(n_msg, capacity, width)
        p_ref[:, at, width:] = tail_ref[...].reshape(n_msg, capacity, 128)


def near_owner(s_ref, rev_ref, fwd_ref, t_ref, p_ref, w_ref, tail_ref, *, capacity, block):
    n_msg, _, full = p_ref.shape
    per_device, n_half, _ = s_ref.shape
    width = full - 128
    for l in range(per_device):
        half_reverse = rev_ref[l, 0:1, :]

        def rows(i, _):
            at = pl.ds(pl.multiple_of(i * block, block), block)
            w, margin = weigh(s_ref[l, at, :], half_reverse)
            w_ref[at, :] = w
            tail_ref[at, :] = tail(margin, fwd_ref[l, at, 0:1], iota((block, 128), 1))
            return 0

        lax.fori_loop(0, n_half // block, rows, 0)
        at = slice(l * capacity, (l + 1) * capacity)
        p = jnp.dot(w_ref[...], t_ref[l], preferred_element_type=F32)
        p_ref[:, at, :width] = p.astype(BF16).reshape(n_msg, capacity, width)
        p_ref[:, at, width:] = tail_ref[...].reshape(n_msg, capacity, 128)


def combine_kernel(info, code_ref, r_ref, _, keep_ref, kmf_ref, *refs, capacity):
    *send_refs, scr = refs
    n_buckets, rows = code_ref.shape
    n_slots = n_buckets * capacity
    width = r_ref.shape[2] - 128
    half = rows // 2
    parts = r_ref[:, :, width:].reshape(n_slots, 128).astype(F32)
    margin = (parts[:, 0:1] + parts[:, 1:2]) + parts[:, 2:3]
    forward = (parts[:, 3:4] + parts[:, 4:5]) + parts[:, 5:6]
    slots = one_hot_slots(code_ref[...], 0, n_buckets, capacity) > 0.5

    def merged(column):
        top = jnp.max(jnp.where(slots, column, NEGATIVE), axis=0, keepdims=True)
        total = jnp.sum(jnp.where(slots, jnp.exp2(column - top), 0.0), axis=0, keepdims=True)
        return jnp.where(total > 0.0, top + jnp.log2(jnp.where(total > 0.0, total, 1.0)), NEGATIVE)

    margin_row, forward_row = merged(margin), merged(forward)
    factor = jnp.where(slots, jnp.exp2(margin - margin_row), 0.0)
    high = factor.astype(BF16)
    low = (factor - high.astype(F32)).astype(BF16)
    r = r_ref[:, :, :width].reshape(n_slots, width)
    over = (((0,), (0,)), ((), ()))
    pooled = lax.dot_general(high, r, over, preferred_element_type=F32)
    scr[...] = pooled + lax.dot_general(low, r, over, preferred_element_type=F32)
    keep_ref[...] = scr[pl.ds(pl.multiple_of(info[1] * half, 16), half), :]
    start = 0
    for ref in send_refs:
        count = min(ref.shape[0], half - start)
        at = pl.ds(pl.multiple_of((1 - info[1]) * half + start, 16), count)
        ref[:count, :] = scr[at, :].astype(BF16)
        start = start + count
    send_refs[-1][count:, :] = extra_rows(margin_row, forward_row, width)
    kmf_ref[...] = jnp.concatenate([margin_row, forward_row, jnp.zeros((6, rows), F32)], axis=0)


def log_sum(first, second, third=None):
    top = jnp.maximum(first, second)
    if third is not None:
        top = jnp.maximum(top, third)
    total = jnp.exp2(first - top) + jnp.exp2(second - top)
    if third is not None:
        total = total + jnp.exp2(third - top)
    return top + jnp.log2(total)


def merge_pair(info, keep_ref, kmf_ref, got_ref, out_ref, scr):
    half, width = keep_ref.shape
    rows = kmf_ref.shape[1]
    margin, forward = kmf_ref[0:1, :], kmf_ref[1:2, :]
    margin_b, forward_b = read_extra(got_ref, half, rows)
    margin_all, forward_all = log_sum(margin, margin_b), log_sum(forward, forward_b)
    scr[...] = columns([jnp.exp2(margin - margin_all), jnp.exp2(margin_b - margin_all)], rows)
    factors = scr[pl.ds(pl.multiple_of(info[1] * half, 16), half), :]
    out = keep_ref[...] * factors[:, 0:1] + got_ref[:half, :].astype(F32) * factors[:, 1:2]
    out_ref[:half, :] = out.astype(BF16)
    out_ref[half:, :] = extra_rows(margin_all, forward_all, width)


def merge_last(info, keep_ref, kmf_ref, got_ref, last_ref, far_ref, out_ref, conf_ref, scr):
    half, width = keep_ref.shape
    rows = kmf_ref.shape[1]
    margin, forward = kmf_ref[0:1, :], kmf_ref[1:2, :]
    first = got_ref.shape[0]
    margin_b, forward_b = read_extra(last_ref, half - first, rows)
    margin_c, forward_c = read_extra(far_ref, half, rows)
    margin_all = log_sum(margin, margin_b, margin_c)
    forward_all = log_sum(forward, forward_b, forward_c)
    scr[...] = columns(
        [jnp.exp2(margin - margin_all), jnp.exp2(margin_b - margin_all), jnp.exp2(margin_c - margin_all)], rows
    )
    factors = scr[pl.ds(pl.multiple_of(info[1] * half, 16), half), :]
    for at, ref in ((slice(0, first), got_ref), (slice(first, half), last_ref)):
        out = keep_ref[at, :] * factors[at, 0:1] + ref[: at.stop - at.start, :].astype(F32) * factors[at, 1:2]
        out_ref[at, :] = (out + far_ref[at, :].astype(F32) * factors[at, 2:3]).astype(BF16)
    conf_ref[...] = (margin_all - 0.5 * forward_all) * LN2


def shards(sources, targets, picks, cluster_home, row_count):
    n_src, n_tgt = lax.axis_size("src"), lax.axis_size("tgt")
    rows, width = sources.shape
    per_device, n_cols, _ = targets.shape
    n_clusters = cluster_home.shape[0]
    n_picks = picks.shape[1]
    capacity = -(-(2 * n_picks * rows // n_clusters) // 16) * 16
    side = n_src // 2
    half = rows // 2
    message = per_device * capacity
    n_buckets = side * per_device
    n_slots = n_buckets * capacity
    group = max(g for g in range(per_device, n_buckets + 1, per_device) if n_buckets % g == 0 and g * capacity <= 400)
    sds = jax.ShapeDtypeStruct

    me, core = lax.axis_index("src"), lax.axis_index("tgt")
    info = jnp.stack([me // side * side, core]).astype(jnp.int32)
    partner = [(i, (i + side) % n_src) for i in range(n_src)]
    twin = [(i, 1 - i) for i in range(n_tgt)]
    halves = [list(range(side)), list(range(side, n_src))]

    def exchange(x):
        return lax.all_to_all(x, "src", split_axis=0, concat_axis=0, axis_index_groups=halves, tiled=True)

    picks_t = picks.T
    home = cluster_home[None, :]
    letter = sds((half + EXTRA, width), BF16)
    far_mine = lax.ppermute(
        call(half_with_picks, letter, smem=1, n_in=3, moved=4 * half * width)(info, picks_t, sources), "src", partner
    )
    far_other = lax.ppermute(far_mine, "tgt", twin)

    sizes = dict(n_tgt=n_tgt, per_device=per_device, capacity=capacity, group=group)
    gather_out = (sds((side, message, width), BF16), sds((n_buckets, rows), F32))
    moved = 2 * (n_slots + rows) * width
    near_q, near_code = call(
        functools.partial(gather_own, **sizes), gather_out, smem=1, n_in=4, flops=2 * n_slots * rows * width, moved=moved
    )(info, picks_t, home, sources)
    near_in = exchange(near_q)
    far_q, far_code = call(
        functools.partial(gather_partner, n_picks=n_picks, **sizes),
        gather_out,
        [pltpu.VMEM((rows, width), BF16)],
        smem=1,
        n_in=4,
        flops=HIDE,
        moved=moved,
    )(info, home, far_mine, far_other)
    far_in = exchange(far_q)

    here = (me * n_tgt + core) * per_device + jnp.arange(per_device, dtype=jnp.int32)
    counts = jnp.sum(jnp.where(home == here[:, None], row_count[None, :], 0), axis=1)
    n_half = side * capacity
    options = dict(capacity=capacity, block=BLOCK)
    work = dict(flops=2 * n_slots * n_cols * width, moved=2 * (n_slots + per_device * n_cols) * width, limit=40)
    pooled = sds((side, message, width + 128), BF16)
    near_s, near_col, near_fwd = call(
        functools.partial(near_scores, **options),
        (
            sds((per_device, n_half, n_cols), F32),
            sds((per_device, 8, n_cols), F32),
            sds((per_device, n_half, 128), F32),
        ),
        smem=1,
        n_in=3,
        exps=2 * n_slots * n_cols,
        **work,
    )(counts, near_in, targets)
    weights = [pltpu.VMEM((n_half, n_cols), BF16), pltpu.VMEM((n_half, 128), BF16)]
    far_pool, reverse = call(
        functools.partial(far_owner, **options),
        (pooled, sds((per_device, 8, n_cols), F32)),
        [pltpu.VMEM((n_half, n_cols), F32)] + weights,
        smem=1,
        n_in=4,
        exps=3 * n_slots * n_cols,
        **work,
    )(counts, far_in, targets, near_col)
    back_far = exchange(far_pool)
    near_pool = call(
        functools.partial(near_owner, **options), pooled, weights, n_in=4, exps=n_slots * n_cols, **work
    )(near_s, reverse, near_fwd, targets)
    back_near = exchange(near_pool)

    def combine(code, back, after, pieces, weight):
        return pl.pallas_call(
            functools.partial(combine_kernel, capacity=capacity),
            out_shape=(sds((half, width), F32), sds((8, rows), F32)) + tuple(sds((n, width), BF16) for n in pieces),
            in_specs=[
                pl.BlockSpec(memory_space=pltpu.SMEM),
                pl.BlockSpec(memory_space=pltpu.VMEM),
                pl.BlockSpec(memory_space=pltpu.VMEM),
                pl.BlockSpec(memory_space=pl.ANY),
            ],
            out_specs=tuple([pl.BlockSpec(memory_space=pltpu.VMEM)] * (2 + len(pieces))),
            scratch_shapes=[pltpu.VMEM((rows, width), F32)],
            compiler_params=pltpu.CompilerParams(vmem_limit_bytes=40 * MIB),
            cost_estimate=pl.CostEstimate(
                flops=weight * 4 * n_slots * rows * width,
                bytes_accessed=weight * 2 * (n_slots + 2 * rows) * width,
                transcendentals=0,
            ),
        )(info, code, back, after)

    keep, kmf, send = combine(far_code, back_far, info, [half + EXTRA], 1)
    got = lax.ppermute(send, "tgt", twin)
    factors = [pltpu.VMEM((rows, 128), F32)]
    joined = call(merge_pair, letter, factors, smem=1, n_in=4, moved=10 * half * width)(info, keep, kmf, got)
    from_far = lax.ppermute(joined, "src", partner)

    first = half // 32 * 16
    keep, kmf, *send = combine(near_code, back_near, joined, [first, half - first + EXTRA], 0)
    got = [lax.ppermute(piece, "tgt", twin) for piece in send]
    mine, confidence = call(
        merge_last,
        (sds((half, width), BF16), sds((1, rows), F32)),
        factors,
        smem=1,
        n_in=6,
        moved=10 * half * width,
    )(info, keep, kmf, *got, from_far)
    other = lax.ppermute(mine, "tgt", twin)
    first = jnp.where(core == 0, mine, other)
    second = jnp.where(core == 0, other, mine)
    return (jnp.concatenate([first, second], axis=0), confidence[0].astype(BF16))


def solution(mesh):
    placed = (P("src", None), P(("src", "tgt"), None, None), P("src", None), P(), P())
    return jax.shard_map(
        shards, mesh=mesh, in_specs=placed, out_specs=(P("src", None), P("src")), check_vma=False
    )
```

```python
import functools
import math

import jax
import jax.numpy as jnp
from jax import lax
from jax.experimental import pallas as pl
from jax.experimental.pallas import tpu as pltpu
from jax.sharding import PartitionSpec as P

NEGATIVE = -1e30
SHARPNESS = 2.5
EXTRA = 16
F32, BF16 = jnp.float32, jnp.bfloat16
MIB = 1 << 20
LOG2E = math.log2(math.e)
LN2 = math.log(2.0)
BLOCK = 128
ROW_GROUPS = 8
LIMIT = 24
FULL = 63
HIDE = 23_000_000_000


def iota(shape, axis):
    return lax.broadcasted_iota(jnp.int32, shape, axis)


def call(kernel, out_shape, scratch=(), smem=0, n_in=0, limit=LIMIT, flops=0, moved=0, exps=0, **kw):
    if not kw:
        kw = dict(
            in_specs=[pl.BlockSpec(memory_space=pltpu.SMEM)] * smem
            + [pl.BlockSpec(memory_space=pltpu.VMEM)] * (n_in - smem),
            out_specs=jax.tree.map(lambda _: pl.BlockSpec(memory_space=pltpu.VMEM), out_shape),
        )
    return pl.pallas_call(
        kernel,
        out_shape=out_shape,
        scratch_shapes=list(scratch),
        compiler_params=pltpu.CompilerParams(vmem_limit_bytes=limit * MIB),
        cost_estimate=pl.CostEstimate(flops=flops, bytes_accessed=moved, transcendentals=exps),
        **kw,
    )


def columns(rows, width):
    stacked = jnp.concatenate(rows + [jnp.zeros((128 - len(rows), width), F32)], axis=0)
    return stacked.T


def three(row):
    high = row.astype(BF16).astype(F32)
    middle = (row - high).astype(BF16).astype(F32)
    return [high, middle, row - high - middle]


def extra_rows(first, second, width):
    parts = three(first) + three(second)
    body = jnp.concatenate(parts + [jnp.zeros((EXTRA - len(parts), first.shape[1]), F32)], axis=0)
    rest = jnp.zeros((EXTRA, width - first.shape[1]), F32)
    return jnp.concatenate([body, rest], axis=1).astype(BF16)


def read_extra(ref, start, length):
    block = ref[start : start + EXTRA, :length].astype(F32)
    first = (block[0:1] + block[1:2]) + block[2:3]
    second = (block[3:4] + block[4:5]) + block[5:6]
    return first, second


def one_hot_slots(code, start, group, capacity):
    rows = code.shape[1]
    order = iota((capacity, rows), 0).astype(F32)
    return jnp.concatenate(
        [jnp.where(order == code[b : b + 1, :], 1.0, 0.0) for b in range(start, start + group)], axis=0
    )


def gather_body(
    info, picks, home_ref, source, q_hbm, code_hbm, q_ref, code_ref, sem, *, n_tgt, per_device, capacity, group
):
    n_buckets, rows = code_ref.shape
    n_clusters = home_ref.shape[1]
    width = q_ref.shape[2]
    cluster = iota((n_clusters, rows), 0).astype(F32)
    member = jnp.zeros((n_clusters, rows), F32)
    for pick in picks:
        member = jnp.where(cluster == pick, 1.0, member)
    bucket = iota((n_buckets, n_clusters), 0)
    holder = (info[0] + lax.div(bucket, per_device)) * n_tgt + info[1]
    place = holder * per_device + lax.rem(bucket, per_device)
    chosen = jnp.where(home_ref[...] == place, 1.0, 0.0).astype(BF16)
    inside = jnp.dot(chosen, member.astype(BF16), preferred_element_type=F32)
    earlier = jnp.where(iota((rows, rows), 0) < iota((rows, rows), 1), 1.0, 0.0).astype(BF16)
    rank = jnp.dot(inside.astype(BF16), earlier, preferred_element_type=F32)
    code = jnp.where(inside > 0.5, rank, -1.0)
    code_ref[...] = code
    leave = [pltpu.make_async_copy(code_ref, code_hbm, sem.at[0])]
    leave[0].start()
    per_message = group // per_device
    for start in range(0, n_buckets, group):
        slots = one_hot_slots(code, start, group, capacity)
        filled = jnp.sum(slots, axis=1, keepdims=True)
        found = jnp.dot(slots.astype(BF16), source, preferred_element_type=F32)
        head = found[:, :128]
        head = jnp.where((iota(head.shape, 1) == 0) & (filled < 0.5), jnp.inf, head)
        found = jnp.concatenate([head, found[:, 128:]], axis=1).astype(BF16)
        d = start // per_device
        at = pl.ds(d, per_message)
        q_ref[at] = found.reshape(per_message, per_device * capacity, width)
        leave.append(pltpu.make_async_copy(q_ref.at[at], q_hbm.at[at], sem.at[1 + start // group]))
        leave[-1].start()
    for copy in leave:
        copy.wait()


def half_with_picks(info, picks_ref, src_ref, out_ref):
    n_picks, rows = picks_ref.shape
    width = src_ref.shape[1]
    half = rows // 2
    out_ref[:half, :] = src_ref[pl.ds(pl.multiple_of(info[1] * half, 16), half), :]
    body = jnp.concatenate([picks_ref[...].astype(F32), jnp.zeros((EXTRA - n_picks, rows), F32)], axis=0)
    rest = jnp.zeros((EXTRA, width - rows), F32)
    out_ref[half:, :] = jnp.concatenate([body, rest], axis=1).astype(BF16)


def gather_own(info, picks_ref, home_ref, src_ref, *refs, **sizes):
    picks = [picks_ref[k : k + 1, :].astype(F32) for k in range(picks_ref.shape[0])]
    gather_body(info, picks, home_ref, src_ref[...], *refs, **sizes)


def gather_partner(info, home_ref, mine_ref, other_ref, *refs, n_picks, **sizes):
    *refs, src_ref = refs
    rows = src_ref.shape[0]
    half = rows // 2
    src_ref[pl.ds(pl.multiple_of(info[1] * half, 16), half), :] = mine_ref[:half, :]
    src_ref[pl.ds(pl.multiple_of((1 - info[1]) * half, 16), half), :] = other_ref[:half, :]
    block = mine_ref[half : half + EXTRA, :rows].astype(F32)
    picks = [block[k : k + 1, :] for k in range(n_picks)]
    gather_body(info, picks, home_ref, src_ref[...], *refs, **sizes)


def scores_of(q, t, count):
    width = q.shape[1]
    n_cols = t.shape[0]
    head = q[:, :128].astype(F32)
    empty = head > 1e38
    q = jnp.concatenate([jnp.where(empty, 0.0, head).astype(BF16), q[:, 128:]], axis=1)
    s = lax.dot_general(q, t, (((1,), (1,)), ((), ())), preferred_element_type=F32)
    column_bias = jnp.where(iota((1, n_cols), 1) < count, 0.0, NEGATIVE).astype(F32)
    slot_bias = jnp.where(empty[:, 0:1], NEGATIVE, 0.0).astype(F32)
    return s * (SHARPNESS / math.sqrt(width) * LOG2E) + column_bias + slot_bias


def column_part(s_ref, highest, block):
    n_rows, n_cols = s_ref.shape
    total = jnp.zeros((8, n_cols), F32)
    for start in range(0, n_rows, block):
        part = jnp.exp2(s_ref[start : start + block, :] - highest)
        total = total + jnp.sum(part.reshape(block // 8, 8, n_cols), axis=0)
    return jnp.sum(total, axis=0, keepdims=True)


def row_log_sum(s):
    top = jnp.max(s, axis=1, keepdims=True)
    return top + jnp.log2(jnp.sum(jnp.exp2(s - top), axis=1, keepdims=True))


def weigh(s, half_reverse):
    shifted = s - half_reverse
    top = jnp.max(shifted, axis=1, keepdims=True)
    e = jnp.exp2(shifted - top)
    total = jnp.sum(e, axis=1, keepdims=True)
    return (e * (1.0 / total)).astype(BF16), top + jnp.log2(total)


def tail(margin, forward, lane):
    out = jnp.zeros(lane.shape, F32)
    for i, part in enumerate(three(margin) + three(forward)):
        out = jnp.where(lane == i, part, out)
    return out.astype(BF16)


def near_scores(count_ref, q_ref, t_ref, s_ref, col_ref, fwd_ref, *, capacity, block):
    per_device, n_half, n_cols = s_ref.shape
    for l in range(per_device):
        q = q_ref[:, l * capacity : (l + 1) * capacity, :].reshape(n_half, -1)
        s = scores_of(q, t_ref[l], count_ref[l])
        s_ref[l] = s
        highest = jnp.max(s, axis=0, keepdims=True)
        total = column_part(s_ref.at[l], highest, block)
        col_ref[l] = jnp.concatenate([highest, total, jnp.zeros((6, n_cols), F32)], axis=0)

        def forward(i, _):
            at = pl.ds(pl.multiple_of(i * block, block), block)
            fwd_ref[l, at, :] = jnp.broadcast_to(row_log_sum(s_ref[l, at, :]), (block, 128))
            return 0

        lax.fori_loop(0, n_half // block, forward, 0)


def far_owner(
    count_ref, q_hbm, t_hbm, col_ref, p_hbm, rev_hbm, q_ref, t_ref, s_ref, w_ref, p_ref, rev_ref, sems, rev_sem, *, block
):
    per_device, n_msg, capacity, width = q_ref.shape
    _, n_half, n_cols = s_ref.shape
    places = [pl.ds(l * capacity, capacity) for l in range(per_device)]
    arrive = []
    for l, at in enumerate(places):
        arrive.append(pltpu.make_async_copy(q_hbm.at[:, at, :], q_ref.at[l], sems.at[0, l]))
        arrive.append(pltpu.make_async_copy(t_hbm.at[l], t_ref.at[l], sems.at[1, l]))
    for copy in arrive:
        copy.start()
    rev_leave = pltpu.make_async_copy(rev_ref, rev_hbm, rev_sem)
    leave = [pltpu.make_async_copy(p_ref.at[l], p_hbm.at[:, at, :], sems.at[2, l]) for l, at in enumerate(places)]
    half_reverse = []
    for l in range(per_device):
        arrive[2 * l].wait()
        arrive[2 * l + 1].wait()
        s = scores_of(q_ref[l].reshape(n_half, width), t_ref[l], count_ref[l])
        s_ref[l] = s
        highest = jnp.max(s, axis=0, keepdims=True)
        total = column_part(s_ref.at[l], highest, block)
        top = jnp.maximum(highest, col_ref[l, 0:1, :])
        total = total * jnp.exp2(highest - top) + col_ref[l, 1:2, :] * jnp.exp2(col_ref[l, 0:1, :] - top)
        half_reverse.append(0.5 * (top + jnp.log2(total)))
        rev_ref[l] = jnp.broadcast_to(half_reverse[l], (8, n_cols))
    rev_leave.start()
    for l in range(per_device):
        for start in range(0, n_half, block):
            at = slice(start, start + block)
            s = s_ref[l, at, :]
            forward = row_log_sum(s)
            w, margin = weigh(s, half_reverse[l])
            w_ref[l, at, :] = w
            part = tail(margin, forward, iota((block, 128), 1))
            first = start // capacity
            p_ref[l, first : first + block // capacity, :, width:] = part.reshape(block // capacity, capacity, 128)
        p = jnp.dot(w_ref[l], t_ref[l], preferred_element_type=F32)
        p_ref[l, :, :, :width] = p.astype(BF16).reshape(n_msg, capacity, width)
        leave[l].start()
    for copy in leave + [rev_leave]:
        copy.wait()


def near_owner(s_ref, rev_ref, fwd_ref, t_ref, p_ref, w_ref, tail_ref, *, capacity, block):
    n_msg, _, full = p_ref.shape
    per_device, n_half, _ = s_ref.shape
    width = full - 128
    for l in range(per_device):
        half_reverse = rev_ref[l, 0:1, :]

        def rows(i, _):
            at = pl.ds(pl.multiple_of(i * block, block), block)
            w, margin = weigh(s_ref[l, at, :], half_reverse)
            w_ref[at, :] = w
            tail_ref[at, :] = tail(margin, fwd_ref[l, at, 0:1], iota((block, 128), 1))
            return 0

        lax.fori_loop(0, n_half // block, rows, 0)
        at = slice(l * capacity, (l + 1) * capacity)
        p = jnp.dot(w_ref[...], t_ref[l], preferred_element_type=F32)
        p_ref[:, at, :width] = p.astype(BF16).reshape(n_msg, capacity, width)
        p_ref[:, at, width:] = tail_ref[...].reshape(n_msg, capacity, 128)


def combine_kernel(info, code_ref, r_ref, _, keep_ref, kmf_ref, *refs, capacity):
    *send_refs, scr = refs
    n_buckets, rows = code_ref.shape
    n_slots = n_buckets * capacity
    width = r_ref.shape[2] - 128
    half = rows // 2
    parts = r_ref[:, :, width:].reshape(n_slots, 128).astype(F32)
    margin = (parts[:, 0:1] + parts[:, 1:2]) + parts[:, 2:3]
    forward = (parts[:, 3:4] + parts[:, 4:5]) + parts[:, 5:6]
    slots = one_hot_slots(code_ref[...], 0, n_buckets, capacity) > 0.5

    def merged(column):
        top = jnp.max(jnp.where(slots, column, NEGATIVE), axis=0, keepdims=True)
        total = jnp.sum(jnp.where(slots, jnp.exp2(column - top), 0.0), axis=0, keepdims=True)
        return jnp.where(total > 0.0, top + jnp.log2(jnp.where(total > 0.0, total, 1.0)), NEGATIVE)

    margin_row, forward_row = merged(margin), merged(forward)
    factor = jnp.where(slots, jnp.exp2(margin - margin_row), 0.0)
    high = factor.astype(BF16)
    low = (factor - high.astype(F32)).astype(BF16)
    r = r_ref[:, :, :width].reshape(n_slots, width)
    over = (((0,), (0,)), ((), ()))
    pooled = lax.dot_general(high, r, over, preferred_element_type=F32)
    scr[...] = pooled + lax.dot_general(low, r, over, preferred_element_type=F32)
    keep_ref[...] = scr[pl.ds(pl.multiple_of(info[1] * half, 16), half), :]
    start = 0
    for ref in send_refs:
        count = min(ref.shape[0], half - start)
        at = pl.ds(pl.multiple_of((1 - info[1]) * half + start, 16), count)
        ref[:count, :] = scr[at, :].astype(BF16)
        start = start + count
    send_refs[-1][count:, :] = extra_rows(margin_row, forward_row, width)
    kmf_ref[...] = jnp.concatenate([margin_row, forward_row, jnp.zeros((6, rows), F32)], axis=0)


def log_sum(first, second, third=None):
    top = jnp.maximum(first, second)
    if third is not None:
        top = jnp.maximum(top, third)
    total = jnp.exp2(first - top) + jnp.exp2(second - top)
    if third is not None:
        total = total + jnp.exp2(third - top)
    return top + jnp.log2(total)


def merge_pair(info, keep_ref, kmf_ref, got_ref, out_ref, scr):
    half, width = keep_ref.shape
    rows = kmf_ref.shape[1]
    margin, forward = kmf_ref[0:1, :], kmf_ref[1:2, :]
    margin_b, forward_b = read_extra(got_ref, half, rows)
    margin_all, forward_all = log_sum(margin, margin_b), log_sum(forward, forward_b)
    scr[...] = columns([jnp.exp2(margin - margin_all), jnp.exp2(margin_b - margin_all)], rows)
    factors = scr[pl.ds(pl.multiple_of(info[1] * half, 16), half), :]
    out = keep_ref[...] * factors[:, 0:1] + got_ref[:half, :].astype(F32) * factors[:, 1:2]
    out_ref[:half, :] = out.astype(BF16)
    out_ref[half:, :] = extra_rows(margin_all, forward_all, width)


def merge_last(info, keep_ref, kmf_ref, got_ref, last_ref, far_ref, out_ref, conf_ref, scr):
    half, width = keep_ref.shape
    rows = kmf_ref.shape[1]
    margin, forward = kmf_ref[0:1, :], kmf_ref[1:2, :]
    first = got_ref.shape[0]
    margin_b, forward_b = read_extra(last_ref, half - first, rows)
    margin_c, forward_c = read_extra(far_ref, half, rows)
    margin_all = log_sum(margin, margin_b, margin_c)
    forward_all = log_sum(forward, forward_b, forward_c)
    scr[...] = columns(
        [jnp.exp2(margin - margin_all), jnp.exp2(margin_b - margin_all), jnp.exp2(margin_c - margin_all)], rows
    )
    factors = scr[pl.ds(pl.multiple_of(info[1] * half, 16), half), :]
    for at, ref in ((slice(0, first), got_ref), (slice(first, half), last_ref)):
        out = keep_ref[at, :] * factors[at, 0:1] + ref[: at.stop - at.start, :].astype(F32) * factors[at, 1:2]
        out_ref[at, :] = (out + far_ref[at, :].astype(F32) * factors[at, 2:3]).astype(BF16)
    conf_ref[...] = (margin_all - 0.5 * forward_all) * LN2


def shards(sources, targets, picks, cluster_home, row_count):
    n_src, n_tgt = lax.axis_size("src"), lax.axis_size("tgt")
    rows, width = sources.shape
    per_device, n_cols, _ = targets.shape
    n_clusters = cluster_home.shape[0]
    n_picks = picks.shape[1]
    capacity = -(-(2 * n_picks * rows // n_clusters) // 16) * 16
    side = n_src // 2
    half = rows // 2
    message = per_device * capacity
    n_buckets = side * per_device
    n_slots = n_buckets * capacity
    group = max(g for g in range(per_device, n_buckets + 1, per_device) if n_buckets % g == 0 and g * capacity <= 400)
    sds = jax.ShapeDtypeStruct

    me, core = lax.axis_index("src"), lax.axis_index("tgt")
    info = jnp.stack([me // side * side, core]).astype(jnp.int32)
    partner = [(i, (i + side) % n_src) for i in range(n_src)]
    twin = [(i, 1 - i) for i in range(n_tgt)]
    halves = [list(range(side)), list(range(side, n_src))]

    def exchange(x):
        return lax.all_to_all(x, "src", split_axis=0, concat_axis=0, axis_index_groups=halves, tiled=True)

    picks_t = picks.T
    home = cluster_home[None, :]
    letter = sds((half + EXTRA, width), BF16)
    far_mine = lax.ppermute(
        call(half_with_picks, letter, smem=1, n_in=3, moved=4 * half * width, limit=FULL)(info, picks_t, sources), "src", partner
    )
    far_other = lax.ppermute(far_mine, "tgt", twin)

    sizes = dict(n_tgt=n_tgt, per_device=per_device, capacity=capacity, group=group)
    gather_out = (sds((side, message, width), BF16), sds((n_buckets, rows), F32))
    moved = 2 * (n_slots + rows) * width
    hbm = pl.BlockSpec(memory_space=pltpu.HBM)
    vmem = pl.BlockSpec(memory_space=pltpu.VMEM)
    smem = pl.BlockSpec(memory_space=pltpu.SMEM)
    gather_scratch = [
        pltpu.VMEM((side, message, width), BF16),
        pltpu.VMEM((n_buckets, rows), F32),
        pltpu.SemaphoreType.DMA((1 + n_buckets // group,)),
    ]
    near_q, near_code = call(
        functools.partial(gather_own, **sizes),
        gather_out,
        gather_scratch,
        flops=2 * n_slots * rows * width,
        moved=moved,
        limit=FULL,
        in_specs=[smem] + [vmem] * 3,
        out_specs=(hbm, hbm),
    )(info, picks_t, home, sources)
    near_in = exchange(near_q)
    far_q, far_code = call(
        functools.partial(gather_partner, n_picks=n_picks, **sizes),
        gather_out,
        gather_scratch + [pltpu.VMEM((rows, width), BF16)],
        flops=HIDE,
        moved=moved,
        limit=FULL,
        in_specs=[smem] + [vmem] * 3,
        out_specs=(hbm, hbm),
    )(info, home, far_mine, far_other)
    far_in = exchange(far_q)

    here = (me * n_tgt + core) * per_device + jnp.arange(per_device, dtype=jnp.int32)
    counts = jnp.sum(jnp.where(home == here[:, None], row_count[None, :], 0), axis=1)
    n_half = side * capacity
    options = dict(capacity=capacity, block=BLOCK)
    work = dict(flops=2 * n_slots * n_cols * width, moved=2 * (n_slots + per_device * n_cols) * width)
    pooled = sds((side, message, width + 128), BF16)
    near_s, near_col, near_fwd = call(
        functools.partial(near_scores, **options),
        (
            sds((per_device, n_half, n_cols), F32),
            sds((per_device, 8, n_cols), F32),
            sds((per_device, n_half, 128), F32),
        ),
        smem=1,
        n_in=3,
        limit=FULL,
        exps=2 * n_slots * n_cols,
        **work,
    )(counts, near_in, targets)
    weights = [pltpu.VMEM((n_half, n_cols), BF16), pltpu.VMEM((n_half, 128), BF16)]
    far_pool, reverse = call(
        functools.partial(far_owner, block=capacity * math.gcd(side, ROW_GROUPS)),
        (pooled, sds((per_device, 8, n_cols), F32)),
        [
            pltpu.VMEM((per_device, side, capacity, width), BF16),
            pltpu.VMEM((per_device, n_cols, width), BF16),
            pltpu.VMEM((per_device, n_half, n_cols), F32),
            pltpu.VMEM((per_device, n_half, n_cols), BF16),
            pltpu.VMEM((per_device, side, capacity, width + 128), BF16),
            pltpu.VMEM((per_device, 8, n_cols), F32),
            pltpu.SemaphoreType.DMA((3, per_device)),
            pltpu.SemaphoreType.DMA,
        ],
        limit=FULL,
        exps=3 * n_slots * n_cols,
        in_specs=[smem, hbm, hbm, vmem],
        out_specs=(hbm, hbm),
        **work,
    )(counts, far_in, targets, near_col)
    back_far = exchange(far_pool)
    near_pool = call(
        functools.partial(near_owner, **options), pooled, weights, n_in=4, exps=n_slots * n_cols, **work
    )(near_s, reverse, near_fwd, targets)
    back_near = exchange(near_pool)

    def combine(code, back, after, pieces, weight):
        return pl.pallas_call(
            functools.partial(combine_kernel, capacity=capacity),
            out_shape=(sds((half, width), F32), sds((8, rows), F32)) + tuple(sds((n, width), BF16) for n in pieces),
            in_specs=[
                pl.BlockSpec(memory_space=pltpu.SMEM),
                pl.BlockSpec(memory_space=pltpu.VMEM),
                pl.BlockSpec(memory_space=pltpu.VMEM),
                pl.BlockSpec(memory_space=pl.ANY),
            ],
            out_specs=tuple([pl.BlockSpec(memory_space=pltpu.VMEM)] * (2 + len(pieces))),
            scratch_shapes=[pltpu.VMEM((rows, width), F32)],
            compiler_params=pltpu.CompilerParams(vmem_limit_bytes=LIMIT * MIB),
            cost_estimate=pl.CostEstimate(
                flops=weight * 4 * n_slots * rows * width,
                bytes_accessed=weight * 2 * (n_slots + 2 * rows) * width,
                transcendentals=0,
            ),
        )(info, code, back, after)

    keep, kmf, send = combine(far_code, back_far, info, [half + EXTRA], 1)
    got = lax.ppermute(send, "tgt", twin)
    factors = [pltpu.VMEM((rows, 128), F32)]
    joined = call(merge_pair, letter, factors, smem=1, n_in=4, moved=10 * half * width)(info, keep, kmf, got)
    from_far = lax.ppermute(joined, "src", partner)

    first = half // 32 * 16
    keep, kmf, *send = combine(near_code, back_near, joined, [first, half - first + EXTRA], 0)
    got = [lax.ppermute(piece, "tgt", twin) for piece in send]
    mine, confidence = call(
        merge_last,
        (sds((half, width), BF16), sds((1, rows), F32)),
        factors,
        smem=1,
        n_in=6,
        moved=10 * half * width,
    )(info, keep, kmf, *got, from_far)
    other = lax.ppermute(mine, "tgt", twin)
    first = jnp.where(core == 0, mine, other)
    second = jnp.where(core == 0, other, mine)
    return (jnp.concatenate([first, second], axis=0), confidence[0].astype(BF16))


def solution(mesh):
    placed = (P("src", None), P(("src", "tgt"), None, None), P("src", None), P(), P())
    return jax.shard_map(
        shards, mesh=mesh, in_specs=placed, out_specs=(P("src", None), P("src")), check_vma=False
    )
```

```python
import functools
import math

import jax
import jax.numpy as jnp
from jax import lax
from jax.experimental import pallas as pl
from jax.experimental.pallas import tpu as pltpu
from jax.sharding import PartitionSpec as P

NEGATIVE = -1e30
SHARPNESS = 2.5
EXTRA = 16
F32, BF16 = jnp.float32, jnp.bfloat16
MIB = 1 << 20
LOG2E = math.log2(math.e)
LN2 = math.log(2.0)
BLOCK = 128
ROW_GROUPS = 8
LIMIT = 24
FULL = 63
AFTER = 2
HIDE = 20_000_000_000


def order_of(side):
    return list(range(1, side))


def iota(shape, axis):
    return lax.broadcasted_iota(jnp.int32, shape, axis)


def call(kernel, out_shape, scratch=(), smem=0, n_in=0, limit=LIMIT, flops=0, moved=0, exps=0, **kw):
    if not kw:
        kw = dict(
            in_specs=[pl.BlockSpec(memory_space=pltpu.SMEM)] * smem
            + [pl.BlockSpec(memory_space=pltpu.VMEM)] * (n_in - smem),
            out_specs=jax.tree.map(lambda _: pl.BlockSpec(memory_space=pltpu.VMEM), out_shape),
        )
    return pl.pallas_call(
        kernel,
        out_shape=out_shape,
        scratch_shapes=list(scratch),
        compiler_params=pltpu.CompilerParams(vmem_limit_bytes=limit * MIB),
        cost_estimate=pl.CostEstimate(flops=flops, bytes_accessed=moved, transcendentals=exps),
        **kw,
    )


def columns(rows, width):
    stacked = jnp.concatenate(rows + [jnp.zeros((128 - len(rows), width), F32)], axis=0)
    return stacked.T


def three(row):
    high = row.astype(BF16).astype(F32)
    middle = (row - high).astype(BF16).astype(F32)
    return [high, middle, row - high - middle]


def extra_rows(first, second, width):
    parts = three(first) + three(second)
    body = jnp.concatenate(parts + [jnp.zeros((EXTRA - len(parts), first.shape[1]), F32)], axis=0)
    rest = jnp.zeros((EXTRA, width - first.shape[1]), F32)
    return jnp.concatenate([body, rest], axis=1).astype(BF16)


def read_extra(ref, start, length):
    block = ref[start : start + EXTRA, :length].astype(F32)
    first = (block[0:1] + block[1:2]) + block[2:3]
    second = (block[3:4] + block[4:5]) + block[5:6]
    return first, second


def one_hot_slots(code, start, group, capacity):
    rows = code.shape[1]
    order = iota((capacity, rows), 0).astype(F32)
    return jnp.concatenate(
        [jnp.where(order == code[b : b + 1, :], 1.0, 0.0) for b in range(start, start + group)], axis=0
    )


def gather_body(
    info, flip, picks, home_ref, source, q_hbm, code_hbm, q_ref, code_ref, sem, *, n_tgt, per_device, capacity, group
):
    n_buckets, rows = code_ref.shape
    n_clusters = home_ref.shape[1]
    width = q_ref.shape[2]
    per_message = group // per_device
    cluster = iota((n_clusters, rows), 0).astype(F32)
    member = jnp.zeros((n_clusters, rows), F32)
    for pick in picks:
        member = jnp.where(cluster == pick, 1.0, member)
    bucket = iota((n_buckets, n_clusters), 0)
    earlier = jnp.where(iota((rows, rows), 0) < iota((rows, rows), 1), 1.0, 0.0).astype(BF16)

    def ranks(turn):
        holder = (info[0] + lax.bitwise_xor(lax.div(bucket, per_device), turn)) * n_tgt + info[1]
        place = holder * per_device + lax.rem(bucket, per_device)
        chosen = jnp.where(home_ref[...] == place, 1.0, 0.0).astype(BF16)
        inside = jnp.dot(chosen, member.astype(BF16), preferred_element_type=F32)
        rank = jnp.dot(inside.astype(BF16), earlier, preferred_element_type=F32)
        return jnp.where(inside > 0.5, rank, -1.0)

    code = ranks(0)
    code_ref[...] = code
    leave = [pltpu.make_async_copy(code_ref, code_hbm, sem.at[0])]
    leave[0].start()
    if flip is not None:
        code = ranks(flip)
    for start in range(0, n_buckets, group):
        slots = one_hot_slots(code, start, group, capacity)
        filled = jnp.sum(slots, axis=1, keepdims=True)
        found = jnp.dot(slots.astype(BF16), source, preferred_element_type=F32)
        head = found[:, :128]
        head = jnp.where((iota(head.shape, 1) == 0) & (filled < 0.5), jnp.inf, head)
        found = jnp.concatenate([head, found[:, 128:]], axis=1).astype(BF16)
        d = start // per_device
        at = pl.ds(d, per_message)
        q_ref[at] = found.reshape(per_message, per_device * capacity, width)
        if flip is None:
            leave.append(pltpu.make_async_copy(q_ref.at[at], q_hbm.at[at], sem.at[1 + start // group]))
            leave[-1].start()
        else:
            for k in range(d, d + per_message):
                leave.append(pltpu.make_async_copy(q_ref.at[k], q_hbm[k], sem.at[1 + k]))
                leave[-1].start()
    for copy in leave:
        copy.wait()


def half_with_picks(info, picks_ref, src_ref, out_ref):
    n_picks, rows = picks_ref.shape
    width = src_ref.shape[1]
    half = rows // 2
    out_ref[:half, :] = src_ref[pl.ds(pl.multiple_of(info[1] * half, 16), half), :]
    body = jnp.concatenate([picks_ref[...].astype(F32), jnp.zeros((EXTRA - n_picks, rows), F32)], axis=0)
    rest = jnp.zeros((EXTRA, width - rows), F32)
    out_ref[half:, :] = jnp.concatenate([body, rest], axis=1).astype(BF16)


def gather_own(info, picks_ref, home_ref, src_ref, *refs, **sizes):
    picks = [picks_ref[k : k + 1, :].astype(F32) for k in range(picks_ref.shape[0])]
    gather_body(info, None, picks, home_ref, src_ref[...], *refs, **sizes)


def gather_partner(info, home_ref, mine_ref, other_ref, *refs, n_picks, **sizes):
    *q_hbm, code_hbm, q_ref, code_ref, sem, src_ref = refs
    rows = src_ref.shape[0]
    half = rows // 2
    src_ref[pl.ds(pl.multiple_of(info[1] * half, 16), half), :] = mine_ref[:half, :]
    src_ref[pl.ds(pl.multiple_of((1 - info[1]) * half, 16), half), :] = other_ref[:half, :]
    block = mine_ref[half : half + EXTRA, :rows].astype(F32)
    picks = [block[k : k + 1, :] for k in range(n_picks)]
    gather_body(info, info[2], picks, home_ref, src_ref[...], q_hbm, code_hbm, q_ref, code_ref, sem, **sizes)


def scores_of(q, t, count):
    width = q.shape[1]
    n_cols = t.shape[0]
    head = q[:, :128].astype(F32)
    empty = head > 1e38
    q = jnp.concatenate([jnp.where(empty, 0.0, head).astype(BF16), q[:, 128:]], axis=1)
    s = lax.dot_general(q, t, (((1,), (1,)), ((), ())), preferred_element_type=F32)
    column_bias = jnp.where(iota((1, n_cols), 1) < count, 0.0, NEGATIVE).astype(F32)
    slot_bias = jnp.where(empty[:, 0:1], NEGATIVE, 0.0).astype(F32)
    return s * (SHARPNESS / math.sqrt(width) * LOG2E) + column_bias + slot_bias


def column_part(s_ref, highest, block):
    n_rows, n_cols = s_ref.shape
    total = jnp.zeros((8, n_cols), F32)
    for start in range(0, n_rows, block):
        part = jnp.exp2(s_ref[start : start + block, :] - highest)
        total = total + jnp.sum(part.reshape(block // 8, 8, n_cols), axis=0)
    return jnp.sum(total, axis=0, keepdims=True)


def row_log_sum(s):
    top = jnp.max(s, axis=1, keepdims=True)
    return top + jnp.log2(jnp.sum(jnp.exp2(s - top), axis=1, keepdims=True))


def weigh(s, half_reverse):
    shifted = s - half_reverse
    top = jnp.max(shifted, axis=1, keepdims=True)
    e = jnp.exp2(shifted - top)
    total = jnp.sum(e, axis=1, keepdims=True)
    return (e * (1.0 / total)).astype(BF16), top + jnp.log2(total)


def tail(margin, forward, lane):
    out = jnp.zeros(lane.shape, F32)
    for i, part in enumerate(three(margin) + three(forward)):
        out = jnp.where(lane == i, part, out)
    return out.astype(BF16)


def near_scores(count_ref, q_ref, t_ref, *refs, capacity, block):
    s_ref, col_ref, fwd_ref = refs[-3:]
    per_device, n_half, n_cols = s_ref.shape
    for l in range(per_device):
        q = q_ref[:, l * capacity : (l + 1) * capacity, :].reshape(n_half, -1)
        s = scores_of(q, t_ref[l], count_ref[l])
        s_ref[l] = s
        highest = jnp.max(s, axis=0, keepdims=True)
        total = column_part(s_ref.at[l], highest, block)
        col_ref[l] = jnp.concatenate([highest, total, jnp.zeros((6, n_cols), F32)], axis=0)

        def forward(i, _):
            at = pl.ds(pl.multiple_of(i * block, block), block)
            fwd_ref[l, at, :] = jnp.broadcast_to(row_log_sum(s_ref[l, at, :]), (block, 128))
            return 0

        lax.fori_loop(0, n_half // block, forward, 0)


def far_owner(info, count_ref, col_ref, t_hbm, *refs, block):
    *q_hbm, p_hbm, rev_hbm, q_ref, t_ref, s_ref, w_ref, p_ref, rev_ref, q_sem, t_sem, p_sem, rev_sem = refs
    per_device, n_msg, capacity, width = q_ref.shape
    _, n_half, n_cols = s_ref.shape
    places = [pl.ds(l * capacity, capacity) for l in range(per_device)]
    arrive, leave = [], []
    for l, at in enumerate(places):
        pieces = [pltpu.make_async_copy(q_hbm[k].at[at, :], q_ref.at[l, k], q_sem.at[l, k]) for k in range(n_msg)]
        arrive.append(pieces + [pltpu.make_async_copy(t_hbm.at[l], t_ref.at[l], t_sem.at[l])])
        to = [p_hbm.at[lax.bitwise_xor(info[2], k), at, :] for k in range(n_msg)]
        leave.append([pltpu.make_async_copy(p_ref.at[l, k], to[k], p_sem.at[l, k]) for k in range(n_msg)])
    for copy in sum(arrive, []):
        copy.start()
    rev_leave = pltpu.make_async_copy(rev_ref, rev_hbm, rev_sem)
    half_reverse = []
    for l in range(per_device):
        for copy in arrive[l]:
            copy.wait()
        s = scores_of(q_ref[l].reshape(n_half, width), t_ref[l], count_ref[l])
        s_ref[l] = s
        highest = jnp.max(s, axis=0, keepdims=True)
        total = column_part(s_ref.at[l], highest, block)
        top = jnp.maximum(highest, col_ref[l, 0:1, :])
        total = total * jnp.exp2(highest - top) + col_ref[l, 1:2, :] * jnp.exp2(col_ref[l, 0:1, :] - top)
        half_reverse.append(0.5 * (top + jnp.log2(total)))
        rev_ref[l] = jnp.broadcast_to(half_reverse[l], (8, n_cols))
    rev_leave.start()
    for l in range(per_device):
        for start in range(0, n_half, block):
            at = slice(start, start + block)
            s = s_ref[l, at, :]
            forward = row_log_sum(s)
            w, margin = weigh(s, half_reverse[l])
            w_ref[l, at, :] = w
            part = tail(margin, forward, iota((block, 128), 1))
            first = start // capacity
            p_ref[l, first : first + block // capacity, :, width:] = part.reshape(block // capacity, capacity, 128)
        p = jnp.dot(w_ref[l], t_ref[l], preferred_element_type=F32)
        p_ref[l, :, :, :width] = p.astype(BF16).reshape(n_msg, capacity, width)
        for copy in leave[l]:
            copy.start()
    for copy in sum(leave, [rev_leave]):
        copy.wait()


def near_owner(s_ref, rev_ref, fwd_ref, t_ref, p_ref, w_ref, tail_ref, *, capacity, block):
    n_msg, _, full = p_ref.shape
    per_device, n_half, _ = s_ref.shape
    width = full - 128
    for l in range(per_device):
        half_reverse = rev_ref[l, 0:1, :]

        def rows(i, _):
            at = pl.ds(pl.multiple_of(i * block, block), block)
            w, margin = weigh(s_ref[l, at, :], half_reverse)
            w_ref[at, :] = w
            tail_ref[at, :] = tail(margin, fwd_ref[l, at, 0:1], iota((block, 128), 1))
            return 0

        lax.fori_loop(0, n_half // block, rows, 0)
        at = slice(l * capacity, (l + 1) * capacity)
        p = jnp.dot(w_ref[...], t_ref[l], preferred_element_type=F32)
        p_ref[:, at, :width] = p.astype(BF16).reshape(n_msg, capacity, width)
        p_ref[:, at, width:] = tail_ref[...].reshape(n_msg, capacity, 128)


def combine_kernel(info, code_ref, r_ref, _, keep_ref, kmf_ref, *refs, capacity):
    *send_refs, scr = refs
    n_buckets, rows = code_ref.shape
    n_slots = n_buckets * capacity
    width = r_ref.shape[2] - 128
    half = rows // 2
    parts = r_ref[:, :, width:].reshape(n_slots, 128).astype(F32)
    margin = (parts[:, 0:1] + parts[:, 1:2]) + parts[:, 2:3]
    forward = (parts[:, 3:4] + parts[:, 4:5]) + parts[:, 5:6]
    slots = one_hot_slots(code_ref[...], 0, n_buckets, capacity) > 0.5

    def merged(column):
        top = jnp.max(jnp.where(slots, column, NEGATIVE), axis=0, keepdims=True)
        total = jnp.sum(jnp.where(slots, jnp.exp2(column - top), 0.0), axis=0, keepdims=True)
        return jnp.where(total > 0.0, top + jnp.log2(jnp.where(total > 0.0, total, 1.0)), NEGATIVE)

    margin_row, forward_row = merged(margin), merged(forward)
    factor = jnp.where(slots, jnp.exp2(margin - margin_row), 0.0)
    high = factor.astype(BF16)
    low = (factor - high.astype(F32)).astype(BF16)
    r = r_ref[:, :, :width].reshape(n_slots, width)
    over = (((0,), (0,)), ((), ()))
    pooled = lax.dot_general(high, r, over, preferred_element_type=F32)
    scr[...] = pooled + lax.dot_general(low, r, over, preferred_element_type=F32)
    keep_ref[...] = scr[pl.ds(pl.multiple_of(info[1] * half, 16), half), :]
    start = 0
    for ref in send_refs:
        count = min(ref.shape[0], half - start)
        at = pl.ds(pl.multiple_of((1 - info[1]) * half + start, 16), count)
        ref[:count, :] = scr[at, :].astype(BF16)
        start = start + count
    send_refs[-1][count:, :] = extra_rows(margin_row, forward_row, width)
    kmf_ref[...] = jnp.concatenate([margin_row, forward_row, jnp.zeros((6, rows), F32)], axis=0)


def log_sum(first, second, third=None):
    top = jnp.maximum(first, second)
    if third is not None:
        top = jnp.maximum(top, third)
    total = jnp.exp2(first - top) + jnp.exp2(second - top)
    if third is not None:
        total = total + jnp.exp2(third - top)
    return top + jnp.log2(total)


def merge_pair(info, keep_ref, kmf_ref, got_ref, out_ref, scr):
    half, width = keep_ref.shape
    rows = kmf_ref.shape[1]
    margin, forward = kmf_ref[0:1, :], kmf_ref[1:2, :]
    margin_b, forward_b = read_extra(got_ref, half, rows)
    margin_all, forward_all = log_sum(margin, margin_b), log_sum(forward, forward_b)
    scr[...] = columns([jnp.exp2(margin - margin_all), jnp.exp2(margin_b - margin_all)], rows)
    factors = scr[pl.ds(pl.multiple_of(info[1] * half, 16), half), :]
    out = keep_ref[...] * factors[:, 0:1] + got_ref[:half, :].astype(F32) * factors[:, 1:2]
    out_ref[:half, :] = out.astype(BF16)
    out_ref[half:, :] = extra_rows(margin_all, forward_all, width)


def merge_last(info, keep_ref, kmf_ref, got_ref, last_ref, far_ref, out_ref, conf_ref, scr):
    half, width = keep_ref.shape
    rows = kmf_ref.shape[1]
    margin, forward = kmf_ref[0:1, :], kmf_ref[1:2, :]
    first = got_ref.shape[0]
    margin_b, forward_b = read_extra(last_ref, half - first, rows)
    margin_c, forward_c = read_extra(far_ref, half, rows)
    margin_all = log_sum(margin, margin_b, margin_c)
    forward_all = log_sum(forward, forward_b, forward_c)
    scr[...] = columns(
        [jnp.exp2(margin - margin_all), jnp.exp2(margin_b - margin_all), jnp.exp2(margin_c - margin_all)], rows
    )
    factors = scr[pl.ds(pl.multiple_of(info[1] * half, 16), half), :]
    for at, ref in ((slice(0, first), got_ref), (slice(first, half), last_ref)):
        out = keep_ref[at, :] * factors[at, 0:1] + ref[: at.stop - at.start, :].astype(F32) * factors[at, 1:2]
        out_ref[at, :] = (out + far_ref[at, :].astype(F32) * factors[at, 2:3]).astype(BF16)
    conf_ref[...] = (margin_all - 0.5 * forward_all) * LN2


def shards(sources, targets, picks, cluster_home, row_count):
    n_src, n_tgt = lax.axis_size("src"), lax.axis_size("tgt")
    rows, width = sources.shape
    per_device, n_cols, _ = targets.shape
    n_clusters = cluster_home.shape[0]
    n_picks = picks.shape[1]
    capacity = -(-(2 * n_picks * rows // n_clusters) // 16) * 16
    side = n_src // 2
    half = rows // 2
    message = per_device * capacity
    n_buckets = side * per_device
    n_slots = n_buckets * capacity
    group = max(g for g in range(per_device, n_buckets + 1, per_device) if n_buckets % g == 0 and g * capacity <= 400)
    sds = jax.ShapeDtypeStruct

    me, core = lax.axis_index("src"), lax.axis_index("tgt")
    info = jnp.stack([me // side * side, core, me % side]).astype(jnp.int32)
    partner = [(i, (i + side) % n_src) for i in range(n_src)]
    twin = [(i, 1 - i) for i in range(n_tgt)]
    halves = [list(range(side)), list(range(side, n_src))]

    def exchange(x):
        return lax.all_to_all(x, "src", split_axis=0, concat_axis=0, axis_index_groups=halves, tiled=True)

    picks_t = picks.T
    home = cluster_home[None, :]
    letter = sds((half + EXTRA, width), BF16)
    far_mine = lax.ppermute(
        call(half_with_picks, letter, smem=1, n_in=3, moved=4 * half * width, limit=FULL)(info, picks_t, sources), "src", partner
    )
    far_other = lax.ppermute(far_mine, "tgt", twin)

    sizes = dict(n_tgt=n_tgt, per_device=per_device, capacity=capacity, group=group)
    gather_out = (sds((side, message, width), BF16), sds((n_buckets, rows), F32))
    moved = 2 * (n_slots + rows) * width
    hbm = pl.BlockSpec(memory_space=pltpu.HBM)
    vmem = pl.BlockSpec(memory_space=pltpu.VMEM)
    smem = pl.BlockSpec(memory_space=pltpu.SMEM)
    gather_scratch = [
        pltpu.VMEM((side, message, width), BF16),
        pltpu.VMEM((n_buckets, rows), F32),
        pltpu.SemaphoreType.DMA((1 + side,)),
    ]
    near_q, near_code = call(
        functools.partial(gather_own, **sizes),
        gather_out,
        gather_scratch,
        flops=2 * n_slots * rows * width,
        moved=moved,
        limit=FULL,
        in_specs=[smem] + [vmem] * 3,
        out_specs=(hbm, hbm),
    )(info, picks_t, home, sources)
    near_in = exchange(near_q)
    *far_q, far_code = call(
        functools.partial(gather_partner, n_picks=n_picks, **sizes),
        tuple([sds((message, width), BF16)] * side) + gather_out[1:],
        gather_scratch + [pltpu.VMEM((rows, width), BF16)],
        flops=HIDE,
        moved=moved,
        limit=FULL,
        in_specs=[smem] + [vmem] * 3,
        out_specs=tuple([hbm] * (side + 1)),
    )(info, home, far_mine, far_other)
    far_in = far_q[:1] + [
        lax.ppermute(far_q[k], "src", [(i, i ^ k) for i in range(n_src)]) for k in order_of(side)
    ]
    after = far_in[1 : 1 + AFTER]
    far_in = far_in[:1] + [far_in[1 + order_of(side).index(k)] for k in range(1, side)]

    here = (me * n_tgt + core) * per_device + jnp.arange(per_device, dtype=jnp.int32)
    counts = jnp.sum(jnp.where(home == here[:, None], row_count[None, :], 0), axis=1)
    n_half = side * capacity
    options = dict(capacity=capacity, block=BLOCK)
    work = dict(flops=2 * n_slots * n_cols * width, moved=2 * (n_slots + per_device * n_cols) * width)
    pooled = sds((side, message, width + 128), BF16)
    near_s, near_col, near_fwd = call(
        functools.partial(near_scores, **options),
        (
            sds((per_device, n_half, n_cols), F32),
            sds((per_device, 8, n_cols), F32),
            sds((per_device, n_half, 128), F32),
        ),
        limit=FULL,
        exps=2 * n_slots * n_cols,
        in_specs=[smem, vmem, vmem] + [pl.BlockSpec(memory_space=pl.ANY)] * len(after),
        out_specs=(vmem, vmem, vmem),
        **work,
    )(counts, near_in, targets, *after)
    weights = [pltpu.VMEM((n_half, n_cols), BF16), pltpu.VMEM((n_half, 128), BF16)]
    far_pool, reverse = call(
        functools.partial(far_owner, block=capacity * math.gcd(side, ROW_GROUPS)),
        (pooled, sds((per_device, 8, n_cols), F32)),
        [
            pltpu.VMEM((per_device, side, capacity, width), BF16),
            pltpu.VMEM((per_device, n_cols, width), BF16),
            pltpu.VMEM((per_device, n_half, n_cols), F32),
            pltpu.VMEM((per_device, n_half, n_cols), BF16),
            pltpu.VMEM((per_device, side, capacity, width + 128), BF16),
            pltpu.VMEM((per_device, 8, n_cols), F32),
            pltpu.SemaphoreType.DMA((per_device, side)),
            pltpu.SemaphoreType.DMA((per_device,)),
            pltpu.SemaphoreType.DMA((per_device, side)),
            pltpu.SemaphoreType.DMA,
        ],
        limit=FULL,
        exps=3 * n_slots * n_cols,
        in_specs=[smem, smem, vmem] + [hbm] * (1 + side),
        out_specs=(hbm, hbm),
        **work,
    )(info, counts, near_col, targets, *far_in)
    back_far = exchange(far_pool)
    near_pool = call(
        functools.partial(near_owner, **options), pooled, weights, n_in=4, exps=n_slots * n_cols, **work
    )(near_s, reverse, near_fwd, targets)
    back_near = exchange(near_pool)

    def combine(code, back, after, pieces, weight):
        return pl.pallas_call(
            functools.partial(combine_kernel, capacity=capacity),
            out_shape=(sds((half, width), F32), sds((8, rows), F32)) + tuple(sds((n, width), BF16) for n in pieces),
            in_specs=[
                pl.BlockSpec(memory_space=pltpu.SMEM),
                pl.BlockSpec(memory_space=pltpu.VMEM),
                pl.BlockSpec(memory_space=pltpu.VMEM),
                pl.BlockSpec(memory_space=pl.ANY),
            ],
            out_specs=tuple([pl.BlockSpec(memory_space=pltpu.VMEM)] * (2 + len(pieces))),
            scratch_shapes=[pltpu.VMEM((rows, width), F32)],
            compiler_params=pltpu.CompilerParams(vmem_limit_bytes=LIMIT * MIB),
            cost_estimate=pl.CostEstimate(
                flops=weight * 4 * n_slots * rows * width,
                bytes_accessed=weight * 2 * (n_slots + 2 * rows) * width,
                transcendentals=0,
            ),
        )(info, code, back, after)

    keep, kmf, send = combine(far_code, back_far, info, [half + EXTRA], 1)
    got = lax.ppermute(send, "tgt", twin)
    factors = [pltpu.VMEM((rows, 128), F32)]
    joined = call(merge_pair, letter, factors, smem=1, n_in=4, moved=10 * half * width)(info, keep, kmf, got)
    from_far = lax.ppermute(joined, "src", partner)

    first = half // 32 * 16
    keep, kmf, *send = combine(near_code, back_near, joined, [first, half - first + EXTRA], 0)
    got = [lax.ppermute(piece, "tgt", twin) for piece in send]
    mine, confidence = call(
        merge_last,
        (sds((half, width), BF16), sds((1, rows), F32)),
        factors,
        smem=1,
        n_in=6,
        moved=10 * half * width,
    )(info, keep, kmf, *got, from_far)
    other = lax.ppermute(mine, "tgt", twin)
    first = jnp.where(core == 0, mine, other)
    second = jnp.where(core == 0, other, mine)
    return (jnp.concatenate([first, second], axis=0), confidence[0].astype(BF16))


def solution(mesh):
    placed = (P("src", None), P(("src", "tgt"), None, None), P("src", None), P(), P())
    return jax.shard_map(
        shards, mesh=mesh, in_specs=placed, out_specs=(P("src", None), P("src")), check_vma=False
    )
```

```python
import functools
import math

import jax
import jax.numpy as jnp
from jax import lax
from jax.experimental import pallas as pl
from jax.experimental.pallas import tpu as pltpu
from jax.sharding import PartitionSpec as P

NEGATIVE = -1e30
SHARPNESS = 2.5
EXTRA = 16
F32, BF16 = jnp.float32, jnp.bfloat16
MIB = 1 << 20
LOG2E = math.log2(math.e)
LN2 = math.log(2.0)
BLOCK = 128
ROW_GROUPS = 8
LIMIT = 24
FULL = 63
HIDE = 20_000_000_000


def iota(shape, axis):
    return lax.broadcasted_iota(jnp.int32, shape, axis)


def place_of(side):
    me = lax.axis_index("src")
    return me // side * side, lax.axis_index("tgt"), lax.rem(me, side)


def call(kernel, out_shape, scratch=(), smem=0, n_in=0, limit=LIMIT, flops=0, moved=0, exps=0, **kw):
    if not kw:
        kw = dict(
            in_specs=[pl.BlockSpec(memory_space=pltpu.SMEM)] * smem
            + [pl.BlockSpec(memory_space=pltpu.VMEM)] * (n_in - smem),
            out_specs=jax.tree.map(lambda _: pl.BlockSpec(memory_space=pltpu.VMEM), out_shape),
        )
    return pl.pallas_call(
        kernel,
        out_shape=out_shape,
        scratch_shapes=list(scratch),
        compiler_params=pltpu.CompilerParams(vmem_limit_bytes=limit * MIB),
        cost_estimate=pl.CostEstimate(flops=flops, bytes_accessed=moved, transcendentals=exps),
        **kw,
    )


def columns(rows, width):
    stacked = jnp.concatenate(rows + [jnp.zeros((128 - len(rows), width), F32)], axis=0)
    return stacked.T


def three(row):
    high = row.astype(BF16).astype(F32)
    middle = (row - high).astype(BF16).astype(F32)
    return [high, middle, row - high - middle]


def extra_rows(first, second, width):
    parts = three(first) + three(second)
    body = jnp.concatenate(parts + [jnp.zeros((EXTRA - len(parts), first.shape[1]), F32)], axis=0)
    rest = jnp.zeros((EXTRA, width - first.shape[1]), F32)
    return jnp.concatenate([body, rest], axis=1).astype(BF16)


def read_extra(ref, start, length):
    block = ref[start : start + EXTRA, :length].astype(F32)
    first = (block[0:1] + block[1:2]) + block[2:3]
    second = (block[3:4] + block[4:5]) + block[5:6]
    return first, second


def one_hot_slots(code, start, group, capacity):
    rows = code.shape[1]
    order = iota((capacity, rows), 0).astype(F32)
    return jnp.concatenate(
        [jnp.where(order == code[b : b + 1, :], 1.0, 0.0) for b in range(start, start + group)], axis=0
    )


def gather_body(
    info, flip, picks, home_ref, load, q_hbm, code_hbm, q_ref, code_ref, sem, *, n_tgt, per_device, capacity, group
):
    n_buckets, rows = code_ref.shape
    n_clusters = home_ref.shape[1]
    width = q_ref.shape[2]
    per_message = group // per_device
    cluster = iota((n_clusters, rows), 0).astype(F32)
    member = jnp.zeros((n_clusters, rows), F32)
    for pick in picks:
        member = jnp.where(cluster == pick, 1.0, member)
    bucket = iota((n_buckets, n_clusters), 0)
    earlier = jnp.where(iota((rows, rows), 0) < iota((rows, rows), 1), 1.0, 0.0).astype(BF16)

    def ranks(turn):
        holder = (info[0] + lax.bitwise_xor(lax.div(bucket, per_device), turn)) * n_tgt + info[1]
        place = holder * per_device + lax.rem(bucket, per_device)
        chosen = jnp.where(home_ref[...] == place, 1.0, 0.0).astype(BF16)
        inside = jnp.dot(chosen, member.astype(BF16), preferred_element_type=F32)
        rank = jnp.dot(inside.astype(BF16), earlier, preferred_element_type=F32)
        return jnp.where(inside > 0.5, rank, -1.0)

    code = ranks(0)
    code_ref[...] = code
    leave = [pltpu.make_async_copy(code_ref, code_hbm, sem.at[0])]
    leave[0].start()
    if flip is not None:
        code = ranks(flip)
    source = load()
    for start in range(0, n_buckets, group):
        slots = one_hot_slots(code, start, group, capacity)
        filled = jnp.sum(slots, axis=1, keepdims=True)
        found = jnp.dot(slots.astype(BF16), source, preferred_element_type=F32)
        head = found[:, :128]
        head = jnp.where((iota(head.shape, 1) == 0) & (filled < 0.5), jnp.inf, head)
        found = jnp.concatenate([head, found[:, 128:]], axis=1).astype(BF16)
        d = start // per_device
        at = pl.ds(d, per_message)
        q_ref[at] = found.reshape(per_message, per_device * capacity, width)
        if flip is None:
            leave.append(pltpu.make_async_copy(q_ref.at[at], q_hbm.at[at], sem.at[1 + start // group]))
            leave[-1].start()
        else:
            for k in range(d, d + per_message):
                leave.append(pltpu.make_async_copy(q_ref.at[k], q_hbm[k], sem.at[1 + k]))
                leave[-1].start()
    for copy in leave:
        copy.wait()


def half_with_picks(picks_hbm, src_hbm, out_ref, picks_ref, sems, *, side):
    _, core, _ = place_of(side)
    n_picks, rows = picks_ref.shape
    width = src_hbm.shape[1]
    half = rows // 2
    mine = pl.ds(pl.multiple_of(core * half, 16), half)
    names = pltpu.make_async_copy(picks_hbm, picks_ref, sems.at[0])
    names.start()
    body = pltpu.make_async_copy(src_hbm.at[mine, :], out_ref.at[pl.ds(0, half), :], sems.at[1])
    body.start()
    names.wait()
    names = jnp.concatenate([picks_ref[...].astype(F32), jnp.zeros((EXTRA - n_picks, rows), F32)], axis=0)
    rest = jnp.zeros((EXTRA, width - rows), F32)
    out_ref[half:, :] = jnp.concatenate([names, rest], axis=1).astype(BF16)
    body.wait()


def gather_own(picks_hbm, home_hbm, src_hbm, *refs, side, **sizes):
    *refs, picks_ref, home_ref, src_ref, sems = refs
    copies = []
    for i, (here, there) in enumerate(((picks_hbm, picks_ref), (home_hbm, home_ref), (src_hbm, src_ref))):
        copies.append(pltpu.make_async_copy(here, there, sems.at[i]))
        copies[-1].start()
    copies[0].wait()
    copies[1].wait()
    picks = [picks_ref[k : k + 1, :].astype(F32) for k in range(picks_ref.shape[0])]

    def load():
        copies[2].wait()
        return src_ref[...]

    gather_body(place_of(side), None, picks, home_ref, load, *refs, **sizes)


def gather_partner(home_ref, mine_ref, other_ref, *refs, n_picks, side, **sizes):
    info = place_of(side)
    *q_hbm, code_hbm, q_ref, code_ref, sem, src_ref = refs
    rows = src_ref.shape[0]
    half = rows // 2
    src_ref[pl.ds(pl.multiple_of(info[1] * half, 16), half), :] = mine_ref[:half, :]
    src_ref[pl.ds(pl.multiple_of((1 - info[1]) * half, 16), half), :] = other_ref[:half, :]
    block = mine_ref[half : half + EXTRA, :rows].astype(F32)
    picks = [block[k : k + 1, :] for k in range(n_picks)]
    load = lambda: src_ref[...]
    gather_body(info, info[2], picks, home_ref, load, q_hbm, code_hbm, q_ref, code_ref, sem, **sizes)


def scores_of(q, t, count):
    width = q.shape[1]
    n_cols = t.shape[0]
    head = q[:, :128].astype(F32)
    empty = head > 1e38
    q = jnp.concatenate([jnp.where(empty, 0.0, head).astype(BF16), q[:, 128:]], axis=1)
    s = lax.dot_general(q, t, (((1,), (1,)), ((), ())), preferred_element_type=F32)
    column_bias = jnp.where(iota((1, n_cols), 1) < count, 0.0, NEGATIVE).astype(F32)
    slot_bias = jnp.where(empty[:, 0:1], NEGATIVE, 0.0).astype(F32)
    return s * (SHARPNESS / math.sqrt(width) * LOG2E) + column_bias + slot_bias


def column_part(s_ref, highest, block):
    n_rows, n_cols = s_ref.shape
    total = jnp.zeros((8, n_cols), F32)
    for start in range(0, n_rows, block):
        part = jnp.exp2(s_ref[start : start + block, :] - highest)
        total = total + jnp.sum(part.reshape(block // 8, 8, n_cols), axis=0)
    return jnp.sum(total, axis=0, keepdims=True)


def row_log_sum(s):
    top = jnp.max(s, axis=1, keepdims=True)
    return top + jnp.log2(jnp.sum(jnp.exp2(s - top), axis=1, keepdims=True))


def weigh(s, half_reverse):
    shifted = s - half_reverse
    top = jnp.max(shifted, axis=1, keepdims=True)
    e = jnp.exp2(shifted - top)
    total = jnp.sum(e, axis=1, keepdims=True)
    return (e * (1.0 / total)).astype(BF16), top + jnp.log2(total)


def put_pool(p_ref, l, p, capacity):
    strips, cols = capacity // 16, p.shape[1] // 128
    for k in range(p_ref.shape[0]):
        for r in range(strips):
            strip = p[k * capacity + 16 * r : k * capacity + 16 * (r + 1)]
            for c in range(cols):
                p_ref[k, (l * strips + r) * cols + c] = strip[:, 128 * c : 128 * (c + 1)]


def put_tail(tail_ref, l, first, margin, forward, capacity):
    strips = capacity // 16
    shape = (margin.shape[0], 128)
    parts = three(jnp.broadcast_to(margin, shape)) + three(jnp.broadcast_to(forward, shape))
    turn = lax.rem(iota(shape, 1), 6)
    mixed = parts[5]
    for i in range(5):
        mixed = jnp.where(turn == i, parts[i], mixed)
    strip_of = lax.div(iota((16, 128), 1), 6)
    for k in range(margin.shape[0] // capacity):
        tile = tail_ref[first + k] if l else jnp.zeros((16, 128), F32)
        for r in range(strips):
            at = slice(k * capacity + 16 * r, k * capacity + 16 * (r + 1))
            tile = jnp.where(strip_of == l * strips + r, mixed[at], tile)
        tail_ref[first + k] = tile


def near_scores(count_ref, q_ref, t_ref, s_ref, col_ref, fwd_ref, *, capacity, block):
    per_device, n_half, n_cols = s_ref.shape
    for l in range(per_device):
        q = q_ref[:, l * capacity : (l + 1) * capacity, :].reshape(n_half, -1)
        s = scores_of(q, t_ref[l], count_ref[l])
        s_ref[l] = s
        highest = jnp.max(s, axis=0, keepdims=True)
        total = column_part(s_ref.at[l], highest, block)
        col_ref[l] = jnp.concatenate([highest, total, jnp.zeros((6, n_cols), F32)], axis=0)

        def forward(i, _):
            at = pl.ds(pl.multiple_of(i * block, block), block)
            fwd_ref[l, at, :] = jnp.broadcast_to(row_log_sum(s_ref[l, at, :]), (block, 128))
            return 0

        lax.fori_loop(0, n_half // block, forward, 0)


def far_owner(count_ref, col_ref, t_ref, *refs, block, side):
    _, _, here = place_of(side)
    *q_hbm, p_hbm, rev_hbm, q_ref, s_ref, w_ref, p_ref, tail_ref, rev_ref, q_sem, p_sem, rev_sem = refs
    per_device, n_msg, capacity, width = q_ref.shape
    _, n_half, n_cols = s_ref.shape
    tiles = capacity * width // 2048
    arrive, leave = [], []
    for l in range(per_device):
        at = pl.ds(l * capacity, capacity)
        arrive.append([pltpu.make_async_copy(q_hbm[k].at[at, :], q_ref.at[l, k], q_sem.at[l, k]) for k in range(n_msg)])
        at = pl.ds(l * tiles, tiles + l // (per_device - 1))
        to = [p_hbm.at[lax.bitwise_xor(here, k), at] for k in range(n_msg)]
        leave.append([pltpu.make_async_copy(p_ref.at[k, at], to[k], p_sem.at[l, k]) for k in range(n_msg)])
    for copy in arrive[0]:
        copy.start()
    rev_leave = pltpu.make_async_copy(rev_ref, rev_hbm, rev_sem)
    half_reverse = []
    for l in range(per_device):
        for copy in arrive[l]:
            copy.wait()
        for copy in arrive[l + 1] if l + 1 < per_device else []:
            copy.start()
        s = scores_of(q_ref[l].reshape(n_half, width), t_ref[l], count_ref[l])
        s_ref[l] = s
        highest = jnp.max(s, axis=0, keepdims=True)
        total = column_part(s_ref.at[l], highest, block)
        top = jnp.maximum(highest, col_ref[l, 0:1, :])
        total = total * jnp.exp2(highest - top) + col_ref[l, 1:2, :] * jnp.exp2(col_ref[l, 0:1, :] - top)
        half_reverse.append(0.5 * (top + jnp.log2(total)))
        rev_ref[l] = jnp.broadcast_to(half_reverse[l], (8, n_cols))
    rev_leave.start()
    for l in range(per_device):
        for start in range(0, n_half, block):
            at = slice(start, start + block)
            s = s_ref[l, at, :]
            forward = row_log_sum(s)
            w, margin = weigh(s, half_reverse[l])
            w_ref[l, at, :] = w
            put_tail(tail_ref, l, start // capacity, margin, forward, capacity)
        p = jnp.dot(w_ref[l], t_ref[l], preferred_element_type=F32).astype(BF16)
        put_pool(p_ref, l, p, capacity)
        if l == per_device - 1:
            p_ref[:, per_device * tiles] = tail_ref[...].astype(BF16)
        for copy in leave[l]:
            copy.start()
    for copy in sum(leave, [rev_leave]):
        copy.wait()


def near_owner(s_ref, rev_ref, fwd_ref, t_ref, p_ref, w_ref, tail_ref, *, capacity, block):
    per_device, n_half, _ = s_ref.shape
    for l in range(per_device):
        half_reverse = rev_ref[l, 0:1, :]
        for start in range(0, n_half, block):
            at = slice(start, start + block)
            w, margin = weigh(s_ref[l, at, :], half_reverse)
            w_ref[at, :] = w
            put_tail(tail_ref, l, start // capacity, margin, fwd_ref[l, at, 0:1], capacity)
        p = jnp.dot(w_ref[...], t_ref[l], preferred_element_type=F32).astype(BF16)
        put_pool(p_ref, l, p, capacity)
    p_ref[:, p_ref.shape[1] - 1] = tail_ref[...].astype(BF16)


def combine_kernel(code_ref, r_ref, _, keep_ref, kmf_ref, *refs, capacity, side):
    _, core, _ = place_of(side)
    *send_refs, r_scr, scr = refs
    n_buckets, rows = code_ref.shape
    width = scr.shape[1]
    half = rows // 2
    n_msg, n_tiles, _, _ = r_ref.shape
    cols = width // 128
    strips = n_tiles // cols
    margin, forward = [], []
    for j in range(n_msg):
        last = r_ref[j, n_tiles - 1].astype(F32)
        last = (last + pltpu.roll(last, 127, 1)) + pltpu.roll(last, 126, 1)
        for r in range(strips):
            margin.append(jnp.broadcast_to(last[:, 6 * r : 6 * r + 1], (16, 128)))
            forward.append(jnp.broadcast_to(last[:, 6 * r + 3 : 6 * r + 4], (16, 128)))
            at = slice((j * strips + r) * 16, (j * strips + r + 1) * 16)
            for c in range(cols):
                r_scr[at, 128 * c : 128 * (c + 1)] = r_ref[j, r * cols + c]
    margin = jnp.concatenate([jnp.concatenate(margin, axis=0)] * (rows // 128), axis=1)
    forward = jnp.concatenate([jnp.concatenate(forward, axis=0)] * (rows // 128), axis=1)
    slots = one_hot_slots(code_ref[...], 0, n_buckets, capacity) > 0.5

    def merged(column):
        top = jnp.max(jnp.where(slots, column, NEGATIVE), axis=0, keepdims=True)
        total = jnp.sum(jnp.where(slots, jnp.exp2(column - top), 0.0), axis=0, keepdims=True)
        return jnp.where(total > 0.0, top + jnp.log2(jnp.where(total > 0.0, total, 1.0)), NEGATIVE)

    margin_row, forward_row = merged(margin), merged(forward)
    factor = jnp.where(slots, jnp.exp2(margin - margin_row), 0.0)
    high = factor.astype(BF16)
    low = (factor - high.astype(F32)).astype(BF16)
    r = r_scr[...]
    over = (((0,), (0,)), ((), ()))
    pooled = lax.dot_general(high, r, over, preferred_element_type=F32)
    scr[...] = pooled + lax.dot_general(low, r, over, preferred_element_type=F32)
    keep_ref[...] = scr[pl.ds(pl.multiple_of(core * half, 16), half), :]
    start = 0
    for ref in send_refs:
        count = min(ref.shape[0], half - start)
        at = pl.ds(pl.multiple_of((1 - core) * half + start, 16), count)
        ref[:count, :] = scr[at, :].astype(BF16)
        start = start + count
    send_refs[-1][count:, :] = extra_rows(margin_row, forward_row, width)
    kmf_ref[...] = jnp.concatenate([margin_row, forward_row, jnp.zeros((6, rows), F32)], axis=0)


def log_sum(first, second, third=None):
    top = jnp.maximum(first, second)
    if third is not None:
        top = jnp.maximum(top, third)
    total = jnp.exp2(first - top) + jnp.exp2(second - top)
    if third is not None:
        total = total + jnp.exp2(third - top)
    return top + jnp.log2(total)


def merge_pair(keep_ref, kmf_ref, got_ref, out_ref, scr, *, side):
    _, core, _ = place_of(side)
    half, width = keep_ref.shape
    rows = kmf_ref.shape[1]
    margin, forward = kmf_ref[0:1, :], kmf_ref[1:2, :]
    margin_b, forward_b = read_extra(got_ref, half, rows)
    margin_all, forward_all = log_sum(margin, margin_b), log_sum(forward, forward_b)
    scr[...] = columns([jnp.exp2(margin - margin_all), jnp.exp2(margin_b - margin_all)], rows)
    factors = scr[pl.ds(pl.multiple_of(core * half, 16), half), :]
    out = keep_ref[...] * factors[:, 0:1] + got_ref[:half, :].astype(F32) * factors[:, 1:2]
    out_ref[:half, :] = out.astype(BF16)
    out_ref[half:, :] = extra_rows(margin_all, forward_all, width)


def merge_last(keep_ref, kmf_ref, got_ref, last_ref, far_ref, out_ref, conf_ref, scr, *, side):
    _, core, _ = place_of(side)
    half, width = keep_ref.shape
    rows = kmf_ref.shape[1]
    margin, forward = kmf_ref[0:1, :], kmf_ref[1:2, :]
    first = got_ref.shape[0]
    margin_b, forward_b = read_extra(last_ref, half - first, rows)
    margin_c, forward_c = read_extra(far_ref, half, rows)
    margin_all = log_sum(margin, margin_b, margin_c)
    forward_all = log_sum(forward, forward_b, forward_c)
    scr[...] = columns(
        [jnp.exp2(margin - margin_all), jnp.exp2(margin_b - margin_all), jnp.exp2(margin_c - margin_all)], rows
    )
    factors = scr[pl.ds(pl.multiple_of(core * half, 16), half), :]
    for at, ref in ((slice(0, first), got_ref), (slice(first, half), last_ref)):
        out = keep_ref[at, :] * factors[at, 0:1] + ref[: at.stop - at.start, :].astype(F32) * factors[at, 1:2]
        out_ref[at, :] = (out + far_ref[at, :].astype(F32) * factors[at, 2:3]).astype(BF16)
    conf_ref[...] = (margin_all - 0.5 * forward_all) * LN2


def shards(sources, targets, picks, cluster_home, row_count):
    n_src, n_tgt = lax.axis_size("src"), lax.axis_size("tgt")
    rows, width = sources.shape
    per_device, n_cols, _ = targets.shape
    n_clusters = cluster_home.shape[0]
    n_picks = picks.shape[1]
    capacity = -(-(2 * n_picks * rows // n_clusters) // 16) * 16
    side = n_src // 2
    half = rows // 2
    message = per_device * capacity
    n_buckets = side * per_device
    n_slots = n_buckets * capacity
    group = max(g for g in range(per_device, n_buckets + 1, per_device) if n_buckets % g == 0 and g * capacity <= 400)
    sds = jax.ShapeDtypeStruct

    me, core = lax.axis_index("src"), lax.axis_index("tgt")
    partner = [(i, (i + side) % n_src) for i in range(n_src)]
    twin = [(i, 1 - i) for i in range(n_tgt)]
    halves = [list(range(side)), list(range(side, n_src))]

    def exchange(x):
        return lax.all_to_all(x, "src", split_axis=0, concat_axis=0, axis_index_groups=halves, tiled=True)

    picks_t = picks.T
    home = cluster_home[None, :]
    letter = sds((half + EXTRA, width), BF16)
    hbm = pl.BlockSpec(memory_space=pltpu.HBM)
    vmem = pl.BlockSpec(memory_space=pltpu.VMEM)
    smem = pl.BlockSpec(memory_space=pltpu.SMEM)
    unread = pl.BlockSpec(memory_space=pl.ANY)
    mine = call(
        functools.partial(half_with_picks, side=side),
        letter,
        [pltpu.VMEM((n_picks, rows), jnp.int32), pltpu.SemaphoreType.DMA((2,))],
        moved=4 * half * width,
        limit=FULL,
        in_specs=[hbm, hbm],
        out_specs=vmem,
    )(picks_t, sources)
    far_mine = lax.ppermute(mine, "src", partner)
    far_other = lax.ppermute(far_mine, "tgt", twin)

    sizes = dict(side=side, n_tgt=n_tgt, per_device=per_device, capacity=capacity, group=group)
    gather_out = (sds((side, message, width), BF16), sds((n_buckets, rows), F32))
    moved = 2 * (n_slots + rows) * width
    gather_scratch = [
        pltpu.VMEM((side, message, width), BF16),
        pltpu.VMEM((n_buckets, rows), F32),
        pltpu.SemaphoreType.DMA((1 + side,)),
    ]
    near_q, near_code = call(
        functools.partial(gather_own, **sizes),
        gather_out,
        gather_scratch
        + [
            pltpu.VMEM((n_picks, rows), jnp.int32),
            pltpu.VMEM((1, n_clusters), jnp.int32),
            pltpu.VMEM((rows, width), BF16),
            pltpu.SemaphoreType.DMA((3,)),
        ],
        flops=2 * n_slots * rows * width,
        moved=moved,
        limit=FULL,
        in_specs=[hbm] * 3,
        out_specs=(hbm, hbm),
    )(picks_t, home, sources)
    near_in = exchange(near_q)
    *far_q, far_code = call(
        functools.partial(gather_partner, n_picks=n_picks, **sizes),
        tuple([sds((message, width), BF16)] * side) + gather_out[1:],
        gather_scratch + [pltpu.VMEM((rows, width), BF16)],
        flops=HIDE,
        moved=moved,
        limit=FULL,
        in_specs=[vmem] * 3,
        out_specs=tuple([hbm] * (side + 1)),
    )(home, far_mine, far_other)
    far_in = far_q[:1] + [
        lax.ppermute(far_q[k], "src", [(i, i ^ k) for i in range(n_src)]) for k in range(1, side)
    ]

    here = (me * n_tgt + core) * per_device + jnp.arange(per_device, dtype=jnp.int32)
    counts = jnp.sum(jnp.where(home == here[:, None], row_count[None, :], 0), axis=1)
    n_half = side * capacity
    options = dict(capacity=capacity, block=BLOCK)
    work = dict(flops=2 * n_slots * n_cols * width, moved=2 * (n_slots + per_device * n_cols) * width)
    n_tiles = message * width // 2048 + 1
    pooled = sds((side, n_tiles, 16, 128), BF16)
    row_block = capacity * math.gcd(side, ROW_GROUPS)
    near_s, near_col, near_fwd = call(
        functools.partial(near_scores, **options),
        (
            sds((per_device, n_half, n_cols), F32),
            sds((per_device, 8, n_cols), F32),
            sds((per_device, n_half, 128), F32),
        ),
        exps=2 * n_slots * n_cols,
        in_specs=[smem, vmem, vmem],
        out_specs=(vmem, vmem, vmem),
        **work,
    )(counts, near_in, targets)
    tails = pltpu.VMEM((side, 16, 128), F32)
    far_pool, reverse = call(
        functools.partial(far_owner, block=row_block, side=side),
        (pltpu.HBM(pooled.shape, BF16), pltpu.HBM((per_device, 8, n_cols), F32)),
        [
            pltpu.VMEM((per_device, side, capacity, width), BF16),
            pltpu.VMEM((per_device, n_half, n_cols), F32),
            pltpu.VMEM((per_device, n_half, n_cols), BF16),
            pltpu.VMEM((side, n_tiles, 16, 128), BF16),
            tails,
            pltpu.VMEM((per_device, 8, n_cols), F32),
            pltpu.SemaphoreType.DMA((per_device, side)),
            pltpu.SemaphoreType.DMA((per_device, side)),
            pltpu.SemaphoreType.DMA,
        ],
        exps=3 * n_slots * n_cols,
        in_specs=[smem, vmem, vmem] + [hbm] * side,
        out_specs=(hbm, hbm),
        **work,
    )(counts, near_col, targets, *far_in)
    back_far = exchange(far_pool)
    near_pool = call(
        functools.partial(near_owner, capacity=capacity, block=row_block),
        pooled,
        [pltpu.VMEM((n_half, n_cols), BF16), tails],
        n_in=4,
        exps=n_slots * n_cols,
        **work,
    )(near_s, reverse, near_fwd, targets)
    back_near = exchange(near_pool)

    def combine(code, back, after, pieces, weight):
        return call(
            functools.partial(combine_kernel, capacity=capacity, side=side),
            (sds((half, width), F32), sds((8, rows), F32)) + tuple(sds((n, width), BF16) for n in pieces),
            [pltpu.VMEM((n_slots, width), BF16), pltpu.VMEM((rows, width), F32)],
            flops=weight * 4 * n_slots * rows * width,
            moved=weight * 2 * (n_slots + 2 * rows) * width,
            in_specs=[vmem, vmem, unread],
            out_specs=tuple([vmem] * (2 + len(pieces))),
        )(code, back, after)

    keep, kmf, send = combine(far_code, back_far, near_code, [half + EXTRA], 1)
    got = lax.ppermute(send, "tgt", twin)
    factors = [pltpu.VMEM((rows, 128), F32)]
    joined = call(
        functools.partial(merge_pair, side=side), letter, factors, n_in=3, moved=10 * half * width
    )(keep, kmf, got)
    from_far = lax.ppermute(joined, "src", partner)

    first = half // 32 * 16
    keep, kmf, *send = combine(near_code, back_near, joined, [first, half - first + EXTRA], 0)
    got = [lax.ppermute(piece, "tgt", twin) for piece in send]
    mine, confidence = call(
        functools.partial(merge_last, side=side),
        (sds((half, width), BF16), sds((1, rows), F32)),
        factors,
        n_in=5,
        moved=10 * half * width,
    )(keep, kmf, *got, from_far)
    other = lax.ppermute(mine, "tgt", twin)
    first = jnp.where(core == 0, mine, other)
    second = jnp.where(core == 0, other, mine)
    return (jnp.concatenate([first, second], axis=0), confidence[0].astype(BF16))


def solution(mesh):
    placed = (P("src", None), P(("src", "tgt"), None, None), P("src", None), P(), P())
    return jax.shard_map(
        shards, mesh=mesh, in_specs=placed, out_specs=(P("src", None), P("src")), check_vma=False
    )
```

```python
import functools
import math

import jax
import jax.numpy as jnp
from jax import lax
from jax.experimental import pallas as pl
from jax.experimental.pallas import tpu as pltpu
from jax.sharding import PartitionSpec as P

NEGATIVE = -1e30
SHARPNESS = 2.5
EXTRA = 16
F32, BF16 = jnp.float32, jnp.bfloat16
MIB = 1 << 20
LOG2E = math.log2(math.e)
LN2 = math.log(2.0)
BLOCK = 128
ROW_GROUPS = 8
LIMIT = 24
FULL = 63
HIDE = 20_000_000_000


def iota(shape, axis):
    return lax.broadcasted_iota(jnp.int32, shape, axis)


def place_of(side):
    me = lax.axis_index("src")
    return me // side * side, lax.axis_index("tgt"), lax.rem(me, side)


def call(kernel, out_shape, scratch=(), smem=0, n_in=0, limit=LIMIT, flops=0, moved=0, exps=0, **kw):
    if not kw:
        kw = dict(
            in_specs=[pl.BlockSpec(memory_space=pltpu.SMEM)] * smem
            + [pl.BlockSpec(memory_space=pltpu.VMEM)] * (n_in - smem),
            out_specs=jax.tree.map(lambda _: pl.BlockSpec(memory_space=pltpu.VMEM), out_shape),
        )
    return pl.pallas_call(
        kernel,
        out_shape=out_shape,
        scratch_shapes=list(scratch),
        compiler_params=pltpu.CompilerParams(vmem_limit_bytes=limit * MIB),
        cost_estimate=pl.CostEstimate(flops=flops, bytes_accessed=moved, transcendentals=exps),
        **kw,
    )


def columns(rows, width):
    stacked = jnp.concatenate(rows + [jnp.zeros((128 - len(rows), width), F32)], axis=0)
    return stacked.T


def three(row):
    high = row.astype(BF16).astype(F32)
    middle = (row - high).astype(BF16).astype(F32)
    return [high, middle, row - high - middle]


def extra_rows(first, second, width):
    parts = three(first) + three(second)
    body = jnp.concatenate(parts + [jnp.zeros((EXTRA - len(parts), first.shape[1]), F32)], axis=0)
    rest = jnp.zeros((EXTRA, width - first.shape[1]), F32)
    return jnp.concatenate([body, rest], axis=1).astype(BF16)


def read_extra(ref, start, length):
    block = ref[start : start + EXTRA, :length].astype(F32)
    first = (block[0:1] + block[1:2]) + block[2:3]
    second = (block[3:4] + block[4:5]) + block[5:6]
    return first, second


def one_hot_slots(code, start, group, capacity):
    rows = code.shape[1]
    order = iota((capacity, rows), 0).astype(F32)
    return jnp.concatenate(
        [jnp.where(order == code[b : b + 1, :], 1.0, 0.0) for b in range(start, start + group)], axis=0
    )


def gather_body(
    info, flip, picks, home_ref, load, q_hbm, code_hbm, q_ref, code_ref, sem, *, n_tgt, per_device, capacity, group
):
    n_buckets, rows = code_ref.shape
    n_clusters = home_ref.shape[1]
    width = q_ref.shape[2]
    per_message = group // per_device
    cluster = iota((n_clusters, rows), 0).astype(F32)
    member = jnp.zeros((n_clusters, rows), F32)
    for pick in picks:
        member = jnp.where(cluster == pick, 1.0, member)
    bucket = iota((n_buckets, n_clusters), 0)
    earlier = jnp.where(iota((rows, rows), 0) < iota((rows, rows), 1), 1.0, 0.0).astype(BF16)

    def ranks(turn):
        holder = (info[0] + lax.bitwise_xor(lax.div(bucket, per_device), turn)) * n_tgt + info[1]
        place = holder * per_device + lax.rem(bucket, per_device)
        chosen = jnp.where(home_ref[...] == place, 1.0, 0.0).astype(BF16)
        inside = jnp.dot(chosen, member.astype(BF16), preferred_element_type=F32)
        rank = jnp.dot(inside.astype(BF16), earlier, preferred_element_type=F32)
        return jnp.where(inside > 0.5, rank, -1.0)

    code = ranks(0)
    code_ref[...] = code
    leave = [pltpu.make_async_copy(code_ref, code_hbm, sem.at[0])]
    leave[0].start()
    if flip is not None:
        code = ranks(flip)
    source = load()
    for start in range(0, n_buckets, group):
        slots = one_hot_slots(code, start, group, capacity)
        filled = jnp.sum(slots, axis=1, keepdims=True)
        found = jnp.dot(slots.astype(BF16), source, preferred_element_type=F32)
        head = found[:, :128]
        head = jnp.where((iota(head.shape, 1) == 0) & (filled < 0.5), jnp.inf, head)
        found = jnp.concatenate([head, found[:, 128:]], axis=1).astype(BF16)
        d = start // per_device
        at = pl.ds(d, per_message)
        q_ref[at] = found.reshape(per_message, per_device * capacity, width)
        if flip is None:
            leave.append(pltpu.make_async_copy(q_ref.at[at], q_hbm.at[at], sem.at[1 + start // group]))
            leave[-1].start()
        else:
            for k in range(d, d + per_message):
                leave.append(pltpu.make_async_copy(q_ref.at[k], q_hbm[k], sem.at[1 + k]))
                leave[-1].start()
    for copy in leave:
        copy.wait()


def half_with_picks(picks_hbm, src_hbm, out_ref, picks_ref, sems, *, side):
    _, core, _ = place_of(side)
    n_picks, rows = picks_ref.shape
    width = src_hbm.shape[1]
    half = rows // 2
    mine = pl.ds(pl.multiple_of(core * half, 16), half)
    names = pltpu.make_async_copy(picks_hbm, picks_ref, sems.at[0])
    names.start()
    body = pltpu.make_async_copy(src_hbm.at[mine, :], out_ref.at[pl.ds(0, half), :], sems.at[1])
    body.start()
    names.wait()
    names = jnp.concatenate([picks_ref[...].astype(F32), jnp.zeros((EXTRA - n_picks, rows), F32)], axis=0)
    rest = jnp.zeros((EXTRA, width - rows), F32)
    out_ref[half:, :] = jnp.concatenate([names, rest], axis=1).astype(BF16)
    body.wait()


def gather_own(picks_hbm, home_hbm, src_hbm, *refs, side, **sizes):
    *refs, picks_ref, home_ref, src_ref, sems = refs
    copies = []
    for i, (here, there) in enumerate(((picks_hbm, picks_ref), (home_hbm, home_ref), (src_hbm, src_ref))):
        copies.append(pltpu.make_async_copy(here, there, sems.at[i]))
        copies[-1].start()
    copies[0].wait()
    copies[1].wait()
    picks = [picks_ref[k : k + 1, :].astype(F32) for k in range(picks_ref.shape[0])]

    def load():
        copies[2].wait()
        return src_ref[...]

    gather_body(place_of(side), None, picks, home_ref, load, *refs, **sizes)


def gather_partner(home_ref, mine_ref, other_ref, *refs, n_picks, side, **sizes):
    info = place_of(side)
    *q_hbm, code_hbm, q_ref, code_ref, sem, src_ref = refs
    rows = src_ref.shape[0]
    half = rows // 2
    src_ref[pl.ds(pl.multiple_of(info[1] * half, 16), half), :] = mine_ref[:half, :]
    src_ref[pl.ds(pl.multiple_of((1 - info[1]) * half, 16), half), :] = other_ref[:half, :]
    block = mine_ref[half : half + EXTRA, :rows].astype(F32)
    picks = [block[k : k + 1, :] for k in range(n_picks)]
    load = lambda: src_ref[...]
    gather_body(info, info[2], picks, home_ref, load, q_hbm, code_hbm, q_ref, code_ref, sem, **sizes)


def scores_of(q, t, count):
    width = q.shape[1]
    n_cols = t.shape[0]
    head = q[:, :128].astype(F32)
    empty = head > 1e38
    q = jnp.concatenate([jnp.where(empty, 0.0, head).astype(BF16), q[:, 128:]], axis=1)
    s = lax.dot_general(q, t, (((1,), (1,)), ((), ())), preferred_element_type=F32)
    column_bias = jnp.where(iota((1, n_cols), 1) < count, 0.0, NEGATIVE).astype(F32)
    slot_bias = jnp.where(empty[:, 0:1], NEGATIVE, 0.0).astype(F32)
    return s * (SHARPNESS / math.sqrt(width) * LOG2E) + column_bias + slot_bias


def column_part(s_ref, highest, block):
    n_rows, n_cols = s_ref.shape
    total = jnp.zeros((8, n_cols), F32)
    for start in range(0, n_rows, block):
        part = jnp.exp2(s_ref[start : start + block, :] - highest)
        total = total + jnp.sum(part.reshape(block // 8, 8, n_cols), axis=0)
    return jnp.sum(total, axis=0, keepdims=True)


def row_log_sum(s):
    top = jnp.max(s, axis=1, keepdims=True)
    return top + jnp.log2(jnp.sum(jnp.exp2(s - top), axis=1, keepdims=True))


def weigh(s, half_reverse):
    shifted = s - half_reverse
    top = jnp.max(shifted, axis=1, keepdims=True)
    e = jnp.exp2(shifted - top)
    total = jnp.sum(e, axis=1, keepdims=True)
    return (e * (1.0 / total)).astype(BF16), top + jnp.log2(total)


def put_pool(p_ref, l, p, capacity):
    strips, cols = capacity // 16, p.shape[1] // 128
    for k in range(p_ref.shape[0]):
        for r in range(strips):
            strip = p[k * capacity + 16 * r : k * capacity + 16 * (r + 1)]
            for c in range(cols):
                p_ref[k, (l * strips + r) * cols + c] = strip[:, 128 * c : 128 * (c + 1)]


def put_tail(tail_ref, l, first, margin, forward, capacity):
    strips = capacity // 16
    shape = (margin.shape[0], 128)
    parts = three(jnp.broadcast_to(margin, shape)) + three(jnp.broadcast_to(forward, shape))
    turn = lax.rem(iota(shape, 1), 6)
    mixed = parts[5]
    for i in range(5):
        mixed = jnp.where(turn == i, parts[i], mixed)
    strip_of = lax.div(iota((16, 128), 1), 6)
    for k in range(margin.shape[0] // capacity):
        tile = tail_ref[first + k] if l else jnp.zeros((16, 128), F32)
        for r in range(strips):
            at = slice(k * capacity + 16 * r, k * capacity + 16 * (r + 1))
            tile = jnp.where(strip_of == l * strips + r, mixed[at], tile)
        tail_ref[first + k] = tile


def near_scores(count_ref, q_ref, t_ref, s_ref, col_ref, fwd_ref, *, capacity, block):
    per_device, n_half, n_cols = s_ref.shape
    for l in range(per_device):
        q = q_ref[:, l * capacity : (l + 1) * capacity, :].reshape(n_half, -1)
        s = scores_of(q, t_ref[l], count_ref[l])
        s_ref[l] = s
        highest = jnp.max(s, axis=0, keepdims=True)
        total = column_part(s_ref.at[l], highest, block)
        col_ref[l] = jnp.concatenate([highest, total, jnp.zeros((6, n_cols), F32)], axis=0)

        def forward(i, _):
            at = pl.ds(pl.multiple_of(i * block, block), block)
            fwd_ref[l, at, :] = jnp.broadcast_to(row_log_sum(s_ref[l, at, :]), (block, 128))
            return 0

        lax.fori_loop(0, n_half // block, forward, 0)


def far_owner(count_ref, col_ref, t_ref, *refs, block, side):
    _, _, here = place_of(side)
    *q_hbm, p_hbm, rev_hbm, q_ref, s_ref, w_ref, p_ref, tail_ref, rev_ref, q_sem, p_sem, rev_sem = refs
    per_device, n_msg, capacity, width = q_ref.shape
    _, n_half, n_cols = s_ref.shape
    tiles = capacity * width // 2048
    arrive, leave = [], []
    for l in range(per_device):
        at = pl.ds(l * capacity, capacity)
        arrive.append([pltpu.make_async_copy(q_hbm[k].at[at, :], q_ref.at[l, k], q_sem.at[l, k]) for k in range(n_msg)])
        at = pl.ds(l * tiles, tiles + l // (per_device - 1))
        to = [p_hbm.at[lax.bitwise_xor(here, k), at] for k in range(n_msg)]
        leave.append([pltpu.make_async_copy(p_ref.at[k, at], to[k], p_sem.at[l, k]) for k in range(n_msg)])
    for copy in arrive[0]:
        copy.start()
    rev_leave = pltpu.make_async_copy(rev_ref, rev_hbm, rev_sem)
    half_reverse = []
    for l in range(per_device):
        for copy in arrive[l]:
            copy.wait()
        for copy in arrive[l + 1] if l + 1 < per_device else []:
            copy.start()
        s = scores_of(q_ref[l].reshape(n_half, width), t_ref[l], count_ref[l])
        s_ref[l] = s
        highest = jnp.max(s, axis=0, keepdims=True)
        total = column_part(s_ref.at[l], highest, block)
        top = jnp.maximum(highest, col_ref[l, 0:1, :])
        total = total * jnp.exp2(highest - top) + col_ref[l, 1:2, :] * jnp.exp2(col_ref[l, 0:1, :] - top)
        half_reverse.append(0.5 * (top + jnp.log2(total)))
        rev_ref[l] = jnp.broadcast_to(half_reverse[l], (8, n_cols))
    rev_leave.start()
    for l in range(per_device):
        for start in range(0, n_half, block):
            at = slice(start, start + block)
            s = s_ref[l, at, :]
            forward = row_log_sum(s)
            w, margin = weigh(s, half_reverse[l])
            w_ref[l, at, :] = w
            put_tail(tail_ref, l, start // capacity, margin, forward, capacity)
        p = jnp.dot(w_ref[l], t_ref[l], preferred_element_type=F32).astype(BF16)
        put_pool(p_ref, l, p, capacity)
        if l == per_device - 1:
            p_ref[:, per_device * tiles] = tail_ref[...].astype(BF16)
        for copy in leave[l]:
            copy.start()
    for copy in sum(leave, [rev_leave]):
        copy.wait()


def near_owner(s_ref, rev_ref, fwd_ref, t_ref, p_ref, w_ref, tail_ref, *, capacity, block):
    per_device, n_half, _ = s_ref.shape
    for l in range(per_device):
        half_reverse = rev_ref[l, 0:1, :]
        for start in range(0, n_half, block):
            at = slice(start, start + block)
            w, margin = weigh(s_ref[l, at, :], half_reverse)
            w_ref[at, :] = w
            put_tail(tail_ref, l, start // capacity, margin, fwd_ref[l, at, 0:1], capacity)
        p = jnp.dot(w_ref[...], t_ref[l], preferred_element_type=F32).astype(BF16)
        put_pool(p_ref, l, p, capacity)
    p_ref[:, p_ref.shape[1] - 1] = tail_ref[...].astype(BF16)


def combine_kernel(code_ref, r_ref, _, *refs, capacity, side, split):
    _, core, _ = place_of(side)
    *outs, r_scr, scr = refs
    n_buckets, rows = code_ref.shape
    width = scr.shape[1]
    half = rows // 2
    n_msg, n_tiles, _, _ = r_ref.shape
    cols = width // 128
    strips = n_tiles // cols
    margin, forward = [], []
    for j in range(n_msg):
        last = r_ref[j, n_tiles - 1].astype(F32)
        last = (last + pltpu.roll(last, 127, 1)) + pltpu.roll(last, 126, 1)
        for r in range(strips):
            margin.append(jnp.broadcast_to(last[:, 6 * r : 6 * r + 1], (16, 128)))
            forward.append(jnp.broadcast_to(last[:, 6 * r + 3 : 6 * r + 4], (16, 128)))
            at = slice((j * strips + r) * 16, (j * strips + r + 1) * 16)
            for c in range(cols):
                r_scr[at, 128 * c : 128 * (c + 1)] = r_ref[j, r * cols + c]
    margin = jnp.concatenate([jnp.concatenate(margin, axis=0)] * (rows // 128), axis=1)
    forward = jnp.concatenate([jnp.concatenate(forward, axis=0)] * (rows // 128), axis=1)
    slots = one_hot_slots(code_ref[...], 0, n_buckets, capacity) > 0.5

    def merged(column):
        top = jnp.max(jnp.where(slots, column, NEGATIVE), axis=0, keepdims=True)
        total = jnp.sum(jnp.where(slots, jnp.exp2(column - top), 0.0), axis=0, keepdims=True)
        return jnp.where(total > 0.0, top + jnp.log2(jnp.where(total > 0.0, total, 1.0)), NEGATIVE)

    margin_row, forward_row = merged(margin), merged(forward)
    factor = jnp.where(slots, jnp.exp2(margin - margin_row), 0.0)
    high = factor.astype(BF16)
    low = (factor - high.astype(F32)).astype(BF16)
    r = r_scr[...]
    over = (((0,), (0,)), ((), ()))
    pooled = lax.dot_general(high, r, over, preferred_element_type=F32)
    scr[...] = pooled + lax.dot_general(low, r, over, preferred_element_type=F32)
    last = extra_rows(margin_row, forward_row, width)
    if split:
        keep_ref, kmf_ref, send_ref = outs
        keep_ref[...] = scr[pl.ds(pl.multiple_of(core * half, 16), half), :]
        send_ref[:half, :] = scr[pl.ds(pl.multiple_of((1 - core) * half, 16), half), :].astype(BF16)
        send_ref[half:, :] = last
        kmf_ref[...] = jnp.concatenate([margin_row, forward_row, jnp.zeros((6, rows), F32)], axis=0)
    else:
        start = 0
        for ref in outs:
            count = min(ref.shape[0], rows - start)
            ref[:count, :] = scr[start : start + count, :].astype(BF16)
            start = start + count
        outs[-1][count:, :] = last


def log_sum(first, second, third=None):
    top = jnp.maximum(first, second)
    if third is not None:
        top = jnp.maximum(top, third)
    total = jnp.exp2(first - top) + jnp.exp2(second - top)
    if third is not None:
        total = total + jnp.exp2(third - top)
    return top + jnp.log2(total)


def merge_pair(keep_ref, kmf_ref, got_ref, out_ref, scr, *, side):
    _, core, _ = place_of(side)
    half, width = keep_ref.shape
    rows = kmf_ref.shape[1]
    margin, forward = kmf_ref[0:1, :], kmf_ref[1:2, :]
    margin_b, forward_b = read_extra(got_ref, half, rows)
    margin_all, forward_all = log_sum(margin, margin_b), log_sum(forward, forward_b)
    scr[...] = columns([jnp.exp2(margin - margin_all), jnp.exp2(margin_b - margin_all)], rows)
    factors = scr[pl.ds(pl.multiple_of(core * half, 16), half), :]
    out = keep_ref[...] * factors[:, 0:1] + got_ref[:half, :].astype(F32) * factors[:, 1:2]
    out_ref[:half, :] = out.astype(BF16)
    out_ref[half:, :] = extra_rows(margin_all, forward_all, width)


def merge_last(*refs, n_pieces, side):
    _, core, _ = place_of(side)
    own, got = refs[:n_pieces], refs[n_pieces : 2 * n_pieces]
    mine_ref, other_ref, out_ref, conf_ref, far_scr = refs[2 * n_pieces :]
    rows, width = out_ref.shape
    half = rows // 2
    first_core = core == 0
    far_scr[pl.ds(pl.multiple_of(core * half, 16), half), :] = mine_ref[:half, :]
    far_scr[pl.ds(pl.multiple_of((1 - core) * half, 16), half), :] = other_ref[:half, :]
    last = own[-1].shape[0] - EXTRA
    pair = read_extra(own[-1], last, rows), read_extra(got[-1], last, rows)
    margin_a, forward_a = [jnp.where(first_core, x, y) for x, y in zip(*pair)]
    margin_b, forward_b = [jnp.where(first_core, y, x) for x, y in zip(*pair)]
    margin_c, forward_c = read_extra(mine_ref, half, rows)
    margin_all = log_sum(margin_a, margin_b, margin_c)
    forward_all = log_sum(forward_a, forward_b, forward_c)
    conf_ref[...] = (margin_all - 0.5 * forward_all) * LN2
    factors = columns([jnp.exp2(x - margin_all) for x in (margin_a, margin_b, margin_c)], rows)
    start = 0
    for x_ref, y_ref in zip(own, got):
        count = min(x_ref.shape[0], rows - start)
        at = slice(start, start + count)
        x, y = x_ref[:count, :], y_ref[:count, :]
        a = jnp.where(first_core, x, y).astype(F32) * factors[at, 0:1]
        b = jnp.where(first_core, y, x).astype(F32) * factors[at, 1:2]
        out_ref[at, :] = (a + b + far_scr[at, :].astype(F32) * factors[at, 2:3]).astype(BF16)
        start = start + count


def shards(sources, targets, picks, cluster_home, row_count):
    n_src, n_tgt = lax.axis_size("src"), lax.axis_size("tgt")
    rows, width = sources.shape
    per_device, n_cols, _ = targets.shape
    n_clusters = cluster_home.shape[0]
    n_picks = picks.shape[1]
    capacity = -(-(2 * n_picks * rows // n_clusters) // 16) * 16
    side = n_src // 2
    half = rows // 2
    message = per_device * capacity
    n_buckets = side * per_device
    n_slots = n_buckets * capacity
    group = max(g for g in range(per_device, n_buckets + 1, per_device) if n_buckets % g == 0 and g * capacity <= 400)
    sds = jax.ShapeDtypeStruct

    me, core = lax.axis_index("src"), lax.axis_index("tgt")
    partner = [(i, (i + side) % n_src) for i in range(n_src)]
    twin = [(i, 1 - i) for i in range(n_tgt)]
    halves = [list(range(side)), list(range(side, n_src))]

    def exchange(x):
        return lax.all_to_all(x, "src", split_axis=0, concat_axis=0, axis_index_groups=halves, tiled=True)

    picks_t = picks.T
    home = cluster_home[None, :]
    letter = sds((half + EXTRA, width), BF16)
    hbm = pl.BlockSpec(memory_space=pltpu.HBM)
    vmem = pl.BlockSpec(memory_space=pltpu.VMEM)
    smem = pl.BlockSpec(memory_space=pltpu.SMEM)
    unread = pl.BlockSpec(memory_space=pl.ANY)
    mine = call(
        functools.partial(half_with_picks, side=side),
        letter,
        [pltpu.VMEM((n_picks, rows), jnp.int32), pltpu.SemaphoreType.DMA((2,))],
        moved=4 * half * width,
        limit=FULL,
        in_specs=[hbm, hbm],
        out_specs=vmem,
    )(picks_t, sources)
    far_mine = lax.ppermute(mine, "src", partner)
    far_other = lax.ppermute(far_mine, "tgt", twin)

    sizes = dict(side=side, n_tgt=n_tgt, per_device=per_device, capacity=capacity, group=group)
    gather_out = (sds((side, message, width), BF16), sds((n_buckets, rows), F32))
    moved = 2 * (n_slots + rows) * width
    gather_scratch = [
        pltpu.VMEM((side, message, width), BF16),
        pltpu.VMEM((n_buckets, rows), F32),
        pltpu.SemaphoreType.DMA((1 + side,)),
    ]
    near_q, near_code = call(
        functools.partial(gather_own, **sizes),
        gather_out,
        gather_scratch
        + [
            pltpu.VMEM((n_picks, rows), jnp.int32),
            pltpu.VMEM((1, n_clusters), jnp.int32),
            pltpu.VMEM((rows, width), BF16),
            pltpu.SemaphoreType.DMA((3,)),
        ],
        flops=2 * n_slots * rows * width,
        moved=moved,
        limit=FULL,
        in_specs=[hbm] * 3,
        out_specs=(hbm, hbm),
    )(picks_t, home, sources)
    near_in = exchange(near_q)
    *far_q, far_code = call(
        functools.partial(gather_partner, n_picks=n_picks, **sizes),
        tuple([pltpu.HBM((message, width), BF16)] * side) + (pltpu.HBM((n_buckets, rows), F32),),
        gather_scratch + [pltpu.VMEM((rows, width), BF16)],
        flops=HIDE,
        moved=moved,
        in_specs=[vmem] * 3,
        out_specs=tuple([hbm] * (side + 1)),
    )(home, far_mine, far_other)
    far_in = far_q[:1] + [
        lax.ppermute(far_q[k], "src", [(i, i ^ k) for i in range(n_src)]) for k in range(1, side)
    ]

    here = (me * n_tgt + core) * per_device + jnp.arange(per_device, dtype=jnp.int32)
    counts = jnp.sum(jnp.where(home == here[:, None], row_count[None, :], 0), axis=1)
    n_half = side * capacity
    options = dict(capacity=capacity, block=BLOCK)
    work = dict(flops=2 * n_slots * n_cols * width, moved=2 * (n_slots + per_device * n_cols) * width)
    n_tiles = message * width // 2048 + 1
    pooled = sds((side, n_tiles, 16, 128), BF16)
    row_block = capacity * math.gcd(side, ROW_GROUPS)
    near_s, near_col, near_fwd = call(
        functools.partial(near_scores, **options),
        (
            sds((per_device, n_half, n_cols), F32),
            sds((per_device, 8, n_cols), F32),
            sds((per_device, n_half, 128), F32),
        ),
        exps=2 * n_slots * n_cols,
        in_specs=[smem, vmem, vmem],
        out_specs=(vmem, vmem, vmem),
        **work,
    )(counts, near_in, targets)
    tails = pltpu.VMEM((side, 16, 128), F32)
    far_pool, reverse = call(
        functools.partial(far_owner, block=row_block, side=side),
        (pltpu.HBM(pooled.shape, BF16), pltpu.HBM((per_device, 8, n_cols), F32)),
        [
            pltpu.VMEM((per_device, side, capacity, width), BF16),
            pltpu.VMEM((per_device, n_half, n_cols), F32),
            pltpu.VMEM((per_device, n_half, n_cols), BF16),
            pltpu.VMEM((side, n_tiles, 16, 128), BF16),
            tails,
            pltpu.VMEM((per_device, 8, n_cols), F32),
            pltpu.SemaphoreType.DMA((per_device, side)),
            pltpu.SemaphoreType.DMA((per_device, side)),
            pltpu.SemaphoreType.DMA,
        ],
        exps=3 * n_slots * n_cols,
        in_specs=[smem, vmem, vmem] + [hbm] * side,
        out_specs=(hbm, hbm),
        **work,
    )(counts, near_col, targets, *far_in)
    back_far = exchange(far_pool)
    near_pool = call(
        functools.partial(near_owner, capacity=capacity, block=row_block),
        pooled,
        [pltpu.VMEM((n_half, n_cols), BF16), tails],
        n_in=4,
        exps=n_slots * n_cols,
        **work,
    )(near_s, reverse, near_fwd, targets)
    back_near = exchange(near_pool)

    def combine(code, back, after, outs, weight, split):
        return call(
            functools.partial(combine_kernel, capacity=capacity, side=side, split=split),
            outs,
            [pltpu.VMEM((n_slots, width), BF16), pltpu.VMEM((rows, width), F32)],
            flops=weight * 4 * n_slots * rows * width,
            moved=weight * 2 * (n_slots + 2 * rows) * width,
            in_specs=[vmem, vmem, unread],
            out_specs=tuple([vmem] * len(outs)),
        )(code, back, after)

    outs = (sds((half, width), F32), sds((8, rows), F32), letter)
    keep, kmf, send = combine(far_code, back_far, near_code, outs, 1, True)
    got = lax.ppermute(send, "tgt", twin)
    joined = call(
        functools.partial(merge_pair, side=side),
        letter,
        [pltpu.VMEM((rows, 128), F32)],
        n_in=3,
        moved=10 * half * width,
    )(keep, kmf, got)
    from_far = lax.ppermute(joined, "src", partner)
    from_far_other = lax.ppermute(from_far, "tgt", twin)

    pieces = [rows // 4] * 3 + [rows // 4 + EXTRA]
    own = combine(near_code, back_near, joined, tuple(sds((n, width), BF16) for n in pieces), 0, False)
    got = [lax.ppermute(piece, "tgt", twin) for piece in own]
    pooled, confidence = call(
        functools.partial(merge_last, n_pieces=len(pieces), side=side),
        (sds((rows, width), BF16), sds((1, rows), F32)),
        [pltpu.VMEM((rows, width), BF16)],
        n_in=2 * len(pieces) + 2,
        moved=10 * rows * width,
    )(*own, *got, from_far, from_far_other)
    return (pooled, confidence[0].astype(BF16))


def solution(mesh):
    placed = (P("src", None), P(("src", "tgt"), None, None), P("src", None), P(), P())
    return jax.shard_map(
        shards, mesh=mesh, in_specs=placed, out_specs=(P("src", None), P("src")), check_vma=False
    )
```

```python
import functools
import math

import jax
import jax.numpy as jnp
from jax import lax
from jax.experimental import pallas as pl
from jax.experimental.pallas import tpu as pltpu
from jax.sharding import PartitionSpec as P

NEGATIVE = -1e30
SHARPNESS = 2.5
EXTRA = 16
F32, BF16 = jnp.float32, jnp.bfloat16
MIB = 1 << 20
LOG2E = math.log2(math.e)
LN2 = math.log(2.0)
BLOCK = 128
ROW_GROUPS = 8
LIMIT = 24
FULL = 63
HIDE = 20_000_000_000


def iota(shape, axis):
    return lax.broadcasted_iota(jnp.int32, shape, axis)


def place_of(side):
    me = lax.axis_index("src")
    return me // side * side, lax.axis_index("tgt"), lax.rem(me, side)


def call(kernel, out_shape, scratch=(), smem=0, n_in=0, limit=LIMIT, flops=0, moved=0, exps=0, **kw):
    if not kw:
        kw = dict(
            in_specs=[pl.BlockSpec(memory_space=pltpu.SMEM)] * smem
            + [pl.BlockSpec(memory_space=pltpu.VMEM)] * (n_in - smem),
            out_specs=jax.tree.map(lambda _: pl.BlockSpec(memory_space=pltpu.VMEM), out_shape),
        )
    return pl.pallas_call(
        kernel,
        out_shape=out_shape,
        scratch_shapes=list(scratch),
        compiler_params=pltpu.CompilerParams(vmem_limit_bytes=limit * MIB),
        cost_estimate=pl.CostEstimate(flops=flops, bytes_accessed=moved, transcendentals=exps),
        **kw,
    )


def columns(rows, width):
    stacked = jnp.concatenate(rows + [jnp.zeros((128 - len(rows), width), F32)], axis=0)
    return stacked.T


def three(row):
    high = row.astype(BF16).astype(F32)
    middle = (row - high).astype(BF16).astype(F32)
    return [high, middle, row - high - middle]


def extra_rows(first, second, width):
    parts = three(first) + three(second)
    body = jnp.concatenate(parts + [jnp.zeros((EXTRA - len(parts), first.shape[1]), F32)], axis=0)
    rest = jnp.zeros((EXTRA, width - first.shape[1]), F32)
    return jnp.concatenate([body, rest], axis=1).astype(BF16)


def read_extra(ref, start, length):
    block = ref[start : start + EXTRA, :length].astype(F32)
    first = (block[0:1] + block[1:2]) + block[2:3]
    second = (block[3:4] + block[4:5]) + block[5:6]
    return first, second


def one_hot_slots(code, start, group, capacity):
    rows = code.shape[1]
    order = iota((capacity, rows), 0).astype(F32)
    return jnp.concatenate(
        [jnp.where(order == code[b : b + 1, :], 1.0, 0.0) for b in range(start, start + group)], axis=0
    )


def gather_body(
    info, flip, picks, home_ref, load, q_hbm, code_hbm, q_ref, code_ref, sem, *, n_tgt, per_device, capacity, group
):
    n_buckets, rows = code_ref.shape
    n_clusters = home_ref.shape[1]
    width = q_ref.shape[2]
    per_message = group // per_device
    cluster = iota((n_clusters, rows), 0).astype(F32)
    member = jnp.zeros((n_clusters, rows), F32)
    for pick in picks:
        member = jnp.where(cluster == pick, 1.0, member)
    bucket = iota((n_buckets, n_clusters), 0)
    earlier = jnp.where(iota((rows, rows), 0) < iota((rows, rows), 1), 1.0, 0.0).astype(BF16)

    def ranks(turn):
        holder = (info[0] + lax.bitwise_xor(lax.div(bucket, per_device), turn)) * n_tgt + info[1]
        place = holder * per_device + lax.rem(bucket, per_device)
        chosen = jnp.where(home_ref[...] == place, 1.0, 0.0).astype(BF16)
        inside = jnp.dot(chosen, member.astype(BF16), preferred_element_type=F32)
        rank = jnp.dot(inside.astype(BF16), earlier, preferred_element_type=F32)
        return jnp.where(inside > 0.5, rank, -1.0)

    code = ranks(0)
    code_ref[...] = code
    leave = [pltpu.make_async_copy(code_ref, code_hbm, sem.at[0])]
    leave[0].start()
    if flip is not None:
        code = ranks(flip)
    source = load()
    for start in range(0, n_buckets, group):
        slots = one_hot_slots(code, start, group, capacity)
        filled = jnp.sum(slots, axis=1, keepdims=True)
        found = jnp.dot(slots.astype(BF16), source, preferred_element_type=F32)
        head = found[:, :128]
        head = jnp.where((iota(head.shape, 1) == 0) & (filled < 0.5), jnp.inf, head)
        found = jnp.concatenate([head, found[:, 128:]], axis=1).astype(BF16)
        d = start // per_device
        at = pl.ds(d, per_message)
        q_ref[at] = found.reshape(per_message, per_device * capacity, width)
        if flip is None:
            leave.append(pltpu.make_async_copy(q_ref.at[at], q_hbm.at[at], sem.at[1 + start // group]))
            leave[-1].start()
        else:
            for k in range(d, d + per_message):
                leave.append(pltpu.make_async_copy(q_ref.at[k], q_hbm[k], sem.at[1 + k]))
                leave[-1].start()
    for copy in leave:
        copy.wait()


def gather_own(picks_hbm, home_hbm, src_hbm, letter_hbm, *refs, side, **sizes):
    *refs, picks_ref, home_ref, src_ref, last_ref, sems = refs
    info = place_of(side)
    copies = []
    for i, (here, there) in enumerate(((picks_hbm, picks_ref), (home_hbm, home_ref), (src_hbm, src_ref))):
        copies.append(pltpu.make_async_copy(here, there, sems.at[i]))
        copies[-1].start()
    copies[0].wait()
    copies[1].wait()
    n_picks, rows = picks_ref.shape
    width = src_ref.shape[1]
    half = rows // 2
    names = picks_ref[...].astype(F32)
    picks = [names[k : k + 1, :] for k in range(n_picks)]
    names = jnp.concatenate([names, jnp.zeros((EXTRA - n_picks, rows), F32)], axis=0)
    last_ref[...] = jnp.concatenate([names, jnp.zeros((EXTRA, width - rows), F32)], axis=1).astype(BF16)
    mine = pl.ds(pl.multiple_of(info[1] * half, 16), half)
    letter = [
        pltpu.make_async_copy(last_ref, letter_hbm.at[pl.ds(half, EXTRA), :], sems.at[3]),
        pltpu.make_async_copy(src_ref.at[mine, :], letter_hbm.at[pl.ds(0, half), :], sems.at[4]),
    ]
    letter[0].start()

    def load():
        copies[2].wait()
        letter[1].start()
        return src_ref[...]

    gather_body(info, None, picks, home_ref, load, *refs, **sizes)
    for copy in letter:
        copy.wait()


def gather_partner(home_ref, mine_ref, other_ref, *refs, n_picks, side, **sizes):
    info = place_of(side)
    *q_hbm, code_hbm, q_ref, code_ref, sem, src_ref = refs
    rows = src_ref.shape[0]
    half = rows // 2
    src_ref[pl.ds(pl.multiple_of(info[1] * half, 16), half), :] = mine_ref[:half, :]
    src_ref[pl.ds(pl.multiple_of((1 - info[1]) * half, 16), half), :] = other_ref[:half, :]
    block = mine_ref[half : half + EXTRA, :rows].astype(F32)
    picks = [block[k : k + 1, :] for k in range(n_picks)]
    load = lambda: src_ref[...]
    gather_body(info, info[2], picks, home_ref, load, q_hbm, code_hbm, q_ref, code_ref, sem, **sizes)


def scores_of(q, t, count):
    width = q.shape[1]
    n_cols = t.shape[0]
    head = q[:, :128].astype(F32)
    empty = head > 1e38
    q = jnp.concatenate([jnp.where(empty, 0.0, head).astype(BF16), q[:, 128:]], axis=1)
    s = lax.dot_general(q, t, (((1,), (1,)), ((), ())), preferred_element_type=F32)
    column_bias = jnp.where(iota((1, n_cols), 1) < count, 0.0, NEGATIVE).astype(F32)
    slot_bias = jnp.where(empty[:, 0:1], NEGATIVE, 0.0).astype(F32)
    return s * (SHARPNESS / math.sqrt(width) * LOG2E) + column_bias + slot_bias


def column_part(s_ref, highest, block):
    n_rows, n_cols = s_ref.shape
    total = jnp.zeros((8, n_cols), F32)
    for start in range(0, n_rows, block):
        part = jnp.exp2(s_ref[start : start + block, :] - highest)
        total = total + jnp.sum(part.reshape(block // 8, 8, n_cols), axis=0)
    return jnp.sum(total, axis=0, keepdims=True)


def row_log_sum(s):
    top = jnp.max(s, axis=1, keepdims=True)
    return top + jnp.log2(jnp.sum(jnp.exp2(s - top), axis=1, keepdims=True))


def weigh(s, half_reverse):
    shifted = s - half_reverse
    top = jnp.max(shifted, axis=1, keepdims=True)
    e = jnp.exp2(shifted - top)
    total = jnp.sum(e, axis=1, keepdims=True)
    return (e * (1.0 / total)).astype(BF16), top + jnp.log2(total)


def put_pool(p_ref, l, p, capacity):
    strips, cols = capacity // 16, p.shape[1] // 128
    for k in range(p_ref.shape[0]):
        for r in range(strips):
            strip = p[k * capacity + 16 * r : k * capacity + 16 * (r + 1)]
            for c in range(cols):
                p_ref[k, (l * strips + r) * cols + c] = strip[:, 128 * c : 128 * (c + 1)]


def put_tail(tail_ref, l, first, margin, forward, capacity):
    strips = capacity // 16
    shape = (margin.shape[0], 128)
    parts = three(jnp.broadcast_to(margin, shape)) + three(jnp.broadcast_to(forward, shape))
    turn = lax.rem(iota(shape, 1), 6)
    mixed = parts[5]
    for i in range(5):
        mixed = jnp.where(turn == i, parts[i], mixed)
    strip_of = lax.div(iota((16, 128), 1), 6)
    for k in range(margin.shape[0] // capacity):
        tile = tail_ref[first + k] if l else jnp.zeros((16, 128), F32)
        for r in range(strips):
            at = slice(k * capacity + 16 * r, k * capacity + 16 * (r + 1))
            tile = jnp.where(strip_of == l * strips + r, mixed[at], tile)
        tail_ref[first + k] = tile


def near_scores(count_ref, q_ref, t_ref, s_ref, col_ref, fwd_ref, *, capacity, block):
    per_device, n_half, n_cols = s_ref.shape
    for l in range(per_device):
        q = q_ref[:, l * capacity : (l + 1) * capacity, :].reshape(n_half, -1)
        s = scores_of(q, t_ref[l], count_ref[l])
        s_ref[l] = s
        highest = jnp.max(s, axis=0, keepdims=True)
        total = column_part(s_ref.at[l], highest, block)
        col_ref[l] = jnp.concatenate([highest, total, jnp.zeros((6, n_cols), F32)], axis=0)

        def forward(i, _):
            at = pl.ds(pl.multiple_of(i * block, block), block)
            fwd_ref[l, at, :] = jnp.broadcast_to(row_log_sum(s_ref[l, at, :]), (block, 128))
            return 0

        lax.fori_loop(0, n_half // block, forward, 0)


def far_owner(count_ref, col_ref, t_ref, *refs, block, side):
    _, _, here = place_of(side)
    *q_hbm, p_hbm, rev_hbm, q_ref, s_ref, w_ref, p_ref, tail_ref, rev_ref, q_sem, p_sem, rev_sem = refs
    per_device, n_msg, capacity, width = q_ref.shape
    _, n_half, n_cols = s_ref.shape
    tiles = capacity * width // 2048
    arrive, leave = [], []
    for l in range(per_device):
        at = pl.ds(l * capacity, capacity)
        arrive.append([pltpu.make_async_copy(q_hbm[k].at[at, :], q_ref.at[l, k], q_sem.at[l, k]) for k in range(n_msg)])
        at = pl.ds(l * tiles, tiles + l // (per_device - 1))
        to = [p_hbm.at[lax.bitwise_xor(here, k), at] for k in range(n_msg)]
        leave.append([pltpu.make_async_copy(p_ref.at[k, at], to[k], p_sem.at[l, k]) for k in range(n_msg)])
    for copy in arrive[0]:
        copy.start()
    rev_leave = pltpu.make_async_copy(rev_ref, rev_hbm, rev_sem)
    half_reverse = []
    for l in range(per_device):
        for copy in arrive[l]:
            copy.wait()
        for copy in arrive[l + 1] if l + 1 < per_device else []:
            copy.start()
        s = scores_of(q_ref[l].reshape(n_half, width), t_ref[l], count_ref[l])
        s_ref[l] = s
        highest = jnp.max(s, axis=0, keepdims=True)
        total = column_part(s_ref.at[l], highest, block)
        top = jnp.maximum(highest, col_ref[l, 0:1, :])
        total = total * jnp.exp2(highest - top) + col_ref[l, 1:2, :] * jnp.exp2(col_ref[l, 0:1, :] - top)
        half_reverse.append(0.5 * (top + jnp.log2(total)))
        rev_ref[l] = jnp.broadcast_to(half_reverse[l], (8, n_cols))
    rev_leave.start()
    for l in range(per_device):
        for start in range(0, n_half, block):
            at = slice(start, start + block)
            s = s_ref[l, at, :]
            forward = row_log_sum(s)
            w, margin = weigh(s, half_reverse[l])
            w_ref[l, at, :] = w
            put_tail(tail_ref, l, start // capacity, margin, forward, capacity)
        p = jnp.dot(w_ref[l], t_ref[l], preferred_element_type=F32).astype(BF16)
        put_pool(p_ref, l, p, capacity)
        if l == per_device - 1:
            p_ref[:, per_device * tiles] = tail_ref[...].astype(BF16)
        for copy in leave[l]:
            copy.start()
    for copy in sum(leave, [rev_leave]):
        copy.wait()


def near_owner(s_ref, rev_ref, fwd_ref, t_ref, p_ref, w_ref, tail_ref, *, capacity, block):
    per_device, n_half, _ = s_ref.shape
    for l in range(per_device):
        half_reverse = rev_ref[l, 0:1, :]
        for start in range(0, n_half, block):
            at = slice(start, start + block)
            w, margin = weigh(s_ref[l, at, :], half_reverse)
            w_ref[at, :] = w
            put_tail(tail_ref, l, start // capacity, margin, fwd_ref[l, at, 0:1], capacity)
        p = jnp.dot(w_ref[...], t_ref[l], preferred_element_type=F32).astype(BF16)
        put_pool(p_ref, l, p, capacity)
    p_ref[:, p_ref.shape[1] - 1] = tail_ref[...].astype(BF16)


def combine_kernel(code_ref, r_ref, _, *refs, capacity, side, split):
    _, core, _ = place_of(side)
    *outs, r_scr, scr = refs
    n_buckets, rows = code_ref.shape
    width = scr.shape[1]
    half = rows // 2
    n_msg, n_tiles, _, _ = r_ref.shape
    cols = width // 128
    strips = n_tiles // cols
    margin, forward = [], []
    for j in range(n_msg):
        last = r_ref[j, n_tiles - 1].astype(F32)
        last = (last + pltpu.roll(last, 127, 1)) + pltpu.roll(last, 126, 1)
        for r in range(strips):
            margin.append(jnp.broadcast_to(last[:, 6 * r : 6 * r + 1], (16, 128)))
            forward.append(jnp.broadcast_to(last[:, 6 * r + 3 : 6 * r + 4], (16, 128)))
            at = slice((j * strips + r) * 16, (j * strips + r + 1) * 16)
            for c in range(cols):
                r_scr[at, 128 * c : 128 * (c + 1)] = r_ref[j, r * cols + c]
    margin = jnp.concatenate([jnp.concatenate(margin, axis=0)] * (rows // 128), axis=1)
    forward = jnp.concatenate([jnp.concatenate(forward, axis=0)] * (rows // 128), axis=1)
    slots = one_hot_slots(code_ref[...], 0, n_buckets, capacity) > 0.5

    def merged(column):
        top = jnp.max(jnp.where(slots, column, NEGATIVE), axis=0, keepdims=True)
        total = jnp.sum(jnp.where(slots, jnp.exp2(column - top), 0.0), axis=0, keepdims=True)
        return jnp.where(total > 0.0, top + jnp.log2(jnp.where(total > 0.0, total, 1.0)), NEGATIVE)

    margin_row, forward_row = merged(margin), merged(forward)
    factor = jnp.where(slots, jnp.exp2(margin - margin_row), 0.0)
    high = factor.astype(BF16)
    low = (factor - high.astype(F32)).astype(BF16)
    r = r_scr[...]
    over = (((0,), (0,)), ((), ()))
    pooled = lax.dot_general(high, r, over, preferred_element_type=F32)
    scr[...] = pooled + lax.dot_general(low, r, over, preferred_element_type=F32)
    last = extra_rows(margin_row, forward_row, width)
    if split:
        keep_ref, kmf_ref, send_ref = outs
        keep_ref[...] = scr[pl.ds(pl.multiple_of(core * half, 16), half), :]
        send_ref[:half, :] = scr[pl.ds(pl.multiple_of((1 - core) * half, 16), half), :].astype(BF16)
        send_ref[half:, :] = last
        kmf_ref[...] = jnp.concatenate([margin_row, forward_row, jnp.zeros((6, rows), F32)], axis=0)
    else:
        start = 0
        for ref in outs:
            count = min(ref.shape[0], rows - start)
            ref[:count, :] = scr[start : start + count, :].astype(BF16)
            start = start + count
        outs[-1][count:, :] = last


def log_sum(first, second, third=None):
    top = jnp.maximum(first, second)
    if third is not None:
        top = jnp.maximum(top, third)
    total = jnp.exp2(first - top) + jnp.exp2(second - top)
    if third is not None:
        total = total + jnp.exp2(third - top)
    return top + jnp.log2(total)


def merge_pair(keep_ref, kmf_ref, got_ref, out_ref, scr, *, side):
    _, core, _ = place_of(side)
    half, width = keep_ref.shape
    rows = kmf_ref.shape[1]
    margin, forward = kmf_ref[0:1, :], kmf_ref[1:2, :]
    margin_b, forward_b = read_extra(got_ref, half, rows)
    margin_all, forward_all = log_sum(margin, margin_b), log_sum(forward, forward_b)
    scr[...] = columns([jnp.exp2(margin - margin_all), jnp.exp2(margin_b - margin_all)], rows)
    factors = scr[pl.ds(pl.multiple_of(core * half, 16), half), :]
    out = keep_ref[...] * factors[:, 0:1] + got_ref[:half, :].astype(F32) * factors[:, 1:2]
    out_ref[:half, :] = out.astype(BF16)
    out_ref[half:, :] = extra_rows(margin_all, forward_all, width)


def merge_last(*refs, n_pieces, side):
    _, core, _ = place_of(side)
    own, got = refs[:n_pieces], refs[n_pieces : 2 * n_pieces]
    mine_ref, other_ref, out_ref, conf_ref, far_scr = refs[2 * n_pieces :]
    rows, width = out_ref.shape
    half = rows // 2
    first_core = core == 0
    far_scr[pl.ds(pl.multiple_of(core * half, 16), half), :] = mine_ref[:half, :]
    far_scr[pl.ds(pl.multiple_of((1 - core) * half, 16), half), :] = other_ref[:half, :]
    last = own[-1].shape[0] - EXTRA
    pair = read_extra(own[-1], last, rows), read_extra(got[-1], last, rows)
    margin_a, forward_a = [jnp.where(first_core, x, y) for x, y in zip(*pair)]
    margin_b, forward_b = [jnp.where(first_core, y, x) for x, y in zip(*pair)]
    margin_c, forward_c = read_extra(mine_ref, half, rows)
    margin_all = log_sum(margin_a, margin_b, margin_c)
    forward_all = log_sum(forward_a, forward_b, forward_c)
    conf_ref[...] = (margin_all - 0.5 * forward_all) * LN2
    factors = columns([jnp.exp2(x - margin_all) for x in (margin_a, margin_b, margin_c)], rows)
    start = 0
    for x_ref, y_ref in zip(own, got):
        count = min(x_ref.shape[0], rows - start)
        at = slice(start, start + count)
        x, y = x_ref[:count, :], y_ref[:count, :]
        a = jnp.where(first_core, x, y).astype(F32) * factors[at, 0:1]
        b = jnp.where(first_core, y, x).astype(F32) * factors[at, 1:2]
        out_ref[at, :] = (a + b + far_scr[at, :].astype(F32) * factors[at, 2:3]).astype(BF16)
        start = start + count


def shards(sources, targets, picks, cluster_home, row_count):
    n_src, n_tgt = lax.axis_size("src"), lax.axis_size("tgt")
    rows, width = sources.shape
    per_device, n_cols, _ = targets.shape
    n_clusters = cluster_home.shape[0]
    n_picks = picks.shape[1]
    capacity = -(-(2 * n_picks * rows // n_clusters) // 16) * 16
    side = n_src // 2
    half = rows // 2
    message = per_device * capacity
    n_buckets = side * per_device
    n_slots = n_buckets * capacity
    group = max(g for g in range(per_device, n_buckets + 1, per_device) if n_buckets % g == 0 and g * capacity <= 400)
    sds = jax.ShapeDtypeStruct

    me, core = lax.axis_index("src"), lax.axis_index("tgt")
    partner = [(i, (i + side) % n_src) for i in range(n_src)]
    twin = [(i, 1 - i) for i in range(n_tgt)]
    halves = [list(range(side)), list(range(side, n_src))]

    def exchange(x):
        return lax.all_to_all(x, "src", split_axis=0, concat_axis=0, axis_index_groups=halves, tiled=True)

    picks_t = picks.T
    home = cluster_home[None, :]
    letter = sds((half + EXTRA, width), BF16)
    hbm = pl.BlockSpec(memory_space=pltpu.HBM)
    vmem = pl.BlockSpec(memory_space=pltpu.VMEM)
    smem = pl.BlockSpec(memory_space=pltpu.SMEM)
    unread = pl.BlockSpec(memory_space=pl.ANY)
    sizes = dict(side=side, n_tgt=n_tgt, per_device=per_device, capacity=capacity, group=group)
    gather_out = (sds((side, message, width), BF16), sds((n_buckets, rows), F32))
    moved = 2 * (n_slots + rows) * width
    gather_scratch = [
        pltpu.VMEM((side, message, width), BF16),
        pltpu.VMEM((n_buckets, rows), F32),
        pltpu.SemaphoreType.DMA((1 + side,)),
    ]
    mine, near_q, near_code = call(
        functools.partial(gather_own, **sizes),
        (letter,) + gather_out,
        gather_scratch
        + [
            pltpu.VMEM((n_picks, rows), jnp.int32),
            pltpu.VMEM((1, n_clusters), jnp.int32),
            pltpu.VMEM((rows, width), BF16),
            pltpu.VMEM((EXTRA, width), BF16),
            pltpu.SemaphoreType.DMA((5,)),
        ],
        flops=2 * n_slots * rows * width,
        moved=moved,
        limit=FULL,
        in_specs=[hbm] * 3,
        out_specs=(hbm, hbm, hbm),
    )(picks_t, home, sources)
    far_mine = lax.ppermute(mine, "src", partner)
    far_other = lax.ppermute(far_mine, "tgt", twin)
    near_in = exchange(near_q)
    *far_q, far_code = call(
        functools.partial(gather_partner, n_picks=n_picks, **sizes),
        tuple([pltpu.HBM((message, width), BF16)] * side) + (pltpu.HBM((n_buckets, rows), F32),),
        gather_scratch + [pltpu.VMEM((rows, width), BF16)],
        flops=HIDE,
        moved=moved,
        in_specs=[vmem] * 3,
        out_specs=tuple([hbm] * (side + 1)),
    )(home, far_mine, far_other)
    far_in = far_q[:1] + [
        lax.ppermute(far_q[k], "src", [(i, i ^ k) for i in range(n_src)]) for k in range(1, side)
    ]

    here = (me * n_tgt + core) * per_device + jnp.arange(per_device, dtype=jnp.int32)
    counts = jnp.sum(jnp.where(home == here[:, None], row_count[None, :], 0), axis=1)
    n_half = side * capacity
    options = dict(capacity=capacity, block=BLOCK)
    work = dict(flops=2 * n_slots * n_cols * width, moved=2 * (n_slots + per_device * n_cols) * width)
    n_tiles = message * width // 2048 + 1
    pooled = sds((side, n_tiles, 16, 128), BF16)
    row_block = capacity * math.gcd(side, ROW_GROUPS)
    near_s, near_col, near_fwd = call(
        functools.partial(near_scores, **options),
        (
            sds((per_device, n_half, n_cols), F32),
            sds((per_device, 8, n_cols), F32),
            sds((per_device, n_half, 128), F32),
        ),
        exps=2 * n_slots * n_cols,
        in_specs=[smem, vmem, vmem],
        out_specs=(vmem, vmem, vmem),
        **work,
    )(counts, near_in, targets)
    tails = pltpu.VMEM((side, 16, 128), F32)
    far_pool, reverse = call(
        functools.partial(far_owner, block=row_block, side=side),
        (pltpu.HBM(pooled.shape, BF16), pltpu.HBM((per_device, 8, n_cols), F32)),
        [
            pltpu.VMEM((per_device, side, capacity, width), BF16),
            pltpu.VMEM((per_device, n_half, n_cols), F32),
            pltpu.VMEM((per_device, n_half, n_cols), BF16),
            pltpu.VMEM((side, n_tiles, 16, 128), BF16),
            tails,
            pltpu.VMEM((per_device, 8, n_cols), F32),
            pltpu.SemaphoreType.DMA((per_device, side)),
            pltpu.SemaphoreType.DMA((per_device, side)),
            pltpu.SemaphoreType.DMA,
        ],
        exps=3 * n_slots * n_cols,
        in_specs=[smem, vmem, vmem] + [hbm] * side,
        out_specs=(hbm, hbm),
        **work,
    )(counts, near_col, targets, *far_in)
    back_far = exchange(far_pool)
    near_pool = call(
        functools.partial(near_owner, capacity=capacity, block=row_block),
        pooled,
        [pltpu.VMEM((n_half, n_cols), BF16), tails],
        n_in=4,
        exps=n_slots * n_cols,
        **work,
    )(near_s, reverse, near_fwd, targets)
    back_near = exchange(near_pool)

    def combine(code, back, after, outs, weight, split):
        return call(
            functools.partial(combine_kernel, capacity=capacity, side=side, split=split),
            outs,
            [pltpu.VMEM((n_slots, width), BF16), pltpu.VMEM((rows, width), F32)],
            flops=weight * 4 * n_slots * rows * width,
            moved=weight * 2 * (n_slots + 2 * rows) * width,
            in_specs=[vmem, vmem, unread],
            out_specs=tuple([vmem] * len(outs)),
        )(code, back, after)

    outs = (sds((half, width), F32), sds((8, rows), F32), letter)
    keep, kmf, send = combine(far_code, back_far, near_code, outs, 1, True)
    got = lax.ppermute(send, "tgt", twin)
    joined = call(
        functools.partial(merge_pair, side=side),
        letter,
        [pltpu.VMEM((rows, 128), F32)],
        n_in=3,
        moved=10 * half * width,
    )(keep, kmf, got)
    from_far = lax.ppermute(joined, "src", partner)
    from_far_other = lax.ppermute(from_far, "tgt", twin)

    pieces = [rows // 4] * 3 + [rows // 4 + EXTRA]
    own = combine(near_code, back_near, joined, tuple(sds((n, width), BF16) for n in pieces), 0, False)
    got = [lax.ppermute(piece, "tgt", twin) for piece in own]
    pooled, confidence = call(
        functools.partial(merge_last, n_pieces=len(pieces), side=side),
        (sds((rows, width), BF16), sds((1, rows), F32)),
        [pltpu.VMEM((rows, width), BF16)],
        n_in=2 * len(pieces) + 2,
        moved=10 * rows * width,
    )(*own, *got, from_far, from_far_other)
    return (pooled, confidence[0].astype(BF16))


def solution(mesh):
    placed = (P("src", None), P(("src", "tgt"), None, None), P("src", None), P(), P())
    return jax.shard_map(
        shards, mesh=mesh, in_specs=placed, out_specs=(P("src", None), P("src")), check_vma=False
    )
```

```python
import functools
import math

import jax
import jax.numpy as jnp
from jax import lax
from jax.experimental import pallas as pl
from jax.experimental.pallas import tpu as pltpu
from jax.sharding import PartitionSpec as P

NEGATIVE = -1e30
SHARPNESS = 2.5
EXTRA = 16
F32, BF16 = jnp.float32, jnp.bfloat16
MIB = 1 << 20
LOG2E = math.log2(math.e)
LN2 = math.log(2.0)
BLOCK = 128
ROW_GROUPS = 4
LIMIT = 24
FULL = 63
HIDE = 20_000_000_000


def iota(shape, axis):
    return lax.broadcasted_iota(jnp.int32, shape, axis)


def place_of(side):
    me = lax.axis_index("src")
    return me // side * side, lax.axis_index("tgt"), lax.rem(me, side)


def call(kernel, out_shape, scratch=(), smem=0, n_in=0, limit=LIMIT, flops=0, moved=0, exps=0, **kw):
    if not kw:
        kw = dict(
            in_specs=[pl.BlockSpec(memory_space=pltpu.SMEM)] * smem
            + [pl.BlockSpec(memory_space=pltpu.VMEM)] * (n_in - smem),
            out_specs=jax.tree.map(lambda _: pl.BlockSpec(memory_space=pltpu.VMEM), out_shape),
        )
    return pl.pallas_call(
        kernel,
        out_shape=out_shape,
        scratch_shapes=list(scratch),
        compiler_params=pltpu.CompilerParams(vmem_limit_bytes=limit * MIB),
        cost_estimate=pl.CostEstimate(flops=flops, bytes_accessed=moved, transcendentals=exps),
        **kw,
    )


def columns(rows, width):
    stacked = jnp.concatenate(rows + [jnp.zeros((128 - len(rows), width), F32)], axis=0)
    return stacked.T


def three(row):
    high = row.astype(BF16).astype(F32)
    middle = (row - high).astype(BF16).astype(F32)
    return [high, middle, row - high - middle]


def extra_rows(first, second, width):
    parts = three(first) + three(second)
    body = jnp.concatenate(parts + [jnp.zeros((EXTRA - len(parts), first.shape[1]), F32)], axis=0)
    rest = jnp.zeros((EXTRA, width - first.shape[1]), F32)
    return jnp.concatenate([body, rest], axis=1).astype(BF16)


def read_extra(ref, start, length):
    block = ref[start : start + EXTRA, :length].astype(F32)
    first = (block[0:1] + block[1:2]) + block[2:3]
    second = (block[3:4] + block[4:5]) + block[5:6]
    return first, second


def one_hot_slots(code, start, group, capacity):
    rows = code.shape[1]
    order = iota((capacity, rows), 0).astype(F32)
    return jnp.concatenate(
        [jnp.where(order == code[b : b + 1, :], 1.0, 0.0) for b in range(start, start + group)], axis=0
    )


def gather_body(
    info, flip, picks, home_ref, load, q_hbm, code_hbm, q_ref, code_ref, sem, *, n_tgt, per_device, capacity, group
):
    n_buckets, rows = code_ref.shape
    n_clusters = home_ref.shape[1]
    width = q_ref.shape[2]
    per_message = group // per_device
    cluster = iota((n_clusters, rows), 0).astype(F32)
    member = jnp.zeros((n_clusters, rows), F32)
    for pick in picks:
        member = jnp.where(cluster == pick, 1.0, member)
    bucket = iota((n_buckets, n_clusters), 0)
    earlier = jnp.where(iota((rows, rows), 0) < iota((rows, rows), 1), 1.0, 0.0).astype(BF16)

    def ranks(turn):
        holder = (info[0] + lax.bitwise_xor(lax.div(bucket, per_device), turn)) * n_tgt + info[1]
        place = holder * per_device + lax.rem(bucket, per_device)
        chosen = jnp.where(home_ref[...] == place, 1.0, 0.0).astype(BF16)
        inside = jnp.dot(chosen, member.astype(BF16), preferred_element_type=F32)
        rank = jnp.dot(inside.astype(BF16), earlier, preferred_element_type=F32)
        return jnp.where(inside > 0.5, rank, -1.0)

    code = ranks(0)
    code_ref[...] = code
    leave = [pltpu.make_async_copy(code_ref, code_hbm, sem.at[0])]
    leave[0].start()
    if flip is not None:
        code = ranks(flip)
    source = load()
    for start in range(0, n_buckets, group):
        slots = one_hot_slots(code, start, group, capacity)
        filled = jnp.sum(slots, axis=1, keepdims=True)
        found = jnp.dot(slots.astype(BF16), source, preferred_element_type=F32)
        head = found[:, :128]
        head = jnp.where((iota(head.shape, 1) == 0) & (filled < 0.5), jnp.inf, head)
        found = jnp.concatenate([head, found[:, 128:]], axis=1).astype(BF16)
        d = start // per_device
        at = pl.ds(d, per_message)
        q_ref[at] = found.reshape(per_message, per_device * capacity, width)
        if flip is None:
            leave.append(pltpu.make_async_copy(q_ref.at[at], q_hbm.at[at], sem.at[1 + start // group]))
            leave[-1].start()
        else:
            for k in range(d, d + per_message):
                leave.append(pltpu.make_async_copy(q_ref.at[k], q_hbm[k], sem.at[1 + k]))
                leave[-1].start()
    for copy in leave:
        copy.wait()


def gather_own(picks_hbm, home_hbm, src_hbm, letter_hbm, *refs, side, **sizes):
    *refs, picks_ref, home_ref, src_ref, last_ref, sems = refs
    info = place_of(side)
    copies = []
    for i, (here, there) in enumerate(((picks_hbm, picks_ref), (home_hbm, home_ref), (src_hbm, src_ref))):
        copies.append(pltpu.make_async_copy(here, there, sems.at[i]))
        copies[-1].start()
    copies[0].wait()
    copies[1].wait()
    n_picks, rows = picks_ref.shape
    width = src_ref.shape[1]
    half = rows // 2
    names = picks_ref[...].astype(F32)
    picks = [names[k : k + 1, :] for k in range(n_picks)]
    names = jnp.concatenate([names, jnp.zeros((EXTRA - n_picks, rows), F32)], axis=0)
    last_ref[...] = jnp.concatenate([names, jnp.zeros((EXTRA, width - rows), F32)], axis=1).astype(BF16)
    mine = pl.ds(pl.multiple_of(info[1] * half, 16), half)
    letter = [
        pltpu.make_async_copy(last_ref, letter_hbm.at[pl.ds(half, EXTRA), :], sems.at[3]),
        pltpu.make_async_copy(src_ref.at[mine, :], letter_hbm.at[pl.ds(0, half), :], sems.at[4]),
    ]
    letter[0].start()

    def load():
        copies[2].wait()
        letter[1].start()
        return src_ref[...]

    gather_body(info, None, picks, home_ref, load, *refs, **sizes)
    for copy in letter:
        copy.wait()


def gather_partner(home_ref, mine_ref, other_ref, *refs, n_picks, side, **sizes):
    info = place_of(side)
    *q_hbm, code_hbm, q_ref, code_ref, sem, src_ref = refs
    rows = src_ref.shape[0]
    half = rows // 2
    src_ref[pl.ds(pl.multiple_of(info[1] * half, 16), half), :] = mine_ref[:half, :]
    src_ref[pl.ds(pl.multiple_of((1 - info[1]) * half, 16), half), :] = other_ref[:half, :]
    block = mine_ref[half : half + EXTRA, :rows].astype(F32)
    picks = [block[k : k + 1, :] for k in range(n_picks)]
    load = lambda: src_ref[...]
    gather_body(info, info[2], picks, home_ref, load, q_hbm, code_hbm, q_ref, code_ref, sem, **sizes)


def scores_of(q, t, count):
    width = q.shape[1]
    n_cols = t.shape[0]
    head = q[:, :128].astype(F32)
    empty = head > 1e38
    q = jnp.concatenate([jnp.where(empty, 0.0, head).astype(BF16), q[:, 128:]], axis=1)
    s = lax.dot_general(q, t, (((1,), (1,)), ((), ())), preferred_element_type=F32)
    column_bias = jnp.where(iota((1, n_cols), 1) < count, 0.0, NEGATIVE).astype(F32)
    slot_bias = jnp.where(empty[:, 0:1], NEGATIVE, 0.0).astype(F32)
    return s * (SHARPNESS / math.sqrt(width) * LOG2E) + column_bias + slot_bias


def column_part(s_ref, highest, block):
    n_rows, n_cols = s_ref.shape
    total = jnp.zeros((8, n_cols), F32)
    for start in range(0, n_rows, block):
        part = jnp.exp2(s_ref[start : start + block, :] - highest)
        total = total + jnp.sum(part.reshape(block // 8, 8, n_cols), axis=0)
    return jnp.sum(total, axis=0, keepdims=True)


def row_log_sum(s):
    top = jnp.max(s, axis=1, keepdims=True)
    return top + jnp.log2(jnp.sum(jnp.exp2(s - top), axis=1, keepdims=True))


def weigh(s, half_reverse):
    shifted = s - half_reverse
    top = jnp.max(shifted, axis=1, keepdims=True)
    e = jnp.exp2(shifted - top)
    total = jnp.sum(e, axis=1, keepdims=True)
    return (e * (1.0 / total)).astype(BF16), top + jnp.log2(total)


def put_pool(p_ref, l, p, capacity):
    strips, cols = capacity // 16, p.shape[1] // 128
    for k in range(p_ref.shape[0]):
        for r in range(strips):
            strip = p[k * capacity + 16 * r : k * capacity + 16 * (r + 1)]
            for c in range(cols):
                p_ref[k, (l * strips + r) * cols + c] = strip[:, 128 * c : 128 * (c + 1)]


def put_tail(tail_ref, l, first, margin, forward, capacity):
    strips = capacity // 16
    shape = (margin.shape[0], 128)
    parts = three(jnp.broadcast_to(margin, shape)) + three(jnp.broadcast_to(forward, shape))
    turn = lax.rem(iota(shape, 1), 6)
    mixed = parts[5]
    for i in range(5):
        mixed = jnp.where(turn == i, parts[i], mixed)
    strip_of = lax.div(iota((16, 128), 1), 6)
    for k in range(margin.shape[0] // capacity):
        tile = tail_ref[first + k] if l else jnp.zeros((16, 128), F32)
        for r in range(strips):
            at = slice(k * capacity + 16 * r, k * capacity + 16 * (r + 1))
            tile = jnp.where(strip_of == l * strips + r, mixed[at], tile)
        tail_ref[first + k] = tile


def near_scores(count_ref, q_ref, t_ref, s_ref, col_ref, fwd_ref, *, capacity, block):
    per_device, n_half, n_cols = s_ref.shape
    for l in range(per_device):
        q = q_ref[:, l * capacity : (l + 1) * capacity, :].reshape(n_half, -1)
        s = scores_of(q, t_ref[l], count_ref[l])
        s_ref[l] = s
        highest = jnp.max(s, axis=0, keepdims=True)
        total = column_part(s_ref.at[l], highest, block)
        col_ref[l] = jnp.concatenate([highest, total, jnp.zeros((6, n_cols), F32)], axis=0)

        def forward(i, _):
            at = pl.ds(pl.multiple_of(i * block, block), block)
            fwd_ref[l, at, :] = jnp.broadcast_to(row_log_sum(s_ref[l, at, :]), (block, 128))
            return 0

        lax.fori_loop(0, n_half // block, forward, 0)


def join_columns(first, second):
    top = jnp.maximum(first[0], second[0])
    return top, first[1] * jnp.exp2(first[0] - top) + second[1] * jnp.exp2(second[0] - top)


def early_scores(count_ref, near_ref, t_ref, *refs, capacity, block):
    *q_refs, s_ref, col_ref = refs
    per_device, _, n_cols = s_ref.shape
    for l in range(per_device):
        q = jnp.concatenate([ref[l * capacity : (l + 1) * capacity, :] for ref in q_refs], axis=0)
        s = scores_of(q, t_ref[l], count_ref[l])
        s_ref[l] = s
        highest = jnp.max(s, axis=0, keepdims=True)
        part = highest, column_part(s_ref.at[l], highest, block)
        top, total = join_columns(part, (near_ref[l, 0:1, :], near_ref[l, 1:2, :]))
        col_ref[l] = jnp.concatenate([top, total, jnp.zeros((6, n_cols), F32)], axis=0)


def far_owner(count_ref, col_ref, t_ref, early_ref, *refs, block, side):
    _, _, here = place_of(side)
    *q_hbm, p_hbm, rev_hbm, q_ref, s_ref, w_ref, p_ref, tail_ref, rev_ref, q_sem, p_sem, rev_sem = refs
    per_device, n_late, capacity, width = q_ref.shape
    _, n_rows, n_cols = s_ref.shape
    n_msg = p_ref.shape[0]
    n_early = early_ref.shape[1]
    tiles = capacity * width // 2048
    arrive, leave = [], []
    for l in range(per_device):
        at = pl.ds(l * capacity, capacity)
        arrive.append([pltpu.make_async_copy(q_hbm[k].at[at, :], q_ref.at[l, k], q_sem.at[l, k]) for k in range(n_late)])
        at = pl.ds(l * tiles, tiles + l // (per_device - 1))
        to = [p_hbm.at[lax.bitwise_xor(here, k), at] for k in range(n_msg)]
        leave.append([pltpu.make_async_copy(p_ref.at[k, at], to[k], p_sem.at[l, k]) for k in range(n_msg)])
    for copy in sum(arrive, []):
        copy.start()
    rev_leave = pltpu.make_async_copy(rev_ref, rev_hbm, rev_sem)
    half_reverse = []
    for l in range(per_device):
        for copy in arrive[l]:
            copy.wait()
        s = scores_of(q_ref[l].reshape(n_rows, width), t_ref[l], count_ref[l])
        s_ref[l] = s
        highest = jnp.max(s, axis=0, keepdims=True)
        part = highest, column_part(s_ref.at[l], highest, block)
        top, total = join_columns(part, (col_ref[l, 0:1, :], col_ref[l, 1:2, :]))
        half_reverse.append(0.5 * (top + jnp.log2(total)))
        rev_ref[l] = jnp.broadcast_to(half_reverse[l], (8, n_cols))
    rev_leave.start()
    for l in range(per_device):
        for start in range(0, n_early + n_rows, block):
            if start < n_early:
                s = early_ref[l, start : start + block, :]
            else:
                s = s_ref[l, start - n_early : start - n_early + block, :]
            forward = row_log_sum(s)
            w, margin = weigh(s, half_reverse[l])
            w_ref[l, start : start + block, :] = w
            put_tail(tail_ref, l, start // capacity, margin, forward, capacity)
        p = jnp.dot(w_ref[l], t_ref[l], preferred_element_type=F32).astype(BF16)
        put_pool(p_ref, l, p, capacity)
        if l == per_device - 1:
            p_ref[:, per_device * tiles] = tail_ref[...].astype(BF16)
        for copy in leave[l]:
            copy.start()
    for copy in sum(leave, [rev_leave]):
        copy.wait()


def near_owner(s_ref, rev_ref, fwd_ref, t_ref, p_ref, w_ref, tail_ref, *, capacity, block):
    per_device, n_half, _ = s_ref.shape
    for l in range(per_device):
        half_reverse = rev_ref[l, 0:1, :]
        for start in range(0, n_half, block):
            at = slice(start, start + block)
            w, margin = weigh(s_ref[l, at, :], half_reverse)
            w_ref[at, :] = w
            put_tail(tail_ref, l, start // capacity, margin, fwd_ref[l, at, 0:1], capacity)
        p = jnp.dot(w_ref[...], t_ref[l], preferred_element_type=F32).astype(BF16)
        put_pool(p_ref, l, p, capacity)
    p_ref[:, p_ref.shape[1] - 1] = tail_ref[...].astype(BF16)


def combine_kernel(code_ref, r_ref, _, *refs, capacity, side, split):
    _, core, _ = place_of(side)
    *outs, r_scr, scr = refs
    n_buckets, rows = code_ref.shape
    width = scr.shape[1]
    half = rows // 2
    n_msg, n_tiles, _, _ = r_ref.shape
    cols = width // 128
    strips = n_tiles // cols
    margin, forward = [], []
    for j in range(n_msg):
        last = r_ref[j, n_tiles - 1].astype(F32)
        last = (last + pltpu.roll(last, 127, 1)) + pltpu.roll(last, 126, 1)
        for r in range(strips):
            margin.append(jnp.broadcast_to(last[:, 6 * r : 6 * r + 1], (16, 128)))
            forward.append(jnp.broadcast_to(last[:, 6 * r + 3 : 6 * r + 4], (16, 128)))
            at = slice((j * strips + r) * 16, (j * strips + r + 1) * 16)
            for c in range(cols):
                r_scr[at, 128 * c : 128 * (c + 1)] = r_ref[j, r * cols + c]
    margin = jnp.concatenate([jnp.concatenate(margin, axis=0)] * (rows // 128), axis=1)
    forward = jnp.concatenate([jnp.concatenate(forward, axis=0)] * (rows // 128), axis=1)
    slots = one_hot_slots(code_ref[...], 0, n_buckets, capacity) > 0.5

    def merged(column):
        top = jnp.max(jnp.where(slots, column, NEGATIVE), axis=0, keepdims=True)
        total = jnp.sum(jnp.where(slots, jnp.exp2(column - top), 0.0), axis=0, keepdims=True)
        return jnp.where(total > 0.0, top + jnp.log2(jnp.where(total > 0.0, total, 1.0)), NEGATIVE)

    margin_row, forward_row = merged(margin), merged(forward)
    factor = jnp.where(slots, jnp.exp2(margin - margin_row), 0.0)
    high = factor.astype(BF16)
    low = (factor - high.astype(F32)).astype(BF16)
    r = r_scr[...]
    over = (((0,), (0,)), ((), ()))
    pooled = lax.dot_general(high, r, over, preferred_element_type=F32)
    scr[...] = pooled + lax.dot_general(low, r, over, preferred_element_type=F32)
    last = extra_rows(margin_row, forward_row, width)
    if split:
        keep_ref, kmf_ref, send_ref = outs
        keep_ref[...] = scr[pl.ds(pl.multiple_of(core * half, 16), half), :]
        send_ref[:half, :] = scr[pl.ds(pl.multiple_of((1 - core) * half, 16), half), :].astype(BF16)
        send_ref[half:, :] = last
        kmf_ref[...] = jnp.concatenate([margin_row, forward_row, jnp.zeros((6, rows), F32)], axis=0)
    else:
        start = 0
        for ref in outs:
            count = min(ref.shape[0], rows - start)
            ref[:count, :] = scr[start : start + count, :].astype(BF16)
            start = start + count
        outs[-1][count:, :] = last


def log_sum(first, second, third=None):
    top = jnp.maximum(first, second)
    if third is not None:
        top = jnp.maximum(top, third)
    total = jnp.exp2(first - top) + jnp.exp2(second - top)
    if third is not None:
        total = total + jnp.exp2(third - top)
    return top + jnp.log2(total)


def merge_pair(keep_ref, kmf_ref, got_ref, out_ref, scr, *, side):
    _, core, _ = place_of(side)
    half, width = keep_ref.shape
    rows = kmf_ref.shape[1]
    margin, forward = kmf_ref[0:1, :], kmf_ref[1:2, :]
    margin_b, forward_b = read_extra(got_ref, half, rows)
    margin_all, forward_all = log_sum(margin, margin_b), log_sum(forward, forward_b)
    scr[...] = columns([jnp.exp2(margin - margin_all), jnp.exp2(margin_b - margin_all)], rows)
    factors = scr[pl.ds(pl.multiple_of(core * half, 16), half), :]
    out = keep_ref[...] * factors[:, 0:1] + got_ref[:half, :].astype(F32) * factors[:, 1:2]
    out_ref[:half, :] = out.astype(BF16)
    out_ref[half:, :] = extra_rows(margin_all, forward_all, width)


def merge_last(*refs, n_pieces, side):
    _, core, _ = place_of(side)
    own, got = refs[:n_pieces], refs[n_pieces : 2 * n_pieces]
    mine_ref, other_ref, out_ref, conf_ref, far_scr = refs[2 * n_pieces :]
    rows, width = out_ref.shape
    half = rows // 2
    first_core = core == 0
    far_scr[pl.ds(pl.multiple_of(core * half, 16), half), :] = mine_ref[:half, :]
    far_scr[pl.ds(pl.multiple_of((1 - core) * half, 16), half), :] = other_ref[:half, :]
    last = own[-1].shape[0] - EXTRA
    pair = read_extra(own[-1], last, rows), read_extra(got[-1], last, rows)
    margin_a, forward_a = [jnp.where(first_core, x, y) for x, y in zip(*pair)]
    margin_b, forward_b = [jnp.where(first_core, y, x) for x, y in zip(*pair)]
    margin_c, forward_c = read_extra(mine_ref, half, rows)
    margin_all = log_sum(margin_a, margin_b, margin_c)
    forward_all = log_sum(forward_a, forward_b, forward_c)
    conf_ref[...] = (margin_all - 0.5 * forward_all) * LN2
    factors = columns([jnp.exp2(x - margin_all) for x in (margin_a, margin_b, margin_c)], rows)
    start = 0
    for x_ref, y_ref in zip(own, got):
        count = min(x_ref.shape[0], rows - start)
        at = slice(start, start + count)
        x, y = x_ref[:count, :], y_ref[:count, :]
        a = jnp.where(first_core, x, y).astype(F32) * factors[at, 0:1]
        b = jnp.where(first_core, y, x).astype(F32) * factors[at, 1:2]
        out_ref[at, :] = (a + b + far_scr[at, :].astype(F32) * factors[at, 2:3]).astype(BF16)
        start = start + count


def shards(sources, targets, picks, cluster_home, row_count):
    n_src, n_tgt = lax.axis_size("src"), lax.axis_size("tgt")
    rows, width = sources.shape
    per_device, n_cols, _ = targets.shape
    n_clusters = cluster_home.shape[0]
    n_picks = picks.shape[1]
    capacity = -(-(2 * n_picks * rows // n_clusters) // 16) * 16
    side = n_src // 2
    half = rows // 2
    message = per_device * capacity
    n_buckets = side * per_device
    n_slots = n_buckets * capacity
    group = max(g for g in range(per_device, n_buckets + 1, per_device) if n_buckets % g == 0 and g * capacity <= 400)
    sds = jax.ShapeDtypeStruct

    me, core = lax.axis_index("src"), lax.axis_index("tgt")
    partner = [(i, (i + side) % n_src) for i in range(n_src)]
    twin = [(i, 1 - i) for i in range(n_tgt)]
    halves = [list(range(side)), list(range(side, n_src))]

    def exchange(x):
        return lax.all_to_all(x, "src", split_axis=0, concat_axis=0, axis_index_groups=halves, tiled=True)

    picks_t = picks.T
    home = cluster_home[None, :]
    letter = sds((half + EXTRA, width), BF16)
    hbm = pl.BlockSpec(memory_space=pltpu.HBM)
    vmem = pl.BlockSpec(memory_space=pltpu.VMEM)
    smem = pl.BlockSpec(memory_space=pltpu.SMEM)
    unread = pl.BlockSpec(memory_space=pl.ANY)
    sizes = dict(side=side, n_tgt=n_tgt, per_device=per_device, capacity=capacity, group=group)
    gather_out = (sds((side, message, width), BF16), sds((n_buckets, rows), F32))
    moved = 2 * (n_slots + rows) * width
    gather_scratch = [
        pltpu.VMEM((side, message, width), BF16),
        pltpu.VMEM((n_buckets, rows), F32),
        pltpu.SemaphoreType.DMA((1 + side,)),
    ]
    mine, near_q, near_code = call(
        functools.partial(gather_own, **sizes),
        (letter,) + gather_out,
        gather_scratch
        + [
            pltpu.VMEM((n_picks, rows), jnp.int32),
            pltpu.VMEM((1, n_clusters), jnp.int32),
            pltpu.VMEM((rows, width), BF16),
            pltpu.VMEM((EXTRA, width), BF16),
            pltpu.SemaphoreType.DMA((5,)),
        ],
        flops=2 * n_slots * rows * width,
        moved=moved,
        limit=FULL,
        in_specs=[hbm] * 3,
        out_specs=(hbm, hbm, hbm),
    )(picks_t, home, sources)
    far_mine = lax.ppermute(mine, "src", partner)
    far_other = lax.ppermute(far_mine, "tgt", twin)
    near_in = exchange(near_q)
    *far_q, far_code = call(
        functools.partial(gather_partner, n_picks=n_picks, **sizes),
        tuple([pltpu.HBM((message, width), BF16)] * side) + (pltpu.HBM((n_buckets, rows), F32),),
        gather_scratch + [pltpu.VMEM((rows, width), BF16)],
        flops=HIDE,
        moved=moved,
        in_specs=[vmem] * 3,
        out_specs=tuple([hbm] * (side + 1)),
    )(home, far_mine, far_other)
    far_in = far_q[:1] + [
        lax.ppermute(far_q[k], "src", [(i, i ^ k) for i in range(n_src)]) for k in range(1, side)
    ]

    here = (me * n_tgt + core) * per_device + jnp.arange(per_device, dtype=jnp.int32)
    counts = jnp.sum(jnp.where(home == here[:, None], row_count[None, :], 0), axis=1)
    n_half = side * capacity
    options = dict(capacity=capacity, block=BLOCK)
    work = dict(flops=2 * n_slots * n_cols * width, moved=2 * (n_slots + per_device * n_cols) * width)
    n_tiles = message * width // 2048 + 1
    pooled = sds((side, n_tiles, 16, 128), BF16)
    row_block = capacity * math.gcd(side, ROW_GROUPS)
    near_s, near_col, near_fwd = call(
        functools.partial(near_scores, **options),
        (
            sds((per_device, n_half, n_cols), F32),
            sds((per_device, 8, n_cols), F32),
            sds((per_device, n_half, 128), F32),
        ),
        exps=2 * n_slots * n_cols,
        in_specs=[smem, vmem, vmem],
        out_specs=(vmem, vmem, vmem),
        **work,
    )(counts, near_in, targets)
    tails = pltpu.VMEM((side, 16, 128), F32)
    early = side // 2
    n_early = early * capacity
    late_block = capacity * math.gcd(early, ROW_GROUPS)
    early_s, early_col = call(
        functools.partial(early_scores, capacity=capacity, block=late_block),
        (sds((per_device, n_early, n_cols), F32), sds((per_device, 8, n_cols), F32)),
        exps=n_slots * n_cols // 2,
        in_specs=[smem] + [vmem] * (2 + early),
        out_specs=(vmem, vmem),
        **work,
    )(counts, near_col, targets, *far_in[:early])
    far_pool, reverse = call(
        functools.partial(far_owner, block=late_block, side=side),
        (pltpu.HBM(pooled.shape, BF16), pltpu.HBM((per_device, 8, n_cols), F32)),
        [
            pltpu.VMEM((per_device, side - early, capacity, width), BF16),
            pltpu.VMEM((per_device, n_half - n_early, n_cols), F32),
            pltpu.VMEM((per_device, n_half, n_cols), BF16),
            pltpu.VMEM((side, n_tiles, 16, 128), BF16),
            tails,
            pltpu.VMEM((per_device, 8, n_cols), F32),
            pltpu.SemaphoreType.DMA((per_device, side - early)),
            pltpu.SemaphoreType.DMA((per_device, side)),
            pltpu.SemaphoreType.DMA,
        ],
        exps=3 * n_slots * n_cols,
        in_specs=[smem, vmem, vmem, vmem] + [hbm] * (side - early),
        out_specs=(hbm, hbm),
        **work,
    )(counts, early_col, targets, early_s, *far_in[early:])
    back_far = exchange(far_pool)
    near_pool = call(
        functools.partial(near_owner, capacity=capacity, block=row_block),
        pooled,
        [pltpu.VMEM((n_half, n_cols), BF16), tails],
        n_in=4,
        exps=n_slots * n_cols,
        **work,
    )(near_s, reverse, near_fwd, targets)
    back_near = exchange(near_pool)

    def combine(code, back, after, outs, weight, split):
        return call(
            functools.partial(combine_kernel, capacity=capacity, side=side, split=split),
            outs,
            [pltpu.VMEM((n_slots, width), BF16), pltpu.VMEM((rows, width), F32)],
            flops=weight * 4 * n_slots * rows * width,
            moved=weight * 2 * (n_slots + 2 * rows) * width,
            in_specs=[vmem, vmem, unread],
            out_specs=tuple([vmem] * len(outs)),
        )(code, back, after)

    outs = (sds((half, width), F32), sds((8, rows), F32), letter)
    keep, kmf, send = combine(far_code, back_far, near_code, outs, 1, True)
    got = lax.ppermute(send, "tgt", twin)
    joined = call(
        functools.partial(merge_pair, side=side),
        letter,
        [pltpu.VMEM((rows, 128), F32)],
        n_in=3,
        moved=10 * half * width,
    )(keep, kmf, got)
    from_far = lax.ppermute(joined, "src", partner)
    from_far_other = lax.ppermute(from_far, "tgt", twin)

    pieces = [rows // 4] * 3 + [rows // 4 + EXTRA]
    own = combine(near_code, back_near, joined, tuple(sds((n, width), BF16) for n in pieces), 0, False)
    got = [lax.ppermute(piece, "tgt", twin) for piece in own]
    pooled, confidence = call(
        functools.partial(merge_last, n_pieces=len(pieces), side=side),
        (sds((rows, width), BF16), sds((1, rows), F32)),
        [pltpu.VMEM((rows, width), BF16)],
        n_in=2 * len(pieces) + 2,
        moved=10 * rows * width,
    )(*own, *got, from_far, from_far_other)
    return (pooled, confidence[0].astype(BF16))


def solution(mesh):
    placed = (P("src", None), P(("src", "tgt"), None, None), P("src", None), P(), P())
    return jax.shard_map(
        shards, mesh=mesh, in_specs=placed, out_specs=(P("src", None), P("src")), check_vma=False
    )
```

```python
import functools
import math

import jax
import jax.numpy as jnp
from jax import lax
from jax.experimental import pallas as pl
from jax.experimental.pallas import tpu as pltpu
from jax.sharding import PartitionSpec as P

NEGATIVE = -1e30
SHARPNESS = 2.5
EXTRA = 16
F32, BF16 = jnp.float32, jnp.bfloat16
MIB = 1 << 20
LOG2E = math.log2(math.e)
LN2 = math.log(2.0)
BLOCK = 128
ROW_GROUPS = 4
LIMIT = 24
FULL = 63
HIDE = 20_000_000_000


def iota(shape, axis):
    return lax.broadcasted_iota(jnp.int32, shape, axis)


def place_of(side):
    me = lax.axis_index("src")
    return me // side * side, lax.axis_index("tgt"), lax.rem(me, side)


def call(kernel, out_shape, scratch=(), smem=0, n_in=0, limit=LIMIT, flops=0, moved=0, exps=0, **kw):
    if not kw:
        kw = dict(
            in_specs=[pl.BlockSpec(memory_space=pltpu.SMEM)] * smem
            + [pl.BlockSpec(memory_space=pltpu.VMEM)] * (n_in - smem),
            out_specs=jax.tree.map(lambda _: pl.BlockSpec(memory_space=pltpu.VMEM), out_shape),
        )
    return pl.pallas_call(
        kernel,
        out_shape=out_shape,
        scratch_shapes=list(scratch),
        compiler_params=pltpu.CompilerParams(vmem_limit_bytes=limit * MIB),
        cost_estimate=pl.CostEstimate(flops=flops, bytes_accessed=moved, transcendentals=exps),
        **kw,
    )


def columns(rows, width):
    stacked = jnp.concatenate(rows + [jnp.zeros((128 - len(rows), width), F32)], axis=0)
    return stacked.T


def three(row):
    high = row.astype(BF16).astype(F32)
    middle = (row - high).astype(BF16).astype(F32)
    return [high, middle, row - high - middle]


def extra_rows(first, second, width):
    parts = three(first) + three(second)
    body = jnp.concatenate(parts + [jnp.zeros((EXTRA - len(parts), first.shape[1]), F32)], axis=0)
    rest = jnp.zeros((EXTRA, width - first.shape[1]), F32)
    return jnp.concatenate([body, rest], axis=1).astype(BF16)


def read_extra(ref, start, length):
    block = ref[start : start + EXTRA, :length].astype(F32)
    first = (block[0:1] + block[1:2]) + block[2:3]
    second = (block[3:4] + block[4:5]) + block[5:6]
    return first, second


def one_hot_slots(code, start, group, capacity):
    rows = code.shape[1]
    order = iota((capacity, rows), 0).astype(F32)
    return jnp.concatenate(
        [jnp.where(order == code[b : b + 1, :], 1.0, 0.0) for b in range(start, start + group)], axis=0
    )


def gather_body(
    info, flip, picks, home_ref, load, q_hbm, code_hbm, q_ref, code_ref, sem, *, n_tgt, per_device, capacity, group
):
    n_buckets, rows = code_ref.shape
    n_clusters = home_ref.shape[1]
    width = q_ref.shape[2]
    per_message = group // per_device
    cluster = iota((n_clusters, rows), 0).astype(F32)
    member = jnp.zeros((n_clusters, rows), F32)
    for pick in picks:
        member = jnp.where(cluster == pick, 1.0, member)
    bucket = iota((n_buckets, n_clusters), 0)
    earlier = jnp.where(iota((rows, rows), 0) < iota((rows, rows), 1), 1.0, 0.0).astype(BF16)

    def ranks(turn):
        holder = (info[0] + lax.bitwise_xor(lax.div(bucket, per_device), turn)) * n_tgt + info[1]
        place = holder * per_device + lax.rem(bucket, per_device)
        chosen = jnp.where(home_ref[...] == place, 1.0, 0.0).astype(BF16)
        inside = jnp.dot(chosen, member.astype(BF16), preferred_element_type=F32)
        rank = jnp.dot(inside.astype(BF16), earlier, preferred_element_type=F32)
        return jnp.where(inside > 0.5, rank, -1.0)

    code = ranks(0 if flip is None else flip)
    code_ref[...] = code
    leave = [pltpu.make_async_copy(code_ref, code_hbm, sem.at[0])]
    leave[0].start()
    source = load()
    for start in range(0, n_buckets, group):
        slots = one_hot_slots(code, start, group, capacity)
        filled = jnp.sum(slots, axis=1, keepdims=True)
        found = jnp.dot(slots.astype(BF16), source, preferred_element_type=F32)
        head = found[:, :128]
        head = jnp.where((iota(head.shape, 1) == 0) & (filled < 0.5), jnp.inf, head)
        found = jnp.concatenate([head, found[:, 128:]], axis=1).astype(BF16)
        d = start // per_device
        at = pl.ds(d, per_message)
        q_ref[at] = found.reshape(per_message, per_device * capacity, width)
        if flip is None:
            leave.append(pltpu.make_async_copy(q_ref.at[at], q_hbm.at[at], sem.at[1 + start // group]))
            leave[-1].start()
        else:
            for k in range(d, d + per_message):
                leave.append(pltpu.make_async_copy(q_ref.at[k], q_hbm[k], sem.at[1 + k]))
                leave[-1].start()
    for copy in leave:
        copy.wait()


def gather_own(picks_hbm, home_hbm, src_hbm, letter_hbm, *refs, side, **sizes):
    *refs, picks_ref, home_ref, src_ref, last_ref, sems = refs
    info = place_of(side)
    copies = []
    for i, (here, there) in enumerate(((picks_hbm, picks_ref), (home_hbm, home_ref), (src_hbm, src_ref))):
        copies.append(pltpu.make_async_copy(here, there, sems.at[i]))
        copies[-1].start()
    copies[0].wait()
    copies[1].wait()
    n_picks, rows = picks_ref.shape
    width = src_ref.shape[1]
    half = rows // 2
    names = picks_ref[...].astype(F32)
    picks = [names[k : k + 1, :] for k in range(n_picks)]
    names = jnp.concatenate([names, jnp.zeros((EXTRA - n_picks, rows), F32)], axis=0)
    last_ref[...] = jnp.concatenate([names, jnp.zeros((EXTRA, width - rows), F32)], axis=1).astype(BF16)
    mine = pl.ds(pl.multiple_of(info[1] * half, 16), half)
    letter = [
        pltpu.make_async_copy(last_ref, letter_hbm.at[pl.ds(half, EXTRA), :], sems.at[3]),
        pltpu.make_async_copy(src_ref.at[mine, :], letter_hbm.at[pl.ds(0, half), :], sems.at[4]),
    ]
    letter[0].start()

    def load():
        copies[2].wait()
        letter[1].start()
        return src_ref[...]

    gather_body(info, None, picks, home_ref, load, *refs, **sizes)
    for copy in letter:
        copy.wait()


def gather_partner(home_ref, mine_ref, other_ref, *refs, n_picks, side, **sizes):
    info = place_of(side)
    *q_hbm, code_hbm, q_ref, code_ref, sem, src_ref = refs
    rows = src_ref.shape[0]
    half = rows // 2
    src_ref[pl.ds(pl.multiple_of(info[1] * half, 16), half), :] = mine_ref[:half, :]
    src_ref[pl.ds(pl.multiple_of((1 - info[1]) * half, 16), half), :] = other_ref[:half, :]
    block = mine_ref[half : half + EXTRA, :rows].astype(F32)
    picks = [block[k : k + 1, :] for k in range(n_picks)]
    load = lambda: src_ref[...]
    gather_body(info, info[2], picks, home_ref, load, q_hbm, code_hbm, q_ref, code_ref, sem, **sizes)


def scores_of(q, t, count):
    width = q.shape[1]
    n_cols = t.shape[0]
    head = q[:, :128].astype(F32)
    empty = head > 1e38
    q = jnp.concatenate([jnp.where(empty, 0.0, head).astype(BF16), q[:, 128:]], axis=1)
    s = lax.dot_general(q, t, (((1,), (1,)), ((), ())), preferred_element_type=F32)
    column_bias = jnp.where(iota((1, n_cols), 1) < count, 0.0, NEGATIVE).astype(F32)
    slot_bias = jnp.where(empty[:, 0:1], NEGATIVE, 0.0).astype(F32)
    return s * (SHARPNESS / math.sqrt(width) * LOG2E) + column_bias + slot_bias


def column_part(s_ref, highest, block):
    n_rows, n_cols = s_ref.shape
    total = jnp.zeros((8, n_cols), F32)
    for start in range(0, n_rows, block):
        part = jnp.exp2(s_ref[start : start + block, :] - highest)
        total = total + jnp.sum(part.reshape(block // 8, 8, n_cols), axis=0)
    return jnp.sum(total, axis=0, keepdims=True)


def row_log_sum(s):
    top = jnp.max(s, axis=1, keepdims=True)
    return top + jnp.log2(jnp.sum(jnp.exp2(s - top), axis=1, keepdims=True))


def weigh(s, half_reverse):
    shifted = s - half_reverse
    top = jnp.max(shifted, axis=1, keepdims=True)
    e = jnp.exp2(shifted - top)
    total = jnp.sum(e, axis=1, keepdims=True)
    return (e * (1.0 / total)).astype(BF16), top + jnp.log2(total)


def put_pool(p_ref, l, p, capacity):
    strips, cols = capacity // 16, p.shape[1] // 128
    for k in range(p_ref.shape[0]):
        for r in range(strips):
            strip = p[k * capacity + 16 * r : k * capacity + 16 * (r + 1)]
            for c in range(cols):
                p_ref[k, (l * strips + r) * cols + c] = strip[:, 128 * c : 128 * (c + 1)]


def put_tail(tail_ref, l, first, margin, forward, capacity):
    strips = capacity // 16
    shape = (margin.shape[0], 128)
    parts = three(jnp.broadcast_to(margin, shape)) + three(jnp.broadcast_to(forward, shape))
    turn = lax.rem(iota(shape, 1), 6)
    mixed = parts[5]
    for i in range(5):
        mixed = jnp.where(turn == i, parts[i], mixed)
    strip_of = lax.div(iota((16, 128), 1), 6)
    for k in range(margin.shape[0] // capacity):
        tile = tail_ref[first + k] if l else jnp.zeros((16, 128), F32)
        for r in range(strips):
            at = slice(k * capacity + 16 * r, k * capacity + 16 * (r + 1))
            tile = jnp.where(strip_of == l * strips + r, mixed[at], tile)
        tail_ref[first + k] = tile


def near_scores(count_ref, q_ref, t_ref, s_ref, col_ref, fwd_ref, *, capacity, block):
    per_device, n_half, n_cols = s_ref.shape
    for l in range(per_device):
        q = q_ref[:, l * capacity : (l + 1) * capacity, :].reshape(n_half, -1)
        s = scores_of(q, t_ref[l], count_ref[l])
        s_ref[l] = s
        highest = jnp.max(s, axis=0, keepdims=True)
        total = column_part(s_ref.at[l], highest, block)
        col_ref[l] = jnp.concatenate([highest, total, jnp.zeros((6, n_cols), F32)], axis=0)

        def forward(i, _):
            at = pl.ds(pl.multiple_of(i * block, block), block)
            fwd_ref[l, at, :] = jnp.broadcast_to(row_log_sum(s_ref[l, at, :]), (block, 128))
            return 0

        lax.fori_loop(0, n_half // block, forward, 0)


def join_columns(first, second):
    top = jnp.maximum(first[0], second[0])
    return top, first[1] * jnp.exp2(first[0] - top) + second[1] * jnp.exp2(second[0] - top)


def early_scores(count_ref, near_ref, t_ref, *refs, capacity, block):
    *q_refs, s_ref, col_ref = refs
    per_device, _, n_cols = s_ref.shape
    for l in range(per_device):
        q = jnp.concatenate([ref[l * capacity : (l + 1) * capacity, :] for ref in q_refs], axis=0)
        s = scores_of(q, t_ref[l], count_ref[l])
        s_ref[l] = s
        highest = jnp.max(s, axis=0, keepdims=True)
        part = highest, column_part(s_ref.at[l], highest, block)
        top, total = join_columns(part, (near_ref[l, 0:1, :], near_ref[l, 1:2, :]))
        col_ref[l] = jnp.concatenate([top, total, jnp.zeros((6, n_cols), F32)], axis=0)


def far_owner(count_ref, col_ref, t_ref, early_ref, *refs, block, side):
    _, _, here = place_of(side)
    *q_hbm, p_hbm, rev_hbm, q_ref, s_ref, w_ref, p_ref, tail_ref, rev_ref, q_sem, p_sem, rev_sem = refs
    per_device, n_late, capacity, width = q_ref.shape
    _, n_rows, n_cols = s_ref.shape
    n_msg = p_ref.shape[0]
    n_early = early_ref.shape[1]
    tiles = capacity * width // 2048
    arrive, leave = [], []
    for l in range(per_device):
        at = pl.ds(l * capacity, capacity)
        arrive.append([pltpu.make_async_copy(q_hbm[k].at[at, :], q_ref.at[l, k], q_sem.at[l, k]) for k in range(n_late)])
        at = pl.ds(l * tiles, tiles + l // (per_device - 1))
        to = [p_hbm.at[lax.bitwise_xor(here, k), at] for k in range(n_msg)]
        leave.append([pltpu.make_async_copy(p_ref.at[k, at], to[k], p_sem.at[l, k]) for k in range(n_msg)])
    for copy in sum(arrive, []):
        copy.start()
    rev_leave = pltpu.make_async_copy(rev_ref, rev_hbm, rev_sem)
    half_reverse = []
    for l in range(per_device):
        for copy in arrive[l]:
            copy.wait()
        s = scores_of(q_ref[l].reshape(n_rows, width), t_ref[l], count_ref[l])
        s_ref[l] = s
        highest = jnp.max(s, axis=0, keepdims=True)
        part = highest, column_part(s_ref.at[l], highest, block)
        top, total = join_columns(part, (col_ref[l, 0:1, :], col_ref[l, 1:2, :]))
        half_reverse.append(0.5 * (top + jnp.log2(total)))
        rev_ref[l] = jnp.broadcast_to(half_reverse[l], (8, n_cols))
    rev_leave.start()
    for l in range(per_device):
        for start in range(0, n_early + n_rows, block):
            if start < n_early:
                s = early_ref[l, start : start + block, :]
            else:
                s = s_ref[l, start - n_early : start - n_early + block, :]
            forward = row_log_sum(s)
            w, margin = weigh(s, half_reverse[l])
            w_ref[l, start : start + block, :] = w
            put_tail(tail_ref, l, start // capacity, margin, forward, capacity)
        p = jnp.dot(w_ref[l], t_ref[l], preferred_element_type=F32).astype(BF16)
        put_pool(p_ref, l, p, capacity)
        if l == per_device - 1:
            p_ref[:, per_device * tiles] = tail_ref[...].astype(BF16)
        for copy in leave[l]:
            copy.start()
    for copy in sum(leave, [rev_leave]):
        copy.wait()


def near_owner(s_ref, rev_ref, fwd_ref, t_ref, p_ref, w_ref, tail_ref, *, capacity, block):
    per_device, n_half, _ = s_ref.shape
    for l in range(per_device):
        half_reverse = rev_ref[l, 0:1, :]
        for start in range(0, n_half, block):
            at = slice(start, start + block)
            w, margin = weigh(s_ref[l, at, :], half_reverse)
            w_ref[at, :] = w
            put_tail(tail_ref, l, start // capacity, margin, fwd_ref[l, at, 0:1], capacity)
        p = jnp.dot(w_ref[...], t_ref[l], preferred_element_type=F32).astype(BF16)
        put_pool(p_ref, l, p, capacity)
    p_ref[:, p_ref.shape[1] - 1] = tail_ref[...].astype(BF16)


def combine_kernel(code_ref, r_ref, _, *refs, capacity, side, split):
    _, core, here = place_of(side)
    *outs, r_scr, scr = refs
    n_buckets, rows = code_ref.shape
    width = scr.shape[1]
    half = rows // 2
    n_msg, n_tiles, _, _ = r_ref.shape
    cols = width // 128
    strips = n_tiles // cols
    margin, forward = [], []
    for j in range(n_msg):
        owner = lax.bitwise_xor(here, j) if split else j
        last = r_ref[owner, n_tiles - 1].astype(F32)
        last = (last + pltpu.roll(last, 127, 1)) + pltpu.roll(last, 126, 1)
        for r in range(strips):
            margin.append(jnp.broadcast_to(last[:, 6 * r : 6 * r + 1], (16, 128)))
            forward.append(jnp.broadcast_to(last[:, 6 * r + 3 : 6 * r + 4], (16, 128)))
            at = slice((j * strips + r) * 16, (j * strips + r + 1) * 16)
            for c in range(cols):
                r_scr[at, 128 * c : 128 * (c + 1)] = r_ref[owner, r * cols + c]
    margin = jnp.concatenate([jnp.concatenate(margin, axis=0)] * (rows // 128), axis=1)
    forward = jnp.concatenate([jnp.concatenate(forward, axis=0)] * (rows // 128), axis=1)
    slots = one_hot_slots(code_ref[...], 0, n_buckets, capacity) > 0.5

    def merged(column):
        top = jnp.max(jnp.where(slots, column, NEGATIVE), axis=0, keepdims=True)
        total = jnp.sum(jnp.where(slots, jnp.exp2(column - top), 0.0), axis=0, keepdims=True)
        return jnp.where(total > 0.0, top + jnp.log2(jnp.where(total > 0.0, total, 1.0)), NEGATIVE)

    margin_row, forward_row = merged(margin), merged(forward)
    factor = jnp.where(slots, jnp.exp2(margin - margin_row), 0.0)
    high = factor.astype(BF16)
    low = (factor - high.astype(F32)).astype(BF16)
    r = r_scr[...]
    over = (((0,), (0,)), ((), ()))
    pooled = lax.dot_general(high, r, over, preferred_element_type=F32)
    scr[...] = pooled + lax.dot_general(low, r, over, preferred_element_type=F32)
    last = extra_rows(margin_row, forward_row, width)
    if split:
        keep_ref, kmf_ref, send_ref = outs
        keep_ref[...] = scr[pl.ds(pl.multiple_of(core * half, 16), half), :]
        send_ref[:half, :] = scr[pl.ds(pl.multiple_of((1 - core) * half, 16), half), :].astype(BF16)
        send_ref[half:, :] = last
        kmf_ref[...] = jnp.concatenate([margin_row, forward_row, jnp.zeros((6, rows), F32)], axis=0)
    else:
        start = 0
        for ref in outs:
            count = min(ref.shape[0], rows - start)
            ref[:count, :] = scr[start : start + count, :].astype(BF16)
            start = start + count
        outs[-1][count:, :] = last


def log_sum(first, second, third=None):
    top = jnp.maximum(first, second)
    if third is not None:
        top = jnp.maximum(top, third)
    total = jnp.exp2(first - top) + jnp.exp2(second - top)
    if third is not None:
        total = total + jnp.exp2(third - top)
    return top + jnp.log2(total)


def merge_pair(keep_ref, kmf_ref, got_ref, out_ref, scr, *, side):
    _, core, _ = place_of(side)
    half, width = keep_ref.shape
    rows = kmf_ref.shape[1]
    margin, forward = kmf_ref[0:1, :], kmf_ref[1:2, :]
    margin_b, forward_b = read_extra(got_ref, half, rows)
    margin_all, forward_all = log_sum(margin, margin_b), log_sum(forward, forward_b)
    scr[...] = columns([jnp.exp2(margin - margin_all), jnp.exp2(margin_b - margin_all)], rows)
    factors = scr[pl.ds(pl.multiple_of(core * half, 16), half), :]
    out = keep_ref[...] * factors[:, 0:1] + got_ref[:half, :].astype(F32) * factors[:, 1:2]
    out_ref[:half, :] = out.astype(BF16)
    out_ref[half:, :] = extra_rows(margin_all, forward_all, width)


def merge_last(*refs, n_pieces, side):
    _, core, _ = place_of(side)
    own, got = refs[:n_pieces], refs[n_pieces : 2 * n_pieces]
    mine_ref, other_ref, out_ref, conf_ref, far_scr = refs[2 * n_pieces :]
    rows, width = out_ref.shape
    half = rows // 2
    first_core = core == 0
    far_scr[pl.ds(pl.multiple_of(core * half, 16), half), :] = mine_ref[:half, :]
    far_scr[pl.ds(pl.multiple_of((1 - core) * half, 16), half), :] = other_ref[:half, :]
    last = own[-1].shape[0] - EXTRA
    pair = read_extra(own[-1], last, rows), read_extra(got[-1], last, rows)
    margin_a, forward_a = [jnp.where(first_core, x, y) for x, y in zip(*pair)]
    margin_b, forward_b = [jnp.where(first_core, y, x) for x, y in zip(*pair)]
    margin_c, forward_c = read_extra(mine_ref, half, rows)
    margin_all = log_sum(margin_a, margin_b, margin_c)
    forward_all = log_sum(forward_a, forward_b, forward_c)
    conf_ref[...] = (margin_all - 0.5 * forward_all) * LN2
    factors = columns([jnp.exp2(x - margin_all) for x in (margin_a, margin_b, margin_c)], rows)
    start = 0
    for x_ref, y_ref in zip(own, got):
        count = min(x_ref.shape[0], rows - start)
        at = slice(start, start + count)
        x, y = x_ref[:count, :], y_ref[:count, :]
        a = jnp.where(first_core, x, y).astype(F32) * factors[at, 0:1]
        b = jnp.where(first_core, y, x).astype(F32) * factors[at, 1:2]
        out_ref[at, :] = (a + b + far_scr[at, :].astype(F32) * factors[at, 2:3]).astype(BF16)
        start = start + count


def shards(sources, targets, picks, cluster_home, row_count):
    n_src, n_tgt = lax.axis_size("src"), lax.axis_size("tgt")
    rows, width = sources.shape
    per_device, n_cols, _ = targets.shape
    n_clusters = cluster_home.shape[0]
    n_picks = picks.shape[1]
    capacity = -(-(2 * n_picks * rows // n_clusters) // 16) * 16
    side = n_src // 2
    half = rows // 2
    message = per_device * capacity
    n_buckets = side * per_device
    n_slots = n_buckets * capacity
    group = max(g for g in range(per_device, n_buckets + 1, per_device) if n_buckets % g == 0 and g * capacity <= 400)
    sds = jax.ShapeDtypeStruct

    me, core = lax.axis_index("src"), lax.axis_index("tgt")
    partner = [(i, (i + side) % n_src) for i in range(n_src)]
    twin = [(i, 1 - i) for i in range(n_tgt)]
    halves = [list(range(side)), list(range(side, n_src))]

    def exchange(x):
        return lax.all_to_all(x, "src", split_axis=0, concat_axis=0, axis_index_groups=halves, tiled=True)

    picks_t = picks.T
    home = cluster_home[None, :]
    letter = sds((half + EXTRA, width), BF16)
    hbm = pl.BlockSpec(memory_space=pltpu.HBM)
    vmem = pl.BlockSpec(memory_space=pltpu.VMEM)
    smem = pl.BlockSpec(memory_space=pltpu.SMEM)
    unread = pl.BlockSpec(memory_space=pl.ANY)
    sizes = dict(side=side, n_tgt=n_tgt, per_device=per_device, capacity=capacity, group=group)
    gather_out = (sds((side, message, width), BF16), sds((n_buckets, rows), F32))
    moved = 2 * (n_slots + rows) * width
    gather_scratch = [
        pltpu.VMEM((side, message, width), BF16),
        pltpu.VMEM((n_buckets, rows), F32),
        pltpu.SemaphoreType.DMA((1 + side,)),
    ]
    mine, near_q, near_code = call(
        functools.partial(gather_own, **sizes),
        (letter,) + gather_out,
        gather_scratch
        + [
            pltpu.VMEM((n_picks, rows), jnp.int32),
            pltpu.VMEM((1, n_clusters), jnp.int32),
            pltpu.VMEM((rows, width), BF16),
            pltpu.VMEM((EXTRA, width), BF16),
            pltpu.SemaphoreType.DMA((5,)),
        ],
        flops=2 * n_slots * rows * width,
        moved=moved,
        limit=FULL,
        in_specs=[hbm] * 3,
        out_specs=(hbm, hbm, hbm),
    )(picks_t, home, sources)
    far_mine = lax.ppermute(mine, "src", partner)
    far_other = lax.ppermute(far_mine, "tgt", twin)
    near_in = exchange(near_q)
    *far_q, far_code = call(
        functools.partial(gather_partner, n_picks=n_picks, **sizes),
        tuple([pltpu.HBM((message, width), BF16)] * side) + (pltpu.HBM((n_buckets, rows), F32),),
        gather_scratch + [pltpu.VMEM((rows, width), BF16)],
        flops=HIDE,
        moved=moved,
        in_specs=[vmem] * 3,
        out_specs=tuple([hbm] * (side + 1)),
    )(home, far_mine, far_other)
    far_in = far_q[:1] + [
        lax.ppermute(far_q[k], "src", [(i, i ^ k) for i in range(n_src)]) for k in range(1, side)
    ]

    here = (me * n_tgt + core) * per_device + jnp.arange(per_device, dtype=jnp.int32)
    counts = jnp.sum(jnp.where(home == here[:, None], row_count[None, :], 0), axis=1)
    n_half = side * capacity
    options = dict(capacity=capacity, block=BLOCK)
    work = dict(flops=2 * n_slots * n_cols * width, moved=2 * (n_slots + per_device * n_cols) * width)
    n_tiles = message * width // 2048 + 1
    pooled = sds((side, n_tiles, 16, 128), BF16)
    row_block = capacity * math.gcd(side, ROW_GROUPS)
    near_s, near_col, near_fwd = call(
        functools.partial(near_scores, **options),
        (
            sds((per_device, n_half, n_cols), F32),
            sds((per_device, 8, n_cols), F32),
            sds((per_device, n_half, 128), F32),
        ),
        exps=2 * n_slots * n_cols,
        in_specs=[smem, vmem, vmem],
        out_specs=(vmem, vmem, vmem),
        **work,
    )(counts, near_in, targets)
    tails = pltpu.VMEM((side, 16, 128), F32)
    early = side * 3 // 4
    n_early = early * capacity
    late_block = capacity * math.gcd(early, ROW_GROUPS)
    early_s, early_col = call(
        functools.partial(early_scores, capacity=capacity, block=late_block),
        (sds((per_device, n_early, n_cols), F32), sds((per_device, 8, n_cols), F32)),
        exps=n_slots * n_cols // 2,
        in_specs=[smem] + [vmem] * (2 + early),
        out_specs=(vmem, vmem),
        **work,
    )(counts, near_col, targets, *far_in[:early])
    far_pool, reverse = call(
        functools.partial(far_owner, block=late_block, side=side),
        (pltpu.HBM(pooled.shape, BF16), pltpu.HBM((per_device, 8, n_cols), F32)),
        [
            pltpu.VMEM((per_device, side - early, capacity, width), BF16),
            pltpu.VMEM((per_device, n_half - n_early, n_cols), F32),
            pltpu.VMEM((per_device, n_half, n_cols), BF16),
            pltpu.VMEM((side, n_tiles, 16, 128), BF16),
            tails,
            pltpu.VMEM((per_device, 8, n_cols), F32),
            pltpu.SemaphoreType.DMA((per_device, side - early)),
            pltpu.SemaphoreType.DMA((per_device, side)),
            pltpu.SemaphoreType.DMA,
        ],
        exps=3 * n_slots * n_cols,
        in_specs=[smem, vmem, vmem, vmem] + [hbm] * (side - early),
        out_specs=(hbm, hbm),
        **work,
    )(counts, early_col, targets, early_s, *far_in[early:])
    back_far = exchange(far_pool)
    near_pool = call(
        functools.partial(near_owner, capacity=capacity, block=row_block),
        pooled,
        [pltpu.VMEM((n_half, n_cols), BF16), tails],
        n_in=4,
        exps=n_slots * n_cols,
        **work,
    )(near_s, reverse, near_fwd, targets)
    back_near = exchange(near_pool)

    def combine(code, back, after, outs, weight, split):
        return call(
            functools.partial(combine_kernel, capacity=capacity, side=side, split=split),
            outs,
            [pltpu.VMEM((n_slots, width), BF16), pltpu.VMEM((rows, width), F32)],
            flops=weight * 4 * n_slots * rows * width,
            moved=weight * 2 * (n_slots + 2 * rows) * width,
            in_specs=[vmem, vmem, unread],
            out_specs=tuple([vmem] * len(outs)),
        )(code, back, after)

    outs = (sds((half, width), F32), sds((8, rows), F32), letter)
    keep, kmf, send = combine(far_code, back_far, near_code, outs, 1, True)
    got = lax.ppermute(send, "tgt", twin)
    joined = call(
        functools.partial(merge_pair, side=side),
        letter,
        [pltpu.VMEM((rows, 128), F32)],
        n_in=3,
        moved=10 * half * width,
    )(keep, kmf, got)
    from_far = lax.ppermute(joined, "src", partner)
    from_far_other = lax.ppermute(from_far, "tgt", twin)

    pieces = [rows // 4] * 3 + [rows // 4 + EXTRA]
    own = combine(near_code, back_near, joined, tuple(sds((n, width), BF16) for n in pieces), 0, False)
    got = [lax.ppermute(piece, "tgt", twin) for piece in own]
    pooled, confidence = call(
        functools.partial(merge_last, n_pieces=len(pieces), side=side),
        (sds((rows, width), BF16), sds((1, rows), F32)),
        [pltpu.VMEM((rows, width), BF16)],
        n_in=2 * len(pieces) + 2,
        moved=10 * rows * width,
    )(*own, *got, from_far, from_far_other)
    return (pooled, confidence[0].astype(BF16))


def solution(mesh):
    placed = (P("src", None), P(("src", "tgt"), None, None), P("src", None), P(), P())
    return jax.shard_map(
        shards, mesh=mesh, in_specs=placed, out_specs=(P("src", None), P("src")), check_vma=False
    )
```
